32 devices in a mesh: section: 2 (over core), dp: 16 (over z, y, x).
Axes of the slice: x: 2, y: 2, z: 4, core: 2. Of those that a mesh axis runs over, the one named last changes fastest.
Arguments:
- embeddings: bfloat16 [2, 32, 512, 768], P('section', 'dp'), may hold values from -6 to 6
- cotangent: bfloat16 [32, 512, 768], P('dp'), may hold values from -6 to 6
- lengths: int32 [32], P('dp'), may hold values from 128 to 512, as said below
- qkv_weight: bfloat16 [2, 768, 2304], P('section'), may hold values from -0.3125 to 0.3125
- query_bias: float32 [2, 768], P('section'), may hold values from -3 to 3
- value_bias: float32 [2, 768], P('section'), may hold values from -3 to 3
- proj_weight: bfloat16 [2, 768, 768], P('section'), may hold values from -1.25 to 1.25
- proj_bias: float32 [2, 768], P('section'), may hold values from -3 to 3
- attn_gain: float32 [2, 768], P('section'), may hold values from 0.25 to 1.75
- attn_bias: float32 [2, 768], P('section'), may hold values from -2 to 2
- inner_weight: bfloat16 [2, 768, 3072], P('section'), may hold values from -0.21875 to 0.21875
- inner_bias: float32 [2, 3072], P('section'), may hold values from -3 to 3
- outer_weight: bfloat16 [2, 3072, 768], P('section'), may hold values from -0.15625 to 0.15625
- outer_bias: float32 [2, 768], P('section'), may hold values from -3 to 3
- ffn_gain: float32 [2, 768], P('section'), may hold values from 0.25 to 1.75
- ffn_bias: float32 [2, 768], P('section'), may hold values from -2 to 2
Outputs:
- block_output: bfloat16 [2, 32, 512, 768], P('section', 'dp')
- embedding_grads: float32 [2, 32, 512, 768], P('section', 'dp')
- grad_qkv_weight: float32 [2, 768, 2304], P('section')
- grad_query_bias: float32 [2, 768], P('section')
- grad_value_bias: float32 [2, 768], P('section')
- grad_proj_weight: float32 [2, 768, 768], P('section')
- grad_proj_bias: float32 [2, 768], P('section')
- grad_attn_gain: float32 [2, 768], P('section')
- grad_attn_bias: float32 [2, 768], P('section')
- grad_inner_weight: float32 [2, 768, 3072], P('section')
- grad_inner_bias: float32 [2, 3072], P('section')
- grad_outer_weight: float32 [2, 3072, 768], P('section')
- grad_outer_bias: float32 [2, 768], P('section')
- grad_ffn_gain: float32 [2, 768], P('section')
- grad_ffn_bias: float32 [2, 768], P('section')
The draws below stay inside these ranges and needn't reach their ends.
Inputs may be any that keep to these rules, and one draw needn't show every extreme that they name: `lengths`: some passage has exactly 512 tokens.
All inputs are finite; a program needn't handle non-finite values.
Results may differ from the reference program's by a relative error of at most 0.015.
The reference program's roundings to bfloat16 on the way count: a program that leaves them out, or rounds other values in their place, can miss the bound.
Values may be sent and summed in bfloat16 or wider, within the bound.
No kernel may reach another device: no remote copies, remote signals or barrier semaphores. Data moves between devices by JAX's collectives and lax.ppermute only.
A program may use at most 320 MiB of HBM per device.

```python
import jax
import jax.numpy as jnp
from jax import lax

D = 768
HEADS = 12
HEAD_DIM = 64
FF = 3072
LEN = 512
ROWS = 32


def draw_lengths(key, part):
    key = jax.random.fold_in(key, 11)
    first_key, second_key, third_key = jax.random.split(key, 3)
    draw_one = jax.random.randint(first_key, (ROWS,), LEN // 4, LEN + 1)
    draw_two = jax.random.randint(second_key, (ROWS,), LEN // 4, LEN + 1)
    shorter = jnp.minimum(draw_one, draw_two)
    chosen = jax.random.randint(third_key, (), 0, ROWS)
    return jnp.where(jnp.arange(ROWS) == chosen, LEN, shorter).astype(jnp.int32)


def block_levels(own_key, shape, shards, least, largest):
    factor_of, own = 1.0, jax.random.fold_in(own_key, 6)
    for dim, shards_of in shards:
        draws = jnp.exp(jax.random.uniform(jax.random.fold_in(own, dim), (shards_of,), jnp.float32, least / len(shards), largest / len(shards)))
        factor_of = factor_of * jnp.repeat(draws, shape[dim] // shards_of).reshape([-1 if axis == dim else 1 for axis in range(len(shape))])
    return factor_of


def scatter_about(stream_key, extent, deviation, reach, cuts=(), kind=jnp.bfloat16):
    entries = jax.random.normal(stream_key, extent, jnp.float32) * deviation
    if len(cuts) > 0:
        entries = block_levels(stream_key, extent, cuts, -0.22, 0.18) * entries
    return jnp.clip(entries, min=-reach, max=reach).astype(kind)


def setup_inputs(seed: int = 0) -> dict:
    keys = jax.random.split(jax.random.key(seed), 17)
    embeddings = scatter_about(keys[0], (2, ROWS, LEN, D), 1.0, 6.0, ((0, 2), (1, 16)))
    cotangent = scatter_about(keys[1], (ROWS, LEN, D), 1.0, 6.0, ((0, 16),))
    lengths = draw_lengths(jax.random.fold_in(keys[16], 71), 0)
    qkv_weight = scatter_about(keys[3], (2, D, 3 * D), (D // 2) ** -0.5, 0.3125, ((0, 2),))
    query_bias = scatter_about(keys[4], (2, D), 0.5, 3.0, ((0, 2),), jnp.float32)
    value_bias = scatter_about(keys[5], (2, D), 0.5, 3.0, ((0, 2),), jnp.float32)
    proj_weight = scatter_about(keys[6], (2, D, D), (D // 32) ** -0.5, 1.25, ((0, 2),))
    proj_bias = scatter_about(keys[7], (2, D), 0.5, 3.0, ((0, 2),), jnp.float32)
    attn_gain = jnp.clip(1.0 + 0.15 * jax.random.normal(keys[8], (2, D), jnp.float32), 0.25, 1.75)
    attn_bias = scatter_about(keys[9], (2, D), 0.3, 2.0, ((0, 2),), jnp.float32)
    inner_weight = scatter_about(keys[10], (2, D, FF), D ** -0.5, 0.21875, ((0, 2),))
    inner_bias = scatter_about(keys[11], (2, FF), 0.5, 3.0, ((0, 2),), jnp.float32)
    outer_weight = scatter_about(keys[12], (2, FF, D), (FF // 2) ** -0.5, 0.15625, ((0, 2),))
    outer_bias = scatter_about(keys[13], (2, D), 0.5, 3.0, ((0, 2),), jnp.float32)
    ffn_gain = jnp.clip(1.0 + 0.15 * jax.random.normal(keys[14], (2, D), jnp.float32), 0.25, 1.75)
    ffn_bias = scatter_about(keys[15], (2, D), 0.3, 2.0, ((0, 2),), jnp.float32)
    return {"embeddings": embeddings, "cotangent": cotangent, "lengths": lengths, "qkv_weight": qkv_weight, "query_bias": query_bias, "value_bias": value_bias, "proj_weight": proj_weight, "proj_bias": proj_bias, "attn_gain": attn_gain, "attn_bias": attn_bias, "inner_weight": inner_weight, "inner_bias": inner_bias, "outer_weight": outer_weight, "outer_bias": outer_bias, "ffn_gain": ffn_gain, "ffn_bias": ffn_bias}


@jax.custom_vjp
def low(v):
    return lax.optimization_barrier(v.astype(jnp.bfloat16)).astype(jnp.float32)

@jax.custom_vjp
def low_back(v):
    return v

def low_keep(v):
    return (low(v), None)

def low_pass(kept, grad):
    return (grad,)

def back_keep(v):
    return (v, None)

def back_low(kept, grad):
    return (low(grad),)
low.defvjp(low_keep, low_pass)
low_back.defvjp(back_keep, back_low)
HIGH = lax.Precision.HIGHEST
EPSILON = 1e-06

def product(form, left_side, right_side):
    return jnp.einsum(form, left_side, right_side, precision=HIGH)

def normalize(hidden):
    centred = hidden - lax.optimization_barrier(jnp.mean(hidden, axis=-1, keepdims=True))
    return centred * lax.rsqrt(lax.optimization_barrier(jnp.mean(centred * centred, axis=-1, keepdims=True)) + EPSILON)

def layer_forward(params, inputs, key_mask):
    qkv_weight, query_bias, value_bias, proj_weight, proj_bias, attn_gain, attn_bias, inner_weight, inner_bias, outer_weight, outer_bias, ffn_gain, ffn_bias = params
    batch_size, length, model_width = inputs.shape
    qkv_shift = jnp.concatenate([query_bias, jnp.zeros_like(query_bias), value_bias])
    packed = low(low_back(product('bld,de->ble', inputs, qkv_weight) + qkv_shift))
    split_parts = packed.reshape(batch_size, length, 3, HEADS, HEAD_DIM)
    query_part, key_part, value_part = (split_parts[:, :, 0], split_parts[:, :, 1], split_parts[:, :, 2])
    raw_scores = low_back(product('bqhe,bkhe->bhqk', query_part, key_part) * HEAD_DIM ** (-0.5))
    masked = jnp.where(key_mask[:, None, None, :], raw_scores, -1e+30)
    attention = low(jax.nn.softmax(masked, axis=-1))
    context = product('bhqk,bkhe->bqhe', attention, value_part).reshape(batch_size, length, model_width)
    context = low(low_back(context))
    attn_out = low_back(product('bld,de->ble', context, proj_weight) + proj_bias)
    normed = normalize(inputs + attn_out) * attn_gain + attn_bias
    inner_sum = low_back(product('bld,di->bli', low(normed), inner_weight) + inner_bias)
    act_low = low(jax.nn.gelu(inner_sum, approximate=False))
    outer_sum = low_back(product('bli,id->bld', act_low, outer_weight) + outer_bias)
    return normalize(normed + outer_sum) * ffn_gain + ffn_bias

def reference(embeddings, cotangent, lengths, qkv_weight, query_bias, value_bias, proj_weight, proj_bias, attn_gain, attn_bias, inner_weight, inner_bias, outer_weight, outer_bias, ffn_gain, ffn_bias):
    widened = tuple((piece.astype(jnp.float32) for piece in (qkv_weight, query_bias, value_bias, proj_weight, proj_bias, attn_gain, attn_bias, inner_weight, inner_bias, outer_weight, outer_bias, ffn_gain, ffn_bias)))
    encoder_params = tuple((piece[0] for piece in widened))
    decoder_params = tuple((piece[1] for piece in widened))
    group_size = 2
    group_count = ROWS // group_size
    positions = jnp.arange(LEN, dtype=jnp.int32)

    def grouped_rows(array):
        return array.reshape((group_count, group_size) + array.shape[1:])
    grouped = (grouped_rows(embeddings[0]), grouped_rows(embeddings[1]), grouped_rows(cotangent), grouped_rows(lengths.astype(jnp.int32)))

    def per_group(totals, item):
        first_in, second_in, cot_rows, len_rows = item
        key_mask = positions[None, :] < len_rows[:, None]

        def two_layers(enc_params, dec_params, enc_input, dec_input):
            enc_out = layer_forward(enc_params, enc_input, key_mask)
            cls_head = low_back(low(enc_out[:, :1]))
            dec_out = layer_forward(dec_params, jnp.concatenate([cls_head, dec_input[:, 1:]], axis=1), key_mask)
            return (dec_out, enc_out)
        (dec_out, enc_out), pullback = jax.vjp(two_layers, encoder_params, decoder_params, first_in.astype(jnp.float32), second_in.astype(jnp.float32))
        weight_row = key_mask[..., None].astype(jnp.float32)
        grad_enc, grad_dec, grad_first, grad_second = pullback((cot_rows.astype(jnp.float32) * weight_row, jnp.zeros_like(enc_out)))
        totals = jax.tree.map(lambda summed, enc_term, dec_term: summed + jnp.stack([enc_term, dec_term]), totals, grad_enc, grad_dec)
        return (totals, (enc_out.astype(jnp.bfloat16), dec_out.astype(jnp.bfloat16), grad_first, grad_second))
    initial = tuple((jnp.zeros_like(piece) for piece in widened))
    totals, (enc_all, dec_all, first_all, second_all) = lax.scan(per_group, initial, grouped)

    def ungroup(array):
        return array.reshape((ROWS,) + array.shape[2:])
    block_output = jnp.stack([ungroup(enc_all), ungroup(dec_all)])
    embedding_grads = jnp.stack([ungroup(first_all), ungroup(second_all)])
    g_qkv, g_query, g_value, g_proj, g_proj_bias, g_attn_gain, g_attn_bias, g_inner, g_inner_bias, g_outer, g_outer_bias, g_ffn_gain, g_ffn_bias = totals
    return (block_output, embedding_grads, g_qkv, g_query, g_value, g_proj, g_proj_bias, g_attn_gain, g_attn_bias, g_inner, g_inner_bias, g_outer, g_outer_bias, g_ffn_gain, g_ffn_bias)
```

```python
from functools import partial

import jax
import jax.numpy as jnp
from jax import lax
from jax.sharding import PartitionSpec as P

HEADS = 12
HEAD_DIM = 64
EPSILON = 1e-06
BIG_NEG = -1e30
BF = jnp.bfloat16
F32 = jnp.float32


def row_norm(hidden):
    centred = hidden - jnp.mean(hidden, axis=-1, keepdims=True)
    scale = lax.rsqrt(jnp.mean(centred * centred, axis=-1, keepdims=True) + EPSILON)
    return (centred * scale, scale)


def norm_back(grad, normal, scale, gain):
    scaled = grad * gain
    return scale * (
        scaled
        - jnp.mean(scaled, axis=-1, keepdims=True)
        - normal * jnp.mean(scaled * normal, axis=-1, keepdims=True)
    )


def dot(form, left, right):
    return jnp.einsum(form, left, right, preferred_element_type=F32)


def gelu(value):
    return jax.nn.gelu(value, approximate=False)


def gelu_slope(value):
    unused, pullback = jax.vjp(gelu, value)
    return pullback(jnp.ones_like(value))[0]


def split_heads(packed):
    parts = packed.reshape(packed.shape[:-1] + (3, HEADS, HEAD_DIM))
    return (parts[..., 0, :, :], parts[..., 1, :, :], parts[..., 2, :, :])


def ffn_forward(params, inputs, context_low):
    proj_weight, proj_bias, attn_gain, attn_bias = params[3:7]
    inner_weight, inner_bias, outer_weight, outer_bias, ffn_gain, ffn_bias = params[7:]
    attn_out = dot("...d,de->...e", context_low, proj_weight) + proj_bias
    first_normal, first_scale = row_norm(inputs.astype(F32) + attn_out)
    normed = first_normal * attn_gain + attn_bias
    inner_sum = dot("...d,di->...i", normed.astype(BF), inner_weight) + inner_bias
    act_low = gelu(inner_sum).astype(BF)
    outer_sum = dot("...i,id->...d", act_low, outer_weight) + outer_bias
    second_normal, second_scale = row_norm(normed + outer_sum)
    result = second_normal * ffn_gain + ffn_bias
    return (result, (first_normal, first_scale, inner_sum, act_low, second_normal, second_scale))


def ffn_backward(params, saved, grad_out):
    proj_weight, proj_bias, attn_gain, attn_bias = params[3:7]
    inner_weight, inner_bias, outer_weight, outer_bias, ffn_gain, ffn_bias = params[7:]
    first_normal, first_scale, inner_sum, act_low, second_normal, second_scale = saved
    second_grad = norm_back(grad_out, second_normal, second_scale, ffn_gain)
    outer_low = second_grad.astype(BF)
    act_grad = dot("...d,id->...i", outer_low, outer_weight)
    inner_low = (act_grad * gelu_slope(inner_sum)).astype(BF)
    normed_grad = second_grad + dot("...i,di->...d", inner_low, inner_weight)
    first_grad = norm_back(normed_grad, first_normal, first_scale, attn_gain)
    proj_low = first_grad.astype(BF)
    context_grad = dot("...e,de->...d", proj_low, proj_weight).astype(BF)
    rows = tuple(range(grad_out.ndim - 1))
    small = (
        jnp.sum(proj_low.astype(F32), axis=rows),
        jnp.sum(normed_grad * first_normal, axis=rows),
        jnp.sum(normed_grad, axis=rows),
        jnp.sum(inner_low.astype(F32), axis=rows),
        jnp.sum(outer_low.astype(F32), axis=rows),
        jnp.sum(grad_out * second_normal, axis=rows),
        jnp.sum(grad_out, axis=rows),
    )
    return (outer_low, inner_low, first_grad, proj_low, context_grad, small)


def local(embeddings, cotangent, lengths, *weights):
    params = tuple(piece[0] for piece in weights)
    qkv_weight, query_bias, value_bias, proj_weight, proj_bias, attn_gain, attn_bias = params[:7]
    encoder = lax.axis_index("section") == 0
    inputs = embeddings[0]
    batch, length, width = inputs.shape
    scale = HEAD_DIM ** (-0.5)
    key_mask = jnp.arange(length, dtype=jnp.int32)[None, :] < lengths[:, None]
    qkv_shift = jnp.concatenate([query_bias, jnp.zeros_like(query_bias), value_bias])

    def project(rows):
        return (dot("...d,de->...e", rows, qkv_weight) + qkv_shift).astype(BF)

    qkv_low = project(inputs)
    query_part, key_part, value_part = split_heads(qkv_low)
    first_scores = dot("bhe,bkhe->bhk", query_part[:, 0], key_part) * scale
    first_scores = jnp.where(key_mask[:, None, :], first_scores, BIG_NEG)
    first_probs = jax.nn.softmax(first_scores, axis=-1)
    first_context = dot("bhk,bkhe->bhe", first_probs.astype(BF), value_part)
    first_context = first_context.reshape(batch, width).astype(BF)
    first_result, first_saved = ffn_forward(params, inputs[:, 0], first_context)
    arrived = lax.ppermute(first_result.astype(BF), "section", [(0, 1)])

    first_rows = jnp.where(encoder, inputs[:, 0], arrived)
    inputs = inputs.at[:, 0].set(first_rows)
    qkv_low = qkv_low.at[:, 0].set(project(first_rows))
    query_part, key_part, value_part = split_heads(qkv_low)
    scores = dot("bqhe,bkhe->bhqk", query_part, key_part) * scale
    scores = jnp.where(key_mask[:, None, None, :], scores, BIG_NEG)
    attention = jax.nn.softmax(scores, axis=-1)
    context = dot("bhqk,bkhe->bqhe", attention.astype(BF), value_part)
    context_low = context.reshape(batch, length, width).astype(BF)
    result, saved = ffn_forward(params, inputs, context_low)

    grad_out = cotangent.astype(F32) * key_mask[..., None].astype(F32)
    outer_low, inner_low, first_grad, proj_low, context_grad, small = ffn_backward(
        params, saved, grad_out
    )
    normed_low = (saved[0] * attn_gain + attn_bias).astype(BF)
    outer_weight_grad = dot("bli,bld->id", saved[3], outer_low)
    inner_weight_grad = dot("bld,bli->di", normed_low, inner_low)
    proj_weight_grad = dot("bld,ble->de", context_low, proj_low)
    context_grad = context_grad.reshape(batch, length, HEADS, HEAD_DIM)
    prob_grad = dot("bqhe,bkhe->bhqk", context_grad, value_part)
    value_grad = dot("bhqk,bqhe->bkhe", attention.astype(BF), context_grad)
    score_low = (
        attention * (prob_grad - jnp.sum(attention * prob_grad, axis=-1, keepdims=True))
    ).astype(BF)
    query_grad = dot("bhqk,bkhe->bqhe", score_low, key_part) * scale
    key_grad = dot("bhqk,bqhe->bkhe", score_low, query_part) * scale
    packed_grad = jnp.stack([query_grad, key_grad, value_grad], axis=2)
    packed_grad = packed_grad.reshape(batch, length, 3 * width).astype(BF)
    packed_sums = jnp.sum(packed_grad.astype(F32), axis=(0, 1))
    qkv_weight_grad = dot("bld,ble->de", inputs, packed_grad)
    input_grad = dot("ble,de->bld", packed_grad, qkv_weight) + first_grad
    returned = lax.ppermute(input_grad[:, 0].astype(BF), "section", [(1, 0)])
    decoder_grads = tuple(
        lax.psum(piece.astype(BF), "dp").astype(F32)
        for piece in (outer_weight_grad, inner_weight_grad, proj_weight_grad, qkv_weight_grad)
    )
    small = (packed_sums[:width], packed_sums[2 * width :]) + small

    e_outer, e_inner, e_first, e_proj, e_context, e_small = ffn_backward(
        params, first_saved, returned.astype(F32)
    )
    e_context = e_context.reshape(batch, HEADS, HEAD_DIM)
    e_query = query_part[:, 0]
    e_prob_grad = dot("bhe,bkhe->bhk", e_context, value_part)
    e_score = (
        first_probs
        * (e_prob_grad - jnp.sum(first_probs * e_prob_grad, axis=-1, keepdims=True))
    ).astype(BF)
    e_probs = first_probs.astype(BF)
    e_query_grad = (dot("bhk,bkhe->bhe", e_score, key_part) * scale).astype(BF)
    e_query = e_query * jnp.asarray(scale, BF)
    key_sums = dot("bhk,bkd->bhd", e_score, inputs).astype(BF)
    value_sums = dot("bhk,bkd->bhd", e_probs, inputs).astype(BF)
    qkv_heads = qkv_weight.reshape(width, 3, HEADS, HEAD_DIM)
    key_back = dot("dhe,bhe->bhd", qkv_heads[:, 1], e_query)
    value_back = dot("dhe,bhe->bhd", qkv_heads[:, 2], e_context)
    e_input_grad = jnp.einsum(
        "bhk,bhd->bkd", e_score, key_back.astype(BF), preferred_element_type=F32
    ) + jnp.einsum("bhk,bhd->bkd", e_probs, value_back.astype(BF), preferred_element_type=F32)
    e_first_grad = e_first + dot("bhe,dhe->bd", e_query_grad, qkv_heads[:, 0])
    e_input_grad = e_input_grad.at[:, 0].add(e_first_grad)
    value_mass = jnp.sum(e_probs.astype(F32), axis=-1, keepdims=True)
    e_small = (
        jnp.sum(e_query_grad.astype(F32), axis=0).reshape(width),
        jnp.sum(e_context.astype(F32) * value_mass, axis=0).reshape(width),
    ) + e_small

    factors = (
        first_saved[3],
        e_outer,
        (first_saved[0] * attn_gain + attn_bias).astype(BF),
        e_inner,
        first_context,
        e_proj,
        inputs[:, 0],
        e_query_grad.reshape(batch, width),
        e_query.reshape(batch, width),
        e_context.reshape(batch, width),
        key_sums.reshape(batch, HEADS * width),
        value_sums.reshape(batch, HEADS * width),
    )
    own_small = jnp.where(encoder, jnp.concatenate(e_small), jnp.concatenate(small))
    payload = jnp.concatenate([piece.reshape(-1) for piece in factors] + [own_small.astype(BF)])
    gathered = lax.all_gather(payload, "dp")
    everyone = []
    place = 0
    for piece in factors:
        everyone.append(gathered[:, place : place + piece.size].reshape((-1,) + piece.shape[1:]))
        place += piece.size
    small_sum = jnp.sum(gathered[:, place:].astype(F32), axis=0)
    small_out = []
    place = 0
    for piece in small:
        small_out.append(small_sum[place : place + piece.size])
        place += piece.size

    def heads(piece):
        return piece.reshape(piece.shape[0], HEADS, -1)

    qkv_pieces = (
        dot("bd,be->de", everyone[6], everyone[7]),
        dot("bhd,bhe->dhe", heads(everyone[10]), heads(everyone[8])).reshape(width, width),
        dot("bhd,bhe->dhe", heads(everyone[11]), heads(everyone[9])).reshape(width, width),
    )
    encoder_grads = (
        dot("bi,bd->id", everyone[0], everyone[1]),
        dot("bd,bi->di", everyone[2], everyone[3]),
        dot("bd,be->de", everyone[4], everyone[5]),
        jnp.concatenate(qkv_pieces, axis=1),
    )
    outer_out, inner_out, proj_out, qkv_out = (
        jnp.where(encoder, first, second) for first, second in zip(encoder_grads, decoder_grads)
    )
    later = jnp.where(jnp.arange(length)[None, :, None] > 0, input_grad, 0.0)
    embed_grads = jnp.where(encoder, e_input_grad, later)
    outputs = (
        result.astype(BF),
        embed_grads,
        qkv_out,
        small_out[0],
        small_out[1],
        proj_out,
        small_out[2],
        small_out[3],
        small_out[4],
        inner_out,
        small_out[5],
        outer_out,
        small_out[6],
        small_out[7],
        small_out[8],
    )
    return tuple(piece[None] for piece in outputs)


def solution(mesh):
    matrix = P("section", None, None)
    vector = P("section", None)
    return jax.shard_map(
        local,
        mesh=mesh,
        in_specs=(P("section", "dp", None, None), P("dp", None, None), P("dp"))
        + (matrix, vector, vector, matrix, vector, vector, vector)
        + (matrix, vector, matrix, vector, vector, vector),
        out_specs=(P("section", "dp", None, None), P("section", "dp", None, None))
        + (matrix, vector, vector, matrix, vector, vector, vector)
        + (matrix, vector, matrix, vector, vector, vector),
        check_vma=False,
    )
```

```python
import math

import jax
import jax.numpy as jnp
from jax import lax
from jax.experimental import pallas as pl
from jax.experimental.pallas import tpu as pltpu
from jax.sharding import PartitionSpec as P

HEADS = 12
HEAD_DIM = 64
PAIR = 2 * HEAD_DIM
EPSILON = 1e-06
BIG_NEG = -1e30
BF = jnp.bfloat16
F32 = jnp.float32
CHUNK = 768
STRIP = 512
GROUP = 16
ROW_TILE = 16
ORDERS = (((1, 4, 2, 8), (2, 8, 1, 4)), ((1, 2, 8, 4), (2, 1, 4, 8)), ((4, 1, 2, 8), (8, 2, 1, 4)))
SWAP = ((0, 1), (1, 0))
KEY_SUMS, VALUE_SUMS, VECTORS, ACTS, INNERS, SMALLS, PAYLOAD = 0, 32, 64, 80, 88, 96, 112
V_OUTER, V_NORMED, V_CONTEXT, V_PROJ, V_INPUT, V_GQUERY, V_QUERY, V_GCONTEXT = range(8)


def params_of(mebibytes):
    return pltpu.CompilerParams(vmem_limit_bytes=mebibytes * 1024 * 1024)


def cost(micros):
    return pl.CostEstimate(flops=int(micros * 1.1e9), bytes_accessed=int(micros * 2e6), transcendentals=0)


def nn(left, right):
    return lax.dot_general(left, right, (((1,), (0,)), ((), ())), preferred_element_type=F32)


def nt(left, right):
    return lax.dot_general(left, right, (((1,), (1,)), ((), ())), preferred_element_type=F32)


def tn(left, right):
    return lax.dot_general(left, right, (((0,), (0,)), ((), ())), preferred_element_type=F32)


def turned(value):
    return jnp.transpose(value.astype(F32)).astype(BF)


def col_sum(value):
    return jnp.sum(value.astype(F32), axis=0, keepdims=True)


def row_norm(hidden):
    centred = hidden - jnp.mean(hidden, axis=-1, keepdims=True)
    scale = lax.rsqrt(jnp.mean(centred * centred, axis=-1, keepdims=True) + EPSILON)
    return (centred * scale, scale)


def norm_back(grad, normal, scale, gain):
    scaled = grad * gain
    return scale * (
        scaled
        - jnp.mean(scaled, axis=-1, keepdims=True)
        - normal * jnp.mean(scaled * normal, axis=-1, keepdims=True)
    )


def gelu_pair(value):
    bell = jnp.exp(-0.5 * (value * value))
    t = 1.0 / (1.0 + (0.3275911 / math.sqrt(2.0)) * jnp.abs(value))
    series = 0.5307027145 * t - 0.7265760135
    series = series * t + 0.7107068705
    series = series * t - 0.142248368
    series = series * t + 0.127414796
    tail = (series * t) * bell
    mass = jnp.where(value >= 0.0, 1.0 - tail, tail)
    return (value * mass, mass + value * (bell * (1.0 / math.sqrt(2.0 * math.pi))))


def fetch(first, own, other, target, sem):
    @pl.when(first)
    def _():
        pltpu.make_async_copy(own, target, sem).start()

    @pl.when(jnp.logical_not(first))
    def _():
        pltpu.make_async_copy(other, target, sem).start()


def landed(own, target, sem):
    pltpu.make_async_copy(own, target, sem).wait()


FAR = pl.BlockSpec(memory_space=pltpu.HBM)
SCALARS = pl.BlockSpec(memory_space=pltpu.SMEM)
NEAR = pl.BlockSpec(memory_space=pltpu.VMEM)


def struct(shape, kind):
    return jax.ShapeDtypeStruct(tuple(shape), kind)


def near(shape, kind):
    return pltpu.VMEM(tuple(shape), kind)


def full(shape):
    return pl.BlockSpec(tuple(shape), lambda *_: (0,) * len(shape))


def far(*values):
    return tuple(pltpu.with_memory_space_constraint(value, pltpu.HBM) for value in values)


def stay(*values):
    return tuple(pltpu.with_memory_space_constraint(value, pltpu.VMEM) for value in values)


QUERY_B, VALUE_B, PROJ_B, ATTN_G, ATTN_B, INNER_B, OUTER_B, FFN_G, FFN_B = range(9)
TABLE_ROWS = (0, 1, 2, 3, 4, 5, 9, 10, 11)


def layer_vectors(mine, other, own):
    def pick(k, part=0):
        row = TABLE_ROWS[k] + part
        return jnp.where(own, mine[row : row + 1, :], other[row : row + 1, :])

    return pick


def qkv_kernel(info_ref, x_ref, w_ref, *refs):
    vectors = refs[:9]
    qb_ref, vb_ref = vectors[QUERY_B], vectors[VALUE_B]
    own_ref, other_ref, table_ref = refs[9:]
    step = pl.program_id(0)
    half = pl.num_programs(0) // 2
    width = x_ref.shape[2]
    x = x_ref[0]

    def put(ref):
        for k, shift in enumerate((qb_ref[...], None, vb_ref[...])):
            made = nn(x, w_ref[:, k * width : (k + 1) * width])
            ref[:, k * width : (k + 1) * width] = (made if shift is None else made + shift).astype(BF)
        ref[:, 3 * width :] = x

    pl.when(step < half)(lambda: put(other_ref))
    pl.when(step >= half)(lambda: put(own_ref))

    @pl.when(step == 0)
    def _():
        for ref, row in zip(vectors, TABLE_ROWS):
            for part in range(ref.shape[1] // width):
                table_ref[row + part : row + part + 1, :] = ref[:, part * width : (part + 1) * width]


def qkv_call(info, inputs, weight, vectors, rows=256):
    count, length, width = inputs.shape
    wide = weight.shape[1] + width
    half = length // rows
    return pl.pallas_call(
        qkv_kernel,
        grid_spec=pltpu.PrefetchScalarGridSpec(
            num_scalar_prefetch=1,
            grid=(2 * half,),
            in_specs=[
                pl.BlockSpec(
                    (1, rows, width),
                    lambda i, info: (jnp.where(i < half, 1 - info[0], info[0]), lax.rem(i, half), 0),
                ),
                pl.BlockSpec(weight.shape, lambda i, info: (0, 0), pipeline_mode=pl.Buffered(1)),
            ]
            + [full(v.shape) for v in vectors],
            out_specs=[
                pl.BlockSpec((rows, wide), lambda i, info: (jnp.maximum(i - half, 0), 0)),
                pl.BlockSpec((rows, wide), lambda i, info: (jnp.minimum(i, half - 1), 0)),
                full((ROW_TILE, width)),
            ],
        ),
        out_shape=[struct((length, wide), BF)] * 2 + [struct((ROW_TILE, width), F32)],
        compiler_params=params_of(16),
        cost_estimate=cost(6),
        name="qkv",
    )(info, *far(inputs, weight, *vectors))


def by_head(value, rows):
    width = value.shape[1]
    lane = lax.broadcasted_iota(jnp.int32, (rows, width), 1)
    row = lax.broadcasted_iota(jnp.int32, (rows, width), 0)
    return jnp.where((lane >= row * HEAD_DIM) & (lane < (row + 1) * HEAD_DIM), value, jnp.zeros((), value.dtype))


def heads_of(value):
    rows, width = value.shape
    lane = lax.broadcasted_iota(jnp.int32, (rows, width), 1)
    row = lax.broadcasted_iota(jnp.int32, (rows, width), 0)
    kept = jnp.where((lane >= row * HEAD_DIM) & (lane < (row + 1) * HEAD_DIM), value, 0.0)
    return jnp.sum(kept, axis=0, keepdims=True)


def two_rows(first, second):
    rows = lax.broadcasted_iota(jnp.int32, (ROW_TILE, first.shape[1]), 0)
    zero = jnp.zeros((), first.dtype)
    return jnp.where(rows == 0, first, jnp.where(rows == 1, second, zero))


def head_kernel(
    info_ref, own_ref, other_ref, wp_ref, wi_ref, wo_ref, table,
    e_ref, probs_ref, c_ref, n1_ref, r1_ref, a_ref, slope_ref, n2_ref, r2_ref,
    wp, wi, wo, sems,
):
    copies = [
        pltpu.make_async_copy(wp_ref, wp, sems.at[0]),
        pltpu.make_async_copy(wi_ref, wi, sems.at[1]),
        pltpu.make_async_copy(wo_ref, wo, sems.at[2]),
    ]
    for copy in copies:
        copy.start()
    pick = layer_vectors(table, table, info_ref[0] == 0)
    width, ff = wi.shape
    length = own_ref.shape[0]
    lane = lax.broadcasted_iota(jnp.int32, (ROW_TILE, length), 1)
    contexts = []
    for i, ref in enumerate((own_ref, other_ref)):
        query = by_head(ref[0:1, 0:width] * jnp.asarray(0.125, BF), ROW_TILE)
        scores = nt(query, ref[:, width : 2 * width])
        scores = jnp.where(lane < info_ref[1 + i], scores, BIG_NEG)
        raised = jnp.exp(scores - jnp.max(scores, axis=-1, keepdims=True))
        probs = raised / jnp.sum(raised, axis=-1, keepdims=True)
        probs_ref[i] = probs
        contexts.append(heads_of(nn(probs.astype(BF), ref[:, 2 * width : 3 * width])))
    context = two_rows(*contexts).astype(BF)
    c_ref[...] = context
    inputs = two_rows(own_ref[0:1, 3 * width :], other_ref[0:1, 3 * width :])
    copies[0].wait()
    n1, r1 = row_norm(inputs.astype(F32) + (nn(context, wp[...]) + pick(PROJ_B)))
    n1_ref[...] = n1
    r1_ref[...] = r1
    normed = n1 * pick(ATTN_G) + pick(ATTN_B)
    copies[1].wait()
    low = normed.astype(BF)
    for c in range(ff // width):
        cols = slice(c * width, (c + 1) * width)
        act, slope = gelu_pair(nn(low, wi[:, cols]) + pick(INNER_B, c))
        a_ref[:, cols] = act.astype(BF)
        slope_ref[:, cols] = slope
    copies[2].wait()
    n2, r2 = row_norm(normed + (nn(a_ref[...], wo[...]) + pick(OUTER_B)))
    n2_ref[...] = n2
    r2_ref[...] = r2
    e_ref[...] = (n2 * pick(FFN_G) + pick(FFN_B)).astype(BF)


def head_call(info, own, other, wp, wi, wo, table):
    length = own.shape[0]
    width, ff = wi.shape
    shapes = [
        struct((ROW_TILE, width), BF),
        struct((2, ROW_TILE, length), F32),
        struct((ROW_TILE, width), BF),
        struct((ROW_TILE, width), F32),
        struct((ROW_TILE, 1), F32),
        struct((ROW_TILE, ff), BF),
        struct((ROW_TILE, ff), F32),
        struct((ROW_TILE, width), F32),
        struct((ROW_TILE, 1), F32),
    ]
    return pl.pallas_call(
        head_kernel,
        in_specs=[SCALARS, NEAR, NEAR, FAR, FAR, FAR, NEAR],
        out_specs=[NEAR] * len(shapes),
        out_shape=shapes,
        scratch_shapes=[pltpu.VMEM(w.shape, BF) for w in (wp, wi, wo)] + [pltpu.SemaphoreType.DMA((3,))],
        compiler_params=params_of(24),
        cost_estimate=cost(7),
        name="head_rows",
    )(info, own, other, *far(wp, wi, wo), table)


def attention_parts(xq, j, width, lane, bias_col):
    base = pl.multiple_of(j * PAIR, PAIR)
    q = xq[:, pl.ds(base, PAIR)] * jnp.asarray(0.125, BF)
    k = xq[:, pl.ds(base + width, PAIR)]
    v = xq[:, pl.ds(base + 2 * width, PAIR)]
    zero = jnp.zeros_like(k)
    parts = []
    for h in range(2):
        mine = (lane >= HEAD_DIM * h) & (lane < HEAD_DIM * (h + 1))
        spare = lane == HEAD_DIM * (1 - h)
        qh = jnp.where(mine, q, jnp.where(spare, jnp.ones_like(q), zero))
        kh = jnp.where(mine, k, jnp.where(spare, bias_col, zero))
        parts.append((mine, qh, kh))
    return base, q, k, v, parts


def place_rows(ref, value, order):
    pieces, rows = ref.shape[0], ref.shape[1]
    for p in range(pieces):
        ref[jnp.bitwise_xor(p, order)] = value[p * rows : (p + 1) * rows, :]


def forward_kernel(train, info_ref, *refs):
    xq_a, xq_b, wq_a, wq_b, wp_a, wp_b, wi_a, wi_b, wo_a, wo_b, mine, table = refs[:12]
    if train:
        head_ref, arrived_ref, cot_ref = refs[12:15]
        (z_ref, xq, wp, wi, wo, ctx, lse_ref, n1_ref, r1_ref, slope_ref, gf_ref, sg_ref, small_ref, keep_ref, send_ref) = refs[15:30]
        wq, lse_scr, acts, cot, sems = refs[30:]
    else:
        z_ref, xq, wp, wi, wo, ctx, sems = refs[12:]
    section = info_ref[0]
    own = section == (1 if train else 0)
    fetch(own, xq_a, xq_b, xq, sems.at[0])
    if train:
        fetch(own, wq_a, wq_b, wq, sems.at[1])
        pltpu.make_async_copy(cot_ref.at[section], cot, sems.at[5]).start()
    fetch(own, wp_a, wp_b, wp, sems.at[2])
    width = wp.shape[0]
    length = xq.shape[0]
    ff = wi.shape[1]
    pick = layer_vectors(mine, table, own)
    count = info_ref[1]
    row = lax.broadcasted_iota(jnp.int32, (length, PAIR), 0)
    lane = lax.broadcasted_iota(jnp.int32, (length, PAIR), 1)
    bias_col = jnp.where(row < count, 0.0, BIG_NEG).astype(BF)
    if train:
        first = jnp.where(section == 0, head_ref[0:1, :], arrived_ref[1:2, :])
        many = jnp.broadcast_to(first, (ROW_TILE, width))
        landed(wq_a, wq, sems.at[1])
        fixed = []
        for k, shift in enumerate((pick(QUERY_B), None, pick(VALUE_B))):
            made = nn(many, wq[:, k * width : (k + 1) * width])
            fixed.append((made if shift is None else made + shift).astype(BF))
        fixed = jnp.concatenate(fixed + [many], axis=1)
    landed(xq_a, xq, sems.at[0])
    fetch(own, wi_a, wi_b, wi, sems.at[3])
    fetch(own, wo_a, wo_b, wo, sems.at[4])
    if train:
        top_rows = xq[0:ROW_TILE, :]
        at_first = lax.broadcasted_iota(jnp.int32, top_rows.shape, 0) == 0
        xq[0:ROW_TILE, :] = jnp.where(at_first, fixed, top_rows)

    def pair_body(j, carry):
        base, q, k, v, parts = attention_parts(xq, j, width, lane, bias_col)
        sides = []
        for h, (mine, qh, kh) in enumerate(parts):
            vh = jnp.where(mine, v, jnp.ones_like(v))
            for s in range(length // STRIP):
                rows = slice(s * STRIP, (s + 1) * STRIP)
                scores = nt(qh[rows, :], kh)
                top = jnp.max(scores, axis=-1, keepdims=True)
                made = nn(jnp.exp(scores - top).astype(BF), vh)
                mass = made[:, HEAD_DIM * (1 - h) : HEAD_DIM * (1 - h) + 1]
                sides.append(made * (1.0 / mass))
                if train:
                    spot = lane[rows, :] == 2 * j + h
                    lse_scr[rows, :] = jnp.where(spot, top + jnp.log(mass), lse_scr[rows, :])
        count_strips = length // STRIP
        for s in range(count_strips):
            rows = slice(s * STRIP, (s + 1) * STRIP)
            both = jnp.where(lane[rows, :] < HEAD_DIM, sides[s], sides[count_strips + s])
            ctx[rows, pl.ds(base, PAIR)] = both.astype(BF)
        return carry

    lax.fori_loop(0, HEADS // 2, pair_body, 0)
    if train:
        lse_ref[...] = jnp.transpose(lse_scr[...])[0:ROW_TILE, :]
    inputs = xq[:, 3 * width :]
    landed(wp_a, wp, sems.at[2])
    n1, r1 = row_norm(inputs.astype(F32) + (nn(ctx[...], wp[...]) + pick(PROJ_B)))
    normed = n1 * pick(ATTN_G) + pick(ATTN_B)
    low = normed.astype(BF)
    if train:
        n1_ref[...] = n1
        r1_ref[...] = r1
    landed(wi_a, wi, sems.at[3])
    landed(wo_a, wo, sems.at[4])
    total = None
    for c in range(ff // CHUNK):
        cols = slice(c * CHUNK, (c + 1) * CHUNK)
        act, slope = gelu_pair(nn(low, wi[:, cols]) + pick(INNER_B, c))
        act = act.astype(BF)
        if train:
            acts[:, cols] = act
            slope_ref[:, cols] = slope.astype(BF)
        term = nn(act, wo[cols, :])
        total = term if total is None else total + term
    n2, r2 = row_norm(normed + (total + pick(OUTER_B)))
    gain = pick(FFN_G)
    z_ref[...] = (n2 * gain + pick(FFN_B)).astype(BF)
    if not train:
        return
    wide_row = lax.broadcasted_iota(jnp.int32, n2.shape, 0)
    pltpu.make_async_copy(cot_ref.at[section], cot, sems.at[5]).wait()
    grad = jnp.where(wide_row < count, cot[...].astype(F32), 0.0)
    second = norm_back(grad, n2, r2, gain)
    sg_ref[...] = second
    gf = second.astype(BF)
    gf_ref[...] = gf
    small_ref[0:1, :] = col_sum(gf)
    small_ref[1:2, :] = col_sum(grad * n2)
    small_ref[2:3, :] = col_sum(grad)
    half_chunks = ff // CHUNK // 2
    rows = send_ref.shape[1]
    each = CHUNK // rows
    for ref, half, order in ((send_ref, 1 - section, info_ref[4]), (keep_ref, section, info_ref[3])):
        for c in range(half_chunks):
            cols = pl.ds(pl.multiple_of((half * half_chunks + c) * CHUNK, CHUNK), CHUNK)
            made = tn(acts[:, cols], gf).astype(BF)
            for p in range(each):
                ref[jnp.bitwise_xor(c * each + p, order)] = made[p * rows : (p + 1) * rows, :]


def forward_call(train, info, pairs, tables, head=None, arrived=None, cot=None):
    xq, wq, wp, wi, wo = (piece[0] for piece in pairs)
    length = xq.shape[0]
    width, ff = wi.shape
    flat = [piece for pair in pairs for piece in pair]
    args = [info] + list(far(*flat)) + list(tables)
    in_specs = [SCALARS] + [FAR] * 10 + [NEAR] * 2
    weights = [near(w.shape, BF) for w in (wp, wi, wo)]
    if train:
        args += [head, arrived] + list(far(cot))
        in_specs += [NEAR, NEAR, FAR]
        shapes = [struct((length, width), BF), near(xq.shape, BF)] + weights
        shapes += [
            near((length, width), BF),
            near((ROW_TILE, length), F32),
            near((length, width), F32),
            near((length, 1), F32),
            near((length, ff), BF),
            near((length, width), BF),
            near((length, width), F32),
            near((8, width), F32),
            near((GROUP, ff // 2 // GROUP, width), BF),
            near((GROUP, ff // 2 // GROUP, width), BF),
        ]
        scratch = [pltpu.VMEM(wq.shape, BF), pltpu.VMEM((length, PAIR), F32), pltpu.VMEM((length, ff), BF)]
        scratch.append(pltpu.VMEM((length, width), BF))
    else:
        shapes = [struct((length, width), BF)]
        scratch = [pltpu.VMEM(xq.shape, BF)] + weights + [pltpu.VMEM((length, width), BF)]
    scratch.append(pltpu.SemaphoreType.DMA((6,)))
    return pl.pallas_call(
        lambda *refs: forward_kernel(train, *refs),
        in_specs=in_specs,
        out_specs=[NEAR] * len(shapes),
        out_shape=shapes,
        scratch_shapes=scratch,
        compiler_params=params_of(20 if train else 24),
        cost_estimate=cost(26 if train else 19),
        name="layer_train" if train else "layer",
    )(*args)


def inner_kernel(
    info_ref, gf_ref, slope_ref, sg_ref, n1_ref, r1_ref, wi_ref, wo_ref, wp_ref, mine, table,
    keep_ref, send_ref, gh_ref, ga_ref, gc_ref, small_ref,
):
    section = info_ref[0]
    pick = layer_vectors(mine, table, section == 1)
    gain = pick(ATTN_G)
    low = jnp.transpose(n1_ref[...] * gain + pick(ATTN_B)).astype(BF)
    ff = wi_ref.shape[1]
    half_chunks = ff // CHUNK // 2
    gf = gf_ref[...]
    gn = sg_ref[...]
    for ref, half, order in ((send_ref, 1 - section, info_ref[6]), (keep_ref, section, info_ref[5])):
        for c in range(half_chunks):
            block = half * half_chunks + c
            cols = pl.ds(pl.multiple_of(block * CHUNK, CHUNK), CHUNK)
            gu = (nt(gf, wo_ref[cols, :]) * slope_ref[:, cols].astype(F32)).astype(BF)
            small_ref[pl.ds(3 + block, 1), :] = col_sum(gu)
            place_rows(ref.at[:, :, c * CHUNK : (c + 1) * CHUNK], nn(low, gu).astype(BF), order)
            gn = gn + nt(gu, wi_ref[:, cols])
    n1 = n1_ref[...]
    gh = norm_back(gn, n1, r1_ref[...], gain)
    gh_ref[...] = gh
    ga = gh.astype(BF)
    ga_ref[...] = ga
    gc_ref[...] = nt(ga, wp_ref[...]).astype(BF)
    small_ref[0:1, :] = col_sum(ga)
    small_ref[1:2, :] = col_sum(gn * n1)
    small_ref[2:3, :] = col_sum(gn)


def inner_call(info, gf, slope, sg, n1, r1, wi, wo, wp, tables):
    tokens, width = gf.shape
    ff = wi.shape[1]
    shapes = [
        near((GROUP, width // GROUP, ff // 2), BF),
        near((GROUP, width // GROUP, ff // 2), BF),
        near((tokens, width), F32),
        near((tokens, width), BF),
        near((tokens, width), BF),
        near((8, width), F32),
    ]
    return pl.pallas_call(
        inner_kernel,
        in_specs=[SCALARS] + [NEAR] * 10,
        out_specs=[NEAR] * len(shapes),
        out_shape=shapes,
        compiler_params=params_of(12),
        cost_estimate=cost(10),
        name="inner_grad",
    )(info, *stay(gf, slope, sg, n1, r1, wi, wo, wp), *tables)


def attention_kernel(
    info_ref, xq, gc_ref, ga_ref, c_ref, lse_ref, keep_ref, send_ref, g_ref, small_ref, xt_scr, ct_scr, mean_scr
):
    section = info_ref[0]
    length, width = gc_ref.shape
    row = lax.broadcasted_iota(jnp.int32, (length, PAIR), 0)
    lane = lax.broadcasted_iota(jnp.int32, (length, PAIR), 1)
    bias_col = jnp.where(row < info_ref[1], 0.0, BIG_NEG).astype(BF)
    ct_scr[...] = turned(c_ref[...])
    xt_scr[...] = turned(xq[:, 3 * width :])
    product = gc_ref[...].astype(F32) * c_ref[...].astype(F32)
    high = product.astype(BF)
    low = (product - high.astype(F32)).astype(BF)
    ones = by_head(jnp.ones((1, width), BF), ROW_TILE)
    mean_scr[...] = nt(ones, high) + nt(ones, low)

    def pair_body(j, carry):
        base, q, k, v, parts = attention_parts(xq, j, width, lane, bias_col)
        kt = turned(k)
        gc = gc_ref[:, pl.ds(base, PAIR)]
        zero = jnp.zeros_like(gc)
        strips = [slice(s * STRIP, (s + 1) * STRIP) for s in range(length // STRIP)]
        gk = [None] * len(strips)
        gv = [None] * len(strips)
        gqt = []
        for h, (mine, qh, kh) in enumerate(parts):
            gch = jnp.where(mine, gc, zero)
            qz = jnp.where(mine, q, zero)
            lse = lse_ref[pl.ds(2 * j + h, 1), :]
            mean = mean_scr[pl.ds(2 * j + h, 1), :]
            gq_h = None
            for s, rows in enumerate(strips):
                probs = jnp.exp(nt(kh[rows, :], qh) - lse)
                gs = (probs * (nt(v[rows, :], gch) - mean)).astype(BF)
                gv_h = nn(probs.astype(BF), gch)
                gk_h = nn(gs, qz)
                term = nn(kt[HEAD_DIM * h : HEAD_DIM * (h + 1), rows], gs)
                gq_h = term if gq_h is None else gq_h + term
                gk[s] = gk_h if h == 0 else gk[s] + gk_h
                gv[s] = gv_h if h == 0 else gv[s] + gv_h
            gqt.append(gq_h)
        gq = jnp.transpose(jnp.concatenate(gqt, axis=0)) * 0.125
        g_ref[:, pl.ds(base, PAIR)] = gq.astype(BF)
        for s, rows in enumerate(strips):
            g_ref[rows, pl.ds(base + width, PAIR)] = gk[s].astype(BF)
            g_ref[rows, pl.ds(base + 2 * width, PAIR)] = gv[s].astype(BF)
        return carry

    lax.fori_loop(0, HEADS // 2, pair_body, 0)
    small_ref[0:1, :] = col_sum(g_ref[:, 0:width])
    small_ref[1:2, :] = col_sum(g_ref[:, 2 * width : 3 * width])
    wide = 3 * width // 2
    for ref, half, order in ((send_ref, 1 - section, info_ref[8]), (keep_ref, section, info_ref[7])):
        cols = pl.ds(pl.multiple_of(half * wide, PAIR), wide)
        place_rows(ref.at[:, :, 0:wide], nn(xt_scr[...], g_ref[:, cols]).astype(BF), order)
        cols = pl.ds(pl.multiple_of(half * (width // 2), PAIR), width // 2)
        place_rows(ref.at[:, :, wide:], nn(ct_scr[...], ga_ref[:, cols]).astype(BF), order)


def attention_call(info, xq, gc, ga, context, lse):
    length, width = gc.shape
    shapes = [
        near((GROUP, width // GROUP, 2 * width), BF),
        near((GROUP, width // GROUP, 2 * width), BF),
        near((length, 3 * width), BF),
        near((8, width), F32),
    ]
    return pl.pallas_call(
        attention_kernel,
        in_specs=[SCALARS] + [NEAR] * 5,
        out_specs=[NEAR] * len(shapes),
        out_shape=shapes,
        scratch_shapes=[
            pltpu.VMEM((width, length), BF),
            pltpu.VMEM((width, length), BF),
            pltpu.VMEM((ROW_TILE, length), F32),
        ],
        compiler_params=params_of(16),
        cost_estimate=cost(14),
        name="attention_grad",
    )(info, *stay(xq, gc, ga, context, lse))


def input_kernel(info_ref, w_a, w_b, g_ref, gh_ref, small1_ref, small2_ref, small3_ref, o_ref, small_ref, w, sem):
    fetch(info_ref[0] == 1, w_a, w_b, w, sem)
    landed(w_a, w, sem)
    made = gh_ref[...] + nt(g_ref[...], w[...])
    o_ref[...] = made
    small_ref[0:2, :] = small3_ref[0:2, :]
    small_ref[2:9, :] = small2_ref[0:7, :]
    small_ref[9:12, :] = small1_ref[0:3, :]
    small_ref[12:16, :] = made[0:4, :]


def input_call(info, g, gh, w, small1, small2, small3):
    return pl.pallas_call(
        input_kernel,
        in_specs=[SCALARS, FAR, FAR] + [NEAR] * 5,
        out_specs=[NEAR] * 2,
        out_shape=[struct(gh.shape, F32), struct((ROW_TILE, gh.shape[1]), F32)],
        scratch_shapes=[pltpu.VMEM(w[0].shape, BF), pltpu.SemaphoreType.DMA(())],
        compiler_params=params_of(12),
        cost_estimate=cost(4),
        name="input_grad",
    )(info, *far(*w), *stay(g, gh, small1, small2, small3))


def head_back_kernel(
    info_ref, small_a, small_b, probs_ref, c_ref, n1_ref, r1_ref, a_ref, slope_ref, n2_ref, r2_ref, own_ref, other_ref,
    wq_ref, wp_ref, wi_ref, wo_ref, table, x_ref, pay_ref, wq, wp, wi, wo, sems,
):
    copies = [
        pltpu.make_async_copy(ref, scr, sems.at[i])
        for i, (ref, scr) in enumerate(((wo_ref, wo), (wi_ref, wi), (wp_ref, wp), (wq_ref, wq)))
    ]
    for copy in copies:
        copy.start()
    width = wp.shape[0]
    length = own_ref.shape[0]
    ff = wi.shape[1]
    n1, n2 = n1_ref[...], n2_ref[...]
    pick = layer_vectors(table, table, info_ref[0] == 0)
    grad = two_rows(small_a[12:13, :], small_b[12:13, :]).astype(BF).astype(F32)
    second = norm_back(grad, n2, r2_ref[...], pick(FFN_G))
    gf = second.astype(BF)
    copies[0].wait()
    gu = (nt(gf, wo[...]) * slope_ref[...]).astype(BF)
    copies[1].wait()
    gn = second + nt(gu, wi[...])
    gh = norm_back(gn, n1, r1_ref[...], pick(ATTN_G))
    ga = gh.astype(BF)
    copies[2].wait()
    gc = nt(ga, wp[...]).astype(BF)
    normed = (n1 * pick(ATTN_G) + pick(ATTN_B)).astype(BF)
    copies[3].wait()
    query_bias = value_bias = jnp.zeros((1, width), F32)
    vectors = {}
    for i, ref in enumerate((own_ref, other_ref)):
        mid = (1 - 2 * i) * info_ref[0] + i
        keys, values, inputs = ref[:, width : 2 * width], ref[:, 2 * width : 3 * width], ref[:, 3 * width :]
        query = ref[0:1, 0:width] * jnp.asarray(0.125, BF)
        gc_row = gc[i : i + 1, :]
        query_heads, gc_heads = by_head(query, ROW_TILE), by_head(gc_row, ROW_TILE)
        probs = probs_ref[i]
        gp = nt(gc_heads, values)
        gs = (probs * (gp - jnp.sum(probs * gp, axis=-1, keepdims=True))).astype(BF)
        low = probs.astype(BF)
        gq = (heads_of(nn(gs, keys)) * 0.125).astype(BF)
        pay_ref[KEY_SUMS + 16 * i : KEY_SUMS + 16 * i + 16, :] = nn(gs, inputs).astype(BF)
        pay_ref[VALUE_SUMS + 16 * i : VALUE_SUMS + 16 * i + 16, :] = nn(low, inputs).astype(BF)
        key_back = nt(query_heads, wq[:, width : 2 * width]).astype(BF)
        value_back = nt(gc_heads, wq[:, 2 * width :]).astype(BF)
        gx = tn(gs, key_back) + tn(low, value_back)
        top = gh[i : i + 1, :] + nt(jnp.broadcast_to(gq, (ROW_TILE, width)), wq[:, 0:width])[0:1, :]
        at_first = lax.broadcasted_iota(jnp.int32, gx.shape, 0) == 0
        x_ref[mid] = gx + jnp.where(at_first, top, 0.0)
        query_bias = query_bias + gq.astype(F32)
        mass = jnp.sum(low.astype(F32), axis=-1, keepdims=True)
        value_bias = value_bias + heads_of(gc_heads.astype(F32) * mass)
        for key, piece in (
            (V_OUTER, gf[i : i + 1, :]),
            (V_NORMED, normed[i : i + 1, :]),
            (V_CONTEXT, c_ref[i : i + 1, :]),
            (V_PROJ, ga[i : i + 1, :]),
            (V_INPUT, ref[0:1, 3 * width :]),
            (V_GQUERY, gq),
            (V_QUERY, query),
            (V_GCONTEXT, gc_row),
        ):
            vectors[2 * key + i] = piece
    gu_sum = col_sum(gu)
    act = a_ref[...]
    own_small = [query_bias, value_bias, col_sum(ga), col_sum(gn * n1), col_sum(gn)]
    own_small += [gu_sum[:, width * k : width * (k + 1)] for k in range(ff // width)]
    own_small += [col_sum(gf), col_sum(grad * n2), col_sum(grad)]

    def stack(pieces):
        row = lax.broadcasted_iota(jnp.int32, (ROW_TILE, width), 0)
        made = jnp.zeros((ROW_TILE, width), F32)
        for k, piece in enumerate(pieces):
            made = jnp.where(row == k, piece.astype(F32), made)
        return made

    pay_ref[VECTORS : VECTORS + 16, :] = stack([vectors[k] for k in range(16)]).astype(BF)
    wide = [value[i : i + 1, width * k : width * (k + 1)] for value in (act, gu) for i in range(2) for k in range(ff // width)]
    pay_ref[ACTS : ACTS + 16, :] = stack(wide).astype(BF)
    pay_ref[SMALLS : SMALLS + 16, :] = jnp.where(info_ref[0] == 0, stack(own_small), small_a[...] + small_b[...]).astype(BF)


def head_back_call(info, small_a, small_b, saved, own, other, wq, wp, wi, wo, table):
    length = own.shape[0]
    width, ff = wi.shape
    args = [small_a, small_b] + list(saved) + [own, other]
    return pl.pallas_call(
        head_back_kernel,
        in_specs=[SCALARS] + [NEAR] * len(args) + [FAR] * 4 + [NEAR],
        out_specs=[NEAR] * 2,
        out_shape=[struct((2, length, width), F32), struct((PAYLOAD, width), BF)],
        scratch_shapes=[pltpu.VMEM(w.shape, BF) for w in (wq, wp, wi, wo)] + [pltpu.SemaphoreType.DMA((4,))],
        compiler_params=params_of(28),
        cost_estimate=cost(12),
        name="head_rows_grad",
    )(info, *args, *far(wq, wp, wi, wo), table)


def outer_final_kernel(info_ref, low_ref, high_ref, gt_ref, o_ref):
    step = pl.program_id(0)
    rows = low_ref.shape[1]
    each = o_ref.shape[0] // rows
    per_half = pl.num_programs(0) // 2

    @pl.when(info_ref[0] == 1)
    def _():
        def fill(ref, first, order):
            for p in range(each):
                o_ref[p * rows : (p + 1) * rows, :] = ref[jnp.bitwise_xor(first + p, order)].astype(F32)

        pl.when(step < per_half)(lambda: fill(low_ref, step * each, info_ref[4]))
        pl.when(step >= per_half)(lambda: fill(high_ref, (step - per_half) * each, info_ref[3]))

    @pl.when(info_ref[0] == 0)
    def _():
        made = None
        for j in range(2):
            left = gt_ref[ACTS + 4 * j + step]
            term = tn(left, gt_ref[VECTORS + 2 * V_OUTER + j])
            made = term if made is None else made + term
        o_ref[...] = made


def outer_final_call(info, low, high, gt):
    width = low.shape[2]
    ff = 2 * low.shape[0] * low.shape[1]
    return pl.pallas_call(
        outer_final_kernel,
        grid=(ff // width,),
        in_specs=[SCALARS, full(low.shape), full(high.shape), full(gt.shape)],
        out_specs=pl.BlockSpec((width, width), lambda i: (i, 0)),
        out_shape=struct((ff, width), F32),
        compiler_params=params_of(32),
        cost_estimate=cost(5),
        name="outer_final",
    )(info, low, high, gt)


def unfold(ref, cols, order, target):
    rows = ref.shape[1]
    for p in range(ref.shape[0]):
        target[p * rows : (p + 1) * rows, :] = ref[jnp.bitwise_xor(p, order), :, cols].astype(F32)


def inner_final_kernel(info_ref, low_ref, high_ref, gt_ref, o_ref):
    step = pl.program_id(0)
    width = o_ref.shape[1]

    @pl.when(info_ref[0] == 1)
    def _():
        for k in range(4):
            ref, order = ((low_ref, info_ref[6]), (high_ref, info_ref[5]))[k // 2]
            cols = slice((k % 2) * width, (k % 2 + 1) * width)
            pl.when(step == k)(lambda ref=ref, order=order, cols=cols: unfold(ref, cols, order, o_ref))

    @pl.when(info_ref[0] == 0)
    def _():
        made = None
        for j in range(2):
            term = tn(gt_ref[VECTORS + 2 * V_NORMED + j], gt_ref[INNERS + 4 * j + step])
            made = term if made is None else made + term
        o_ref[...] = made


def inner_final_call(info, low, high, gt):
    width = gt.shape[2]
    ff = 2 * low.shape[2]
    return pl.pallas_call(
        inner_final_kernel,
        grid=(ff // width,),
        in_specs=[SCALARS, full(low.shape), full(high.shape), full(gt.shape)],
        out_specs=pl.BlockSpec((width, width), lambda i: (0, i)),
        out_shape=struct((width, ff), F32),
        compiler_params=params_of(32),
        cost_estimate=cost(5),
        name="inner_final",
    )(info, low, high, gt)


def qkv_final_kernel(info_ref, low_ref, high_ref, gt_ref, o_ref, p_ref):
    width = p_ref.shape[0]
    wide = 3 * width // 2
    half = width // 2

    @pl.when(info_ref[0] == 1)
    def _():
        for ref, order, k in ((low_ref, info_ref[8], 0), (high_ref, info_ref[7], 1)):
            unfold(ref, slice(0, wide), order, o_ref.at[:, k * wide : (k + 1) * wide])
            unfold(ref, slice(wide, wide + half), order, p_ref.at[:, k * half : (k + 1) * half])

    @pl.when(info_ref[0] == 0)
    def _():
        def pairs(left, right):
            return tn(gt_ref[VECTORS + 2 * left], gt_ref[VECTORS + 2 * right]) + tn(
                gt_ref[VECTORS + 2 * left + 1], gt_ref[VECTORS + 2 * right + 1]
            )

        p_ref[...] = pairs(V_CONTEXT, V_PROJ)
        o_ref[:, 0:width] = pairs(V_INPUT, V_GQUERY)
        chips = gt_ref.shape[1]
        lane = lax.broadcasted_iota(jnp.int32, (chips, width), 1)
        for place, base, key in ((1, KEY_SUMS, V_QUERY), (2, VALUE_SUMS, V_GCONTEXT)):
            made = None
            for j in range(2):
                left = gt_ref[base + 16 * j : base + 16 * j + HEADS].reshape(HEADS * chips, width)
                row = gt_ref[VECTORS + 2 * key + j]
                heads = [
                    jnp.where((lane >= HEAD_DIM * h) & (lane < HEAD_DIM * (h + 1)), row, jnp.zeros_like(row))
                    for h in range(HEADS)
                ]
                term = tn(left, jnp.concatenate(heads, axis=0))
                made = term if made is None else made + term
            o_ref[:, place * width : (place + 1) * width] = made


def qkv_final_call(info, low, high, gt):
    width = gt.shape[2]
    return pl.pallas_call(
        qkv_final_kernel,
        in_specs=[SCALARS, full(low.shape), full(high.shape), full(gt.shape)],
        out_specs=[full((width, 3 * width)), full((width, width))],
        out_shape=[struct((width, 3 * width), F32), struct((width, width), F32)],
        compiler_params=params_of(32),
        cost_estimate=cost(6),
        name="qkv_final",
    )(info, low, high, gt)


def swap(value):
    return lax.ppermute(value, "section", SWAP)


def add_low(left, right):
    return (left.astype(F32) + right.astype(F32)).astype(BF)


def hop(value, stage, orders):
    chips = lax.axis_size("dp")
    pairs = [
        (section * chips + chip, section * chips + (chip ^ orders[section][stage]))
        for section in range(2)
        for chip in range(chips)
    ]
    return lax.ppermute(value, ("section", "dp"), pairs)


def after(value, *others):
    return lax.optimization_barrier((value,) + others)[0]


def beside(made, *sums):
    tied = lax.optimization_barrier(tuple(made) + tuple(one.coming for one in sums))
    for one, coming in zip(sums, tied[len(made) :]):
        one.coming = coming
    return tied[: len(made)]


class Sum:
    def __init__(self, keep, send, group):
        self.part, self.coming, self.orders = keep, swap(send), ORDERS[group]

    def add(self):
        half = self.part.shape[0] if self.coming.shape[0] == self.part.shape[0] else self.part.shape[0] // 2
        self.part = add_low(self.part[:half], self.coming)
        return self.part

    def halve(self, stage):
        self.coming = hop(self.part[self.part.shape[0] // 2 :], stage, self.orders)

    def across(self):
        chips = lax.axis_size("dp")
        if chips > GROUP:
            groups = [[low + GROUP * high for high in range(chips // GROUP)] for low in range(GROUP)]
            self.part = lax.psum(self.part, "dp", axis_index_groups=groups)

    def double(self, stage):
        self.coming = hop(self.part, stage, self.orders)

    def join(self):
        self.part = jnp.concatenate([self.part, self.coming], axis=0)
        return self.part


def order_of(chip, orders):
    place = jnp.int32(0)
    for stage in range(4):
        bit = (chip // orders[stage]) % 2
        place = place + bit * (8 >> stage)
    return place


def local(embeddings, cotangent, lengths, *weights):
    (wq, query_bias, value_bias, wp, proj_bias, attn_gain, attn_bias, wi, inner_bias, wo, outer_bias, ffn_gain, ffn_bias) = (
        piece[0] for piece in weights
    )
    section = lax.axis_index("section")
    chip = lax.axis_index("dp")
    first_section = section == 0
    inputs = embeddings[0]
    width = inputs.shape[2]
    scalars = [section, jnp.where(first_section, lengths[0], lengths[1]), jnp.where(first_section, lengths[1], lengths[0])]
    for orders in ORDERS:
        places = [order_of(chip, order) for order in orders]
        scalars += [jnp.where(first_section, places[0], places[1]), jnp.where(first_section, places[1], places[0])]
    info = jnp.stack(scalars).astype(jnp.int32)
    vectors = [weights[k] for k in (1, 2, 4, 5, 6, 8, 10, 11, 12)]
    own, other, own_table = qkv_call(info, inputs, wq, vectors)
    tables = (own_table, swap(own_table))
    wp_pair = (wp, swap(wp))
    wi_pair = (wi, swap(wi))
    xq_pair = (own, swap(other))
    wq_pair = (wq, swap(wq))
    wo_pair = (wo, swap(wo))
    head = head_call(info, own, other, wp, wi, wo, own_table)
    arrived = swap(head[0])
    pairs = (xq_pair, wq_pair, wp_pair, wi_pair, wo_pair)
    (z, xq_d, wp_d, wi_d, wo_d, context, lse, n1, r1, slope, gf, sg, small1, outer_keep, outer_send) = forward_call(
        True, info, pairs, tables, head[0], arrived, cotangent
    )
    g1 = Sum(outer_keep, outer_send, 0)

    made = inner_call(info, gf, slope, sg, n1, r1, wi_d, wo_d, wp_d, tables)
    inner_keep, inner_send, gh, ga, gc, small2 = beside(made, g1)
    g1.add()
    g1.halve(0)
    g2 = Sum(inner_keep, inner_send, 1)

    made = attention_call(info, xq_d, after(gc, g1.part), ga, context, lse)
    qkv_keep, qkv_send, g_qkv, small3 = beside(made, g1, g2)
    g1.add()
    g1.halve(1)
    g2.add()
    g2.halve(0)
    g3 = Sum(qkv_keep, qkv_send, 2)

    made = input_call(info, after(g_qkv, g1.part, g2.part), gh, wq_pair, small1, small2, small3)
    gx, dsmall = beside(made, g3)
    g3.add()
    g3.halve(0)
    dsmall_other = after(swap(dsmall), g3.part)
    made = head_back_call(info, dsmall, dsmall_other, head[1:], own, other, wq, wp, wi, wo, own_table)
    encoder_gx, payload = beside(made, g1, g2, g3)
    gathered = lax.all_gather(payload, "dp")
    g1.add()
    g1.halve(2)
    g2.add()
    g2.halve(1)
    g3.add()
    g3.halve(1)
    gx_other = swap(gx)

    late = (own_table, after(tables[1], g1.part, g2.part, g3.part))
    made = forward_call(False, info, pairs, late)
    (e_low,) = beside(made, g1, g2, g3)
    g1.add()
    g1.halve(3)
    g2.add()
    g2.halve(2)
    g3.add()
    g3.halve(2)
    z_other = swap(jnp.where(first_section, z, e_low))
    z_mine = jnp.where(first_section, e_low, z)
    decoder_gx = jnp.stack([after(gx_other, g3.part), gx])
    later = jnp.arange(gx.shape[0])[None, :, None] > 0
    embed_grads = jnp.where(first_section, encoder_gx, jnp.where(later, decoder_gx, 0.0))
    (embed_grads,) = beside((embed_grads,), g1, g2, g3)

    g1.add()
    g1.across()
    g1.double(3)
    g2.add()
    g2.halve(3)
    g3.add()
    g3.halve(3)
    z_other = after(z_other, g3.part)
    outputs = jnp.where(first_section, jnp.stack([z_mine, z_other]), jnp.stack([z_other, z_mine]))
    (outputs,) = beside((outputs,), g1, g2, g3)
    g1.join()
    g1.double(2)
    g2.add()
    g2.across()
    g2.double(3)
    g3.add()
    g3.across()
    g3.double(3)
    g1.join()
    g1.double(1)
    g2.join()
    g2.double(2)
    g3.join()
    g3.double(2)
    g1.join()
    g1.double(0)
    g2.join()
    g2.double(1)
    g3.join()
    g3.double(1)
    gt = jnp.transpose(after(gathered, g3.part), (1, 0, 2))
    sums = jnp.sum(gt[SMALLS : SMALLS + 12].astype(F32), axis=1)
    gt, sums = beside((gt, sums), g1, g2, g3)
    outer_half = g1.join()
    outer_other = swap(outer_half)
    g2.join()
    g2.double(0)
    g3.join()
    g3.double(0)
    outer_grad = outer_final_call(info, after(outer_other, g2.part, g3.part), outer_half, gt)
    (outer_grad,) = beside((outer_grad,), g2, g3)
    inner_half = g2.join()
    inner_other = swap(inner_half)
    qkv_half = g3.join()
    qkv_other = swap(qkv_half)
    inner_grad = inner_final_call(info, after(inner_other, qkv_half), inner_half, gt)
    qkv_grad, proj_grad = qkv_final_call(info, after(qkv_other, inner_grad), qkv_half, gt)
    results = (
        outputs,
        embed_grads,
        qkv_grad,
        sums[0],
        sums[1],
        proj_grad,
        sums[2],
        sums[3],
        sums[4],
        inner_grad,
        sums[5:9].reshape(-1),
        outer_grad,
        sums[9],
        sums[10],
        sums[11],
    )
    return tuple(piece[None] for piece in results)


def solution(mesh):
    matrix = P("section", None, None)
    vector = P("section", None)
    return jax.shard_map(
        local,
        mesh=mesh,
        in_specs=(P("section", "dp", None, None), P("dp", None, None), P("dp"))
        + (matrix, vector, vector, matrix, vector, vector, vector)
        + (matrix, vector, matrix, vector, vector, vector),
        out_specs=(P("section", "dp", None, None), P("section", "dp", None, None))
        + (matrix, vector, vector, matrix, vector, vector, vector)
        + (matrix, vector, matrix, vector, vector, vector),
        check_vma=False,
    )
```

```python
import math

import jax
import jax.numpy as jnp
from jax import lax
from jax.experimental import pallas as pl
from jax.experimental.pallas import tpu as pltpu
from jax.sharding import PartitionSpec as P

HEADS = 12
HEAD_DIM = 64
PAIR = 2 * HEAD_DIM
EPSILON = 1e-06
BIG_NEG = -1e30
BF = jnp.bfloat16
F32 = jnp.float32
CHUNK = 768
STRIP = 512
GROUP = 16
ROW_TILE = 16
ORDERS = (((2, 1, 8, 4), (1, 4, 2, 8)), ((8, 1, 2, 4), (2, 4, 8, 1)), ((1, 2, 4, 8), (2, 1, 8, 4)))
SWAP = ((0, 1), (1, 0))
KEY_SUMS, VALUE_SUMS, VECTORS, ACTS, INNERS, FACTORS = 0, 24, 48, 64, 72, 80
V_OUTER, V_NORMED, V_CONTEXT, V_PROJ, V_INPUT, V_GQUERY, V_QUERY, V_GCONTEXT = range(8)


def params_of(mebibytes):
    return pltpu.CompilerParams(vmem_limit_bytes=mebibytes * 1024 * 1024)


def cost(micros):
    return pl.CostEstimate(flops=int(micros * 1.1e9), bytes_accessed=int(micros * 2e6), transcendentals=0)


def nn(left, right):
    return lax.dot_general(left, right, (((1,), (0,)), ((), ())), preferred_element_type=F32)


def nt(left, right):
    return lax.dot_general(left, right, (((1,), (1,)), ((), ())), preferred_element_type=F32)


def tn(left, right):
    return lax.dot_general(left, right, (((0,), (0,)), ((), ())), preferred_element_type=F32)


def turned(value):
    return jnp.transpose(value.astype(F32)).astype(BF)


def col_sum(value):
    return jnp.sum(value.astype(F32), axis=0, keepdims=True)


def row_norm(hidden):
    centred = hidden - jnp.mean(hidden, axis=-1, keepdims=True)
    scale = lax.rsqrt(jnp.mean(centred * centred, axis=-1, keepdims=True) + EPSILON)
    return (centred * scale, scale)


def norm_back(grad, normal, scale, gain):
    scaled = grad * gain
    return scale * (
        scaled
        - jnp.mean(scaled, axis=-1, keepdims=True)
        - normal * jnp.mean(scaled * normal, axis=-1, keepdims=True)
    )


def gelu_pair(value):
    bell = jnp.exp(-0.5 * (value * value))
    t = 1.0 / (1.0 + (0.3275911 / math.sqrt(2.0)) * jnp.abs(value))
    series = 0.5307027145 * t - 0.7265760135
    series = series * t + 0.7107068705
    series = series * t - 0.142248368
    series = series * t + 0.127414796
    tail = (series * t) * bell
    mass = jnp.where(value >= 0.0, 1.0 - tail, tail)
    return (value * mass, mass + value * (bell * (1.0 / math.sqrt(2.0 * math.pi))))


def fetch(first, own, other, target, sem):
    @pl.when(first)
    def _():
        pltpu.make_async_copy(own, target, sem).start()

    @pl.when(jnp.logical_not(first))
    def _():
        pltpu.make_async_copy(other, target, sem).start()


def landed(own, target, sem):
    pltpu.make_async_copy(own, target, sem).wait()


FAR = pl.BlockSpec(memory_space=pltpu.HBM)
ANYWHERE = pl.BlockSpec(memory_space=pl.ANY)
SCALARS = pl.BlockSpec(memory_space=pltpu.SMEM)
NEAR = pl.BlockSpec(memory_space=pltpu.VMEM)


def struct(shape, kind):
    return jax.ShapeDtypeStruct(tuple(shape), kind)


def near(shape, kind):
    return pltpu.VMEM(tuple(shape), kind)


def full(shape):
    return pl.BlockSpec(tuple(shape), lambda *_: (0,) * len(shape))


def far(*values):
    return tuple(pltpu.with_memory_space_constraint(value, pltpu.HBM) for value in values)


def stay(*values):
    return tuple(pltpu.with_memory_space_constraint(value, pltpu.VMEM) for value in values)


QUERY_B, VALUE_B, PROJ_B, ATTN_G, ATTN_B, INNER_B, OUTER_B, FFN_G, FFN_B = range(9)
TABLE_ROWS = (0, 1, 2, 3, 4, 5, 9, 10, 11)


def layer_vectors(mine, other, own):
    def pick(k, part=0):
        row = TABLE_ROWS[k] + part
        return jnp.where(own, mine[row : row + 1, :], other[row : row + 1, :])

    return pick


def qkv_kernel(info_ref, x_ref, w_ref, *refs):
    vectors = refs[:9]
    qb_ref, vb_ref = vectors[QUERY_B], vectors[VALUE_B]
    own_ref, other_ref, table_ref = refs[9:]
    step = pl.program_id(0)
    half = pl.num_programs(0) // 2
    width = x_ref.shape[2]
    x = x_ref[0]

    def put(ref):
        for k, shift in enumerate((qb_ref[...], None, vb_ref[...])):
            made = nn(x, w_ref[:, k * width : (k + 1) * width])
            ref[:, k * width : (k + 1) * width] = (made if shift is None else made + shift).astype(BF)
        ref[:, 3 * width :] = x

    pl.when(step < half)(lambda: put(other_ref))
    pl.when(step >= half)(lambda: put(own_ref))

    @pl.when(step == 0)
    def _():
        for ref, row in zip(vectors, TABLE_ROWS):
            for part in range(ref.shape[1] // width):
                table_ref[row + part : row + part + 1, :] = ref[:, part * width : (part + 1) * width]


def qkv_call(info, inputs, weight, vectors, rows=256):
    count, length, width = inputs.shape
    wide = weight.shape[1] + width
    half = length // rows
    return pl.pallas_call(
        qkv_kernel,
        grid_spec=pltpu.PrefetchScalarGridSpec(
            num_scalar_prefetch=1,
            grid=(2 * half,),
            in_specs=[
                pl.BlockSpec(
                    (1, rows, width),
                    lambda i, info: (jnp.where(i < half, 1 - info[0], info[0]), lax.rem(i, half), 0),
                ),
                pl.BlockSpec(weight.shape, lambda i, info: (0, 0), pipeline_mode=pl.Buffered(1)),
            ]
            + [full(v.shape) for v in vectors],
            out_specs=[
                pl.BlockSpec((rows, wide), lambda i, info: (jnp.maximum(i - half, 0), 0)),
                pl.BlockSpec((rows, wide), lambda i, info: (jnp.minimum(i, half - 1), 0)),
                full((ROW_TILE, width)),
            ],
        ),
        out_shape=[struct((length, wide), BF)] * 2 + [struct((ROW_TILE, width), F32)],
        compiler_params=params_of(50),
        cost_estimate=cost(6),
        name="qkv",
    )(info, *far(inputs, weight, *vectors))


def by_head(value, rows):
    width = value.shape[1]
    lane = lax.broadcasted_iota(jnp.int32, (rows, width), 1)
    row = lax.broadcasted_iota(jnp.int32, (rows, width), 0)
    return jnp.where((lane >= row * HEAD_DIM) & (lane < (row + 1) * HEAD_DIM), value, jnp.zeros((), value.dtype))


def heads_of(value):
    rows, width = value.shape
    lane = lax.broadcasted_iota(jnp.int32, (rows, width), 1)
    row = lax.broadcasted_iota(jnp.int32, (rows, width), 0)
    kept = jnp.where((lane >= row * HEAD_DIM) & (lane < (row + 1) * HEAD_DIM), value, 0.0)
    return jnp.sum(kept, axis=0, keepdims=True)


def two_rows(first, second):
    rows = lax.broadcasted_iota(jnp.int32, (ROW_TILE, first.shape[1]), 0)
    zero = jnp.zeros((), first.dtype)
    return jnp.where(rows == 0, first, jnp.where(rows == 1, second, zero))


def kept_places(width, ff, length):
    sizes = (("n1", width), ("n2", width), ("context", width), ("acts", ff), ("slope", ff), ("probs", 2 * length))
    places, start = {}, 0
    for name, size in sizes + (("r1", PAIR), ("r2", PAIR)):
        places[name] = (start, size)
        start += size
    return places


def head_kernel(
    info_ref, own_ref, other_ref, wp_ref, wi_ref, wo_ref, table,
    e_ref, kept_ref, acts, wp, wi, wo, sems,
):
    copies = [
        pltpu.make_async_copy(wp_ref, wp, sems.at[0]),
        pltpu.make_async_copy(wi_ref, wi, sems.at[1]),
        pltpu.make_async_copy(wo_ref, wo, sems.at[2]),
    ]
    for copy in copies:
        copy.start()
    pick = layer_vectors(table, table, info_ref[0] == 0)
    width, ff = wi.shape
    length = own_ref.shape[0]
    places = kept_places(width, ff, length)

    def put(name, value, offset=0):
        start = places[name][0] + offset
        kept_ref[:, start : start + value.shape[1]] = value.astype(F32)

    lane = lax.broadcasted_iota(jnp.int32, (ROW_TILE, length), 1)
    contexts = []
    for i, ref in enumerate((own_ref, other_ref)):
        query = by_head(ref[0:1, 0:width] * jnp.asarray(0.125, BF), ROW_TILE)
        scores = nt(query, ref[:, width : 2 * width])
        scores = jnp.where(lane < info_ref[1 + i], scores, BIG_NEG)
        raised = jnp.exp(scores - jnp.max(scores, axis=-1, keepdims=True))
        probs = raised / jnp.sum(raised, axis=-1, keepdims=True)
        put("probs", probs, i * length)
        contexts.append(heads_of(nn(probs.astype(BF), ref[:, 2 * width : 3 * width])))
    context = two_rows(*contexts).astype(BF)
    put("context", context)
    inputs = two_rows(own_ref[0:1, 3 * width :], other_ref[0:1, 3 * width :])
    copies[0].wait()
    n1, r1 = row_norm(inputs.astype(F32) + (nn(context, wp[...]) + pick(PROJ_B)))
    put("n1", n1)
    put("r1", r1)
    normed = n1 * pick(ATTN_G) + pick(ATTN_B)
    copies[1].wait()
    low = normed.astype(BF)
    for c in range(ff // width):
        cols = slice(c * width, (c + 1) * width)
        act, slope = gelu_pair(nn(low, wi[:, cols]) + pick(INNER_B, c))
        act = act.astype(BF)
        acts[:, cols] = act
        put("acts", act, c * width)
        put("slope", slope, c * width)
    copies[2].wait()
    n2, r2 = row_norm(normed + (nn(acts[...], wo[...]) + pick(OUTER_B)))
    put("n2", n2)
    put("r2", r2)
    e_ref[...] = (n2 * pick(FFN_G) + pick(FFN_B)).astype(BF)


def head_call(info, own, other, wp, wi, wo, table):
    length = own.shape[0]
    width, ff = wi.shape
    kept = max(place + size for place, size in kept_places(width, ff, length).values())
    shapes = [struct((ROW_TILE, width), BF), struct((ROW_TILE, kept), F32)]
    return pl.pallas_call(
        head_kernel,
        in_specs=[SCALARS, NEAR, NEAR, FAR, FAR, FAR, NEAR],
        out_specs=[NEAR] * len(shapes),
        out_shape=shapes,
        scratch_shapes=[pltpu.VMEM((ROW_TILE, ff), BF)]
        + [pltpu.VMEM(w.shape, BF) for w in (wp, wi, wo)]
        + [pltpu.SemaphoreType.DMA((3,))],
        compiler_params=params_of(22),
        cost_estimate=cost(7),
        name="head_rows",
    )(info, own, other, *far(wp, wi, wo), table)


def replace_first(xq, fixed):
    top_rows = xq[0:ROW_TILE, :]
    at_first = lax.broadcasted_iota(jnp.int32, top_rows.shape, 0) == 0
    xq[0:ROW_TILE, :] = jnp.where(at_first, fixed, top_rows)


def attention_parts(xq, j, width, lane, bias_col):
    base = pl.multiple_of(j * PAIR, PAIR)
    q = xq[:, pl.ds(base, PAIR)] * jnp.asarray(0.125, BF)
    k = xq[:, pl.ds(base + width, PAIR)]
    v = xq[:, pl.ds(base + 2 * width, PAIR)]
    zero = jnp.zeros_like(k)
    parts = []
    for h in range(2):
        mine = (lane >= HEAD_DIM * h) & (lane < HEAD_DIM * (h + 1))
        spare = lane == HEAD_DIM * (1 - h)
        qh = jnp.where(mine, q, jnp.where(spare, jnp.ones_like(q), zero))
        kh = jnp.where(mine, k, jnp.where(spare, bias_col, zero))
        parts.append((mine, qh, kh))
    return base, q, k, v, parts


def place_rows(ref, value, order):
    pieces, rows = ref.shape[0], ref.shape[1]
    for p in range(pieces):
        ref[jnp.bitwise_xor(p, order)] = value[p * rows : (p + 1) * rows, :]


def attend(xq, ctx, lse_scr, width, lane, bias_col):
    def pair_body(j, carry):
        base, q, k, v, parts = attention_parts(xq, j, width, lane, bias_col)
        sides = []
        for h, (mine, qh, kh) in enumerate(parts):
            vh = jnp.where(mine, v, jnp.ones_like(v))
            scores = nt(qh, kh)
            top = jnp.max(scores, axis=-1, keepdims=True)
            made = nn(jnp.exp(scores - top).astype(BF), vh)
            mass = made[:, HEAD_DIM * (1 - h) : HEAD_DIM * (1 - h) + 1]
            sides.append(made * (1.0 / mass))
            if lse_scr is not None:
                lse_scr[...] = jnp.where(lane == 2 * j + h, top + jnp.log(mass), lse_scr[...])
        ctx[:, pl.ds(base, PAIR)] = jnp.where(lane < HEAD_DIM, sides[0], sides[1]).astype(BF)
        return carry

    lax.fori_loop(0, HEADS // 2, pair_body, 0)


def mixing_kernel(info_ref, xq_a, xq_b, wp_a, wp_b, mine, table, normed_ref, xq, wp, ctx, sems):
    own = info_ref[0] == 0
    fetch(own, xq_a, xq_b, xq, sems.at[0])
    fetch(own, wp_a, wp_b, wp, sems.at[1])
    width = wp.shape[0]
    length = xq.shape[0]
    pick = layer_vectors(mine, table, own)
    lane = lax.broadcasted_iota(jnp.int32, (length, PAIR), 1)
    row = lax.broadcasted_iota(jnp.int32, (length, PAIR), 0)
    bias_col = jnp.where(row < info_ref[1], 0.0, BIG_NEG).astype(BF)
    landed(xq_a, xq, sems.at[0])
    attend(xq, ctx, None, width, lane, bias_col)
    landed(wp_a, wp, sems.at[1])
    n1, r1 = row_norm(xq[:, 3 * width :].astype(F32) + (nn(ctx[...], wp[...]) + pick(PROJ_B)))
    normed_ref[...] = n1 * pick(ATTN_G) + pick(ATTN_B)


def mixing_call(info, xq, wp, tables):
    length = xq[0].shape[0]
    width = wp[0].shape[0]
    return pl.pallas_call(
        mixing_kernel,
        in_specs=[SCALARS] + [FAR] * 4 + [NEAR] * 2,
        out_specs=NEAR,
        out_shape=struct((length, width), F32),
        scratch_shapes=[
            pltpu.VMEM(xq[0].shape, BF),
            pltpu.VMEM(wp[0].shape, BF),
            pltpu.VMEM((length, width), BF),
            pltpu.SemaphoreType.DMA((2,)),
        ],
        compiler_params=params_of(16),
        cost_estimate=cost(10),
        name="mixing",
    )(info, *far(*xq, *wp), *tables)


def train_kernel(
    info_ref, xq_a, xq_b, wq_a, wq_b, wp_a, wp_b, wi_a, wi_b, wo_a, wo_b, mine, table, head_ref, arrived_ref, cot_ref,
    z_ref, wp, wi, wo, ctx, lse_ref, fixed_ref, n1_ref, r1_ref, slope_ref, gf_ref, sg_ref, small_ref, keep_ref, send_ref,
    xq, lse_scr, sems,
):
    section = info_ref[0]
    own = section == 1
    fetch(own, xq_a, xq_b, xq, sems.at[0])
    width = wp.shape[0]
    length = xq.shape[0]
    ff = wi.shape[1]
    thirds = [(pl.ds(k * width, width), wo.at[pl.ds(k * width, width)]) for k in range(3)]
    for k, (cols, place) in enumerate(thirds):
        fetch(own, wq_a.at[:, cols], wq_b.at[:, cols], place, sems.at[5 + k])
    fetch(own, wp_a, wp_b, wp, sems.at[2])
    pick = layer_vectors(mine, table, own)
    lane = lax.broadcasted_iota(jnp.int32, (length, PAIR), 1)
    row = lax.broadcasted_iota(jnp.int32, (length, PAIR), 0)
    bias_col = jnp.where(row < info_ref[1], 0.0, BIG_NEG).astype(BF)
    many = jnp.broadcast_to(jnp.where(section == 0, head_ref[0:1, :], arrived_ref[1:2, :]), (ROW_TILE, width))
    fixed = []
    for k, shift in enumerate((pick(QUERY_B), None, pick(VALUE_B))):
        cols, place = thirds[k]
        landed(wq_a.at[:, cols], place, sems.at[5 + k])
        made = nn(many, place[...])
        fixed.append((made if shift is None else made + shift).astype(BF))
    fixed = jnp.concatenate(fixed + [many], axis=1)
    fixed_ref[...] = fixed
    landed(xq_a, xq, sems.at[0])
    fetch(own, wi_a, wi_b, wi, sems.at[3])
    fetch(own, wo_a, wo_b, wo, sems.at[4])
    copy = pltpu.make_async_copy(cot_ref.at[section], gf_ref, sems.at[1])
    copy.start()
    replace_first(xq, fixed)
    attend(xq, ctx, lse_scr, width, lane, bias_col)
    lse_ref[...] = jnp.transpose(lse_scr[...])[0:ROW_TILE, :]
    landed(wp_a, wp, sems.at[2])
    n1, r1 = row_norm(xq[:, 3 * width :].astype(F32) + (nn(ctx[...], wp[...]) + pick(PROJ_B)))
    n1_ref[...] = n1
    r1_ref[...] = r1
    normed = n1 * pick(ATTN_G) + pick(ATTN_B)
    low = normed.astype(BF)
    landed(wi_a, wi, sems.at[3])
    landed(wo_a, wo, sems.at[4])
    total = None
    for c in range(ff // CHUNK):
        cols = slice(c * CHUNK, (c + 1) * CHUNK)
        act, slope = gelu_pair(nn(low, wi[:, cols]) + pick(INNER_B, c))
        act = act.astype(BF)
        xq[:, cols] = act
        slope_ref[:, cols] = slope.astype(BF)
        term = nn(act, wo[cols, :])
        total = term if total is None else total + term
    n2, r2 = row_norm(normed + (total + pick(OUTER_B)))
    gain = pick(FFN_G)
    z_ref[...] = (n2 * gain + pick(FFN_B)).astype(BF)
    wide_row = lax.broadcasted_iota(jnp.int32, n2.shape, 0)
    copy.wait()
    grad = jnp.where(wide_row < info_ref[1], gf_ref[...].astype(F32), 0.0)
    second = norm_back(grad, n2, r2, gain)
    sg_ref[...] = second
    gf = second.astype(BF)
    gf_ref[...] = gf
    small_ref[0:1, :] = col_sum(gf)
    small_ref[1:2, :] = col_sum(grad * n2)
    small_ref[2:3, :] = col_sum(grad)
    half_chunks = ff // CHUNK // 2
    rows = send_ref.shape[1]
    each = CHUNK // rows
    for ref, half, order in ((send_ref, 1 - section, info_ref[4]), (keep_ref, section, info_ref[3])):
        for c in range(half_chunks):
            cols = pl.ds(pl.multiple_of((half * half_chunks + c) * CHUNK, CHUNK), CHUNK)
            made = tn(xq[:, cols], gf).astype(BF)
            for p in range(each):
                ref[jnp.bitwise_xor(c * each + p, order)] = made[p * rows : (p + 1) * rows, :]


def train_call(info, pairs, tables, head, arrived, cot):
    xq, wq, wp, wi, wo = (piece[0] for piece in pairs)
    length = xq.shape[0]
    width, ff = wi.shape
    args = [info]
    in_specs = [SCALARS]
    for pair in pairs:
        args += far(*pair)
        in_specs += [FAR, FAR]
    args += [*tables, head, arrived, *far(cot)]
    shapes = [
        struct((length, width), BF),
        near(wp.shape, BF),
        near(wi.shape, BF),
        near(wo.shape, BF),
        near((length, width), BF),
        near((ROW_TILE, length), F32),
        near((ROW_TILE, 4 * width), BF),
        near((length, width), F32),
        near((length, 1), F32),
        near((length, ff), BF),
        near((length, width), BF),
        near((length, width), F32),
        near((8, width), F32),
        near((GROUP, ff // 2 // GROUP, width), BF),
        near((GROUP, ff // 2 // GROUP, width), BF),
    ]
    return pl.pallas_call(
        train_kernel,
        in_specs=in_specs + [NEAR] * 4 + [FAR],
        out_specs=[NEAR] * len(shapes),
        out_shape=shapes,
        scratch_shapes=[
            pltpu.VMEM(xq.shape, BF),
            pltpu.VMEM((length, PAIR), F32),
            pltpu.SemaphoreType.DMA((8,)),
        ],
        compiler_params=params_of(14),
        cost_estimate=cost(26),
        name="layer_train",
    )(*args)


def feed_kernel(info_ref, normed_ref, wi_a, wi_b, wo_a, wo_b, mine, other, z_ref, wi, wo, sems):
    own = info_ref[0] == 0
    fetch(own, wi_a, wi_b, wi, sems.at[0])
    fetch(own, wo_a, wo_b, wo, sems.at[1])
    pick = layer_vectors(mine, other, own)
    normed = normed_ref[...]
    low = normed.astype(BF)
    landed(wi_a, wi, sems.at[0])
    landed(wo_a, wo, sems.at[1])
    total = None
    for c in range(wi.shape[1] // CHUNK):
        cols = slice(c * CHUNK, (c + 1) * CHUNK)
        act, slope = gelu_pair(nn(low, wi[:, cols]) + pick(INNER_B, c))
        term = nn(act.astype(BF), wo[cols, :])
        total = term if total is None else total + term
    n2, r2 = row_norm(normed + (total + pick(OUTER_B)))
    z_ref[...] = (n2 * pick(FFN_G) + pick(FFN_B)).astype(BF)


def feed_call(info, normed, wi, wo, tables):
    return pl.pallas_call(
        feed_kernel,
        in_specs=[SCALARS, NEAR] + [FAR] * 4 + [NEAR] * 2,
        out_specs=NEAR,
        out_shape=struct(normed.shape, BF),
        scratch_shapes=[pltpu.VMEM(wi[0].shape, BF), pltpu.VMEM(wo[0].shape, BF), pltpu.SemaphoreType.DMA((2,))],
        compiler_params=params_of(24),
        cost_estimate=cost(11),
        name="layer_feed",
    )(info, normed, *far(*wi, *wo), *tables)


def inner_kernel(
    info_ref, gf_ref, slope_ref, sg_ref, n1_ref, r1_ref, wi_ref, wo_ref, wp_ref, mine, table,
    keep_ref, send_ref, gh_ref, ga_ref, gc_ref, small_ref,
):
    section = info_ref[0]
    pick = layer_vectors(mine, table, section == 1)
    gain = pick(ATTN_G)
    low = jnp.transpose(n1_ref[...] * gain + pick(ATTN_B)).astype(BF)
    ff = wi_ref.shape[1]
    half_chunks = ff // CHUNK // 2
    gf = gf_ref[...]
    gn = sg_ref[...]
    for ref, half, order in ((send_ref, 1 - section, info_ref[6]), (keep_ref, section, info_ref[5])):
        for c in range(half_chunks):
            block = half * half_chunks + c
            cols = pl.ds(pl.multiple_of(block * CHUNK, CHUNK), CHUNK)
            gu = (nt(gf, wo_ref[cols, :]) * slope_ref[:, cols].astype(F32)).astype(BF)
            small_ref[pl.ds(3 + block, 1), :] = col_sum(gu)
            place_rows(ref.at[:, :, c * CHUNK : (c + 1) * CHUNK], nn(low, gu).astype(BF), order)
            gn = gn + nt(gu, wi_ref[:, cols])
    n1 = n1_ref[...]
    gh = norm_back(gn, n1, r1_ref[...], gain)
    gh_ref[...] = gh
    ga = gh.astype(BF)
    ga_ref[...] = ga
    gc_ref[...] = nt(ga, wp_ref[...]).astype(BF)
    small_ref[0:1, :] = col_sum(ga)
    small_ref[1:2, :] = col_sum(gn * n1)
    small_ref[2:3, :] = col_sum(gn)


def inner_call(info, gf, slope, sg, n1, r1, wi, wo, wp, tables):
    tokens, width = gf.shape
    ff = wi.shape[1]
    shapes = [
        near((GROUP, width // GROUP, ff // 2), BF),
        near((GROUP, width // GROUP, ff // 2), BF),
        near((tokens, width), F32),
        near((tokens, width), BF),
        near((tokens, width), BF),
        near((8, width), F32),
    ]
    return pl.pallas_call(
        inner_kernel,
        in_specs=[SCALARS] + [NEAR] * 10,
        out_specs=[NEAR] * len(shapes),
        out_shape=shapes,
        compiler_params=params_of(12),
        cost_estimate=cost(10),
        name="inner_grad",
    )(info, *stay(gf, slope, sg, n1, r1, wi, wo, wp), *tables)


def attention_kernel(
    info_ref, xq_a, xq_b, fixed_ref, gc_ref, ga_ref, c_ref, lse_ref, keep_ref, send_ref, g_ref, small_ref,
    xq, xt_scr, ct_scr, mean_scr, sem,
):
    section = info_ref[0]
    fetch(section == 1, xq_a, xq_b, xq, sem)
    length, width = gc_ref.shape
    row = lax.broadcasted_iota(jnp.int32, (length, PAIR), 0)
    lane = lax.broadcasted_iota(jnp.int32, (length, PAIR), 1)
    bias_col = jnp.where(row < info_ref[1], 0.0, BIG_NEG).astype(BF)
    ct_scr[...] = turned(c_ref[...])
    product = gc_ref[...].astype(F32) * c_ref[...].astype(F32)
    high = product.astype(BF)
    low = (product - high.astype(F32)).astype(BF)
    ones = by_head(jnp.ones((1, width), BF), ROW_TILE)
    mean_scr[...] = nt(ones, high) + nt(ones, low)
    landed(xq_a, xq, sem)
    replace_first(xq, fixed_ref[...])
    xt_scr[...] = turned(xq[:, 3 * width :])

    def pair_body(j, carry):
        base, q, k, v, parts = attention_parts(xq, j, width, lane, bias_col)
        kt = turned(k)
        gc = gc_ref[:, pl.ds(base, PAIR)]
        zero = jnp.zeros_like(gc)
        strips = [slice(s * STRIP, (s + 1) * STRIP) for s in range(length // STRIP)]
        gk = [None] * len(strips)
        gv = [None] * len(strips)
        gqt = []
        for h, (mine, qh, kh) in enumerate(parts):
            gch = jnp.where(mine, gc, zero)
            qz = jnp.where(mine, q, zero)
            lse = lse_ref[pl.ds(2 * j + h, 1), :]
            mean = mean_scr[pl.ds(2 * j + h, 1), :]
            gq_h = None
            for s, rows in enumerate(strips):
                probs = jnp.exp(nt(kh[rows, :], qh) - lse)
                gs = (probs * (nt(v[rows, :], gch) - mean)).astype(BF)
                gv_h = nn(probs.astype(BF), gch)
                gk_h = nn(gs, qz)
                term = nn(kt[HEAD_DIM * h : HEAD_DIM * (h + 1), rows], gs)
                gq_h = term if gq_h is None else gq_h + term
                gk[s] = gk_h if h == 0 else gk[s] + gk_h
                gv[s] = gv_h if h == 0 else gv[s] + gv_h
            gqt.append(gq_h)
        gq = jnp.transpose(jnp.concatenate(gqt, axis=0)) * 0.125
        g_ref[:, pl.ds(base, PAIR)] = gq.astype(BF)
        for s, rows in enumerate(strips):
            g_ref[rows, pl.ds(base + width, PAIR)] = gk[s].astype(BF)
            g_ref[rows, pl.ds(base + 2 * width, PAIR)] = gv[s].astype(BF)
        return carry

    lax.fori_loop(0, HEADS // 2, pair_body, 0)
    small_ref[0:1, :] = col_sum(g_ref[:, 0:width])
    small_ref[1:2, :] = col_sum(g_ref[:, 2 * width : 3 * width])
    wide = 3 * width // 2
    for ref, half, order in ((send_ref, 1 - section, info_ref[8]), (keep_ref, section, info_ref[7])):
        cols = pl.ds(pl.multiple_of(half * wide, PAIR), wide)
        place_rows(ref.at[:, :, 0:wide], nn(xt_scr[...], g_ref[:, cols]).astype(BF), order)
        cols = pl.ds(pl.multiple_of(half * (width // 2), PAIR), width // 2)
        place_rows(ref.at[:, :, wide:], nn(ct_scr[...], ga_ref[:, cols]).astype(BF), order)


def attention_call(info, xq, fixed, gc, ga, context, lse):
    length, width = gc.shape
    shapes = [
        near((GROUP, width // GROUP, 2 * width), BF),
        near((GROUP, width // GROUP, 2 * width), BF),
        near((length, 3 * width), BF),
        near((8, width), F32),
    ]
    return pl.pallas_call(
        attention_kernel,
        in_specs=[SCALARS, FAR, FAR] + [NEAR] * 5,
        out_specs=[NEAR] * len(shapes),
        out_shape=shapes,
        scratch_shapes=[
            pltpu.VMEM(xq[0].shape, BF),
            pltpu.VMEM((width, length), BF),
            pltpu.VMEM((width, length), BF),
            pltpu.VMEM((ROW_TILE, length), F32),
            pltpu.SemaphoreType.DMA(()),
        ],
        compiler_params=params_of(18),
        cost_estimate=cost(14),
        name="attention_grad",
    )(info, *far(*xq), *stay(fixed, gc, ga, context, lse))


def input_kernel(info_ref, w_a, w_b, g_ref, gh_ref, small1_ref, small2_ref, small3_ref, o_ref, small_ref, w, sem):
    fetch(info_ref[0] == 1, w_a, w_b, w, sem)
    landed(w_a, w, sem)
    made = gh_ref[...] + nt(g_ref[...], w[...])
    o_ref[...] = made
    small_ref[0:2, :] = small3_ref[0:2, :]
    small_ref[2:9, :] = small2_ref[0:7, :]
    small_ref[9:12, :] = small1_ref[0:3, :]
    small_ref[12:16, :] = made[0:4, :]


def input_call(info, g, gh, w, small1, small2, small3):
    return pl.pallas_call(
        input_kernel,
        in_specs=[SCALARS, FAR, FAR] + [NEAR] * 5,
        out_specs=[NEAR] * 2,
        out_shape=[struct(gh.shape, F32), struct((ROW_TILE, gh.shape[1]), F32)],
        scratch_shapes=[pltpu.VMEM(w[0].shape, BF), pltpu.SemaphoreType.DMA(())],
        compiler_params=params_of(12),
        cost_estimate=cost(4),
        name="input_grad",
    )(info, *far(*w), *stay(g, gh, small1, small2, small3))


def head_back_kernel(
    info_ref, small_a, small_b, kept_ref, own_ref, other_ref,
    wq_ref, wp_ref, wi_ref, wo_ref, table, x_ref, pay_ref, later_ref, sums_ref, wq, wp, wi, wo, sems,
):
    copies = [
        pltpu.make_async_copy(ref, scr, sems.at[i])
        for i, (ref, scr) in enumerate(((wo_ref, wo), (wi_ref, wi), (wp_ref, wp), (wq_ref, wq)))
    ]
    for copy in copies:
        copy.start()
    width = wp.shape[0]
    length = own_ref.shape[0]
    ff = wi.shape[1]
    places = kept_places(width, ff, length)

    def kept(name, offset=0, size=None):
        start = places[name][0] + offset
        return kept_ref[:, start : start + (places[name][1] if size is None else size)]

    n1, n2 = kept("n1"), kept("n2")
    context = kept("context").astype(BF)
    pick = layer_vectors(table, table, info_ref[0] == 0)
    grad = two_rows(small_a[12:13, :], small_b[12:13, :]).astype(BF).astype(F32)
    second = norm_back(grad, n2, kept("r2", 0, 1), pick(FFN_G))
    gf = second.astype(BF)
    copies[0].wait()
    gu = (nt(gf, wo[...]) * kept("slope")).astype(BF)
    copies[1].wait()
    gn = second + nt(gu, wi[...])
    gh = norm_back(gn, n1, kept("r1", 0, 1), pick(ATTN_G))
    ga = gh.astype(BF)
    copies[2].wait()
    gc = nt(ga, wp[...]).astype(BF)
    normed = (n1 * pick(ATTN_G) + pick(ATTN_B)).astype(BF)
    copies[3].wait()
    query_bias = value_bias = jnp.zeros((1, width), F32)
    vectors = {}
    sums_of = []
    for i, ref in enumerate((own_ref, other_ref)):
        mid = (1 - 2 * i) * info_ref[0] + i
        keys, values, inputs = ref[:, width : 2 * width], ref[:, 2 * width : 3 * width], ref[:, 3 * width :]
        query = ref[0:1, 0:width] * jnp.asarray(0.125, BF)
        gc_row = gc[i : i + 1, :]
        query_heads, gc_heads = by_head(query, ROW_TILE), by_head(gc_row, ROW_TILE)
        probs = kept("probs", i * length, length)
        gp = nt(gc_heads, values)
        gs = (probs * (gp - jnp.sum(probs * gp, axis=-1, keepdims=True))).astype(BF)
        low = probs.astype(BF)
        gq = (heads_of(nn(gs, keys)) * 0.125).astype(BF)
        sums_of += [(KEY_SUMS + HEADS * i, nn(gs, inputs)), (VALUE_SUMS + HEADS * i, nn(low, inputs))]
        key_back = nt(query_heads, wq[:, width : 2 * width]).astype(BF)
        value_back = nt(gc_heads, wq[:, 2 * width :]).astype(BF)
        gx = tn(gs, key_back) + tn(low, value_back)
        top = gh[i : i + 1, :] + nt(jnp.broadcast_to(gq, (ROW_TILE, width)), wq[:, 0:width])[0:1, :]
        at_first = lax.broadcasted_iota(jnp.int32, gx.shape, 0) == 0
        x_ref[mid] = gx + jnp.where(at_first, top, 0.0)
        query_bias = query_bias + gq.astype(F32)
        mass = jnp.sum(low.astype(F32), axis=-1, keepdims=True)
        value_bias = value_bias + heads_of(gc_heads.astype(F32) * mass)
        for key, piece in (
            (V_OUTER, gf[i : i + 1, :]),
            (V_NORMED, normed[i : i + 1, :]),
            (V_CONTEXT, context[i : i + 1, :]),
            (V_PROJ, ga[i : i + 1, :]),
            (V_INPUT, ref[0:1, 3 * width :]),
            (V_GQUERY, gq),
            (V_QUERY, query),
            (V_GCONTEXT, gc_row),
        ):
            vectors[2 * key + i] = piece
    gu_sum = col_sum(gu)
    act = kept("acts").astype(BF)
    own_small = [query_bias, value_bias, col_sum(ga), col_sum(gn * n1), col_sum(gn)]
    own_small += [gu_sum[:, width * k : width * (k + 1)] for k in range(ff // width)]
    own_small += [col_sum(gf), col_sum(grad * n2), col_sum(grad)]

    def stack(pieces):
        row = lax.broadcasted_iota(jnp.int32, (ROW_TILE, width), 0)
        made = jnp.zeros((ROW_TILE, width), F32)
        for k, piece in enumerate(pieces):
            made = jnp.where(row == k, piece.astype(F32), made)
        return made

    wide = [value[i : i + 1, width * k : width * (k + 1)] for value in (act, gu) for i in range(2) for k in range(ff // width)]
    rows = [value[h : h + 1, :] for place, value in sums_of for h in range(HEADS)]
    rows = rows[0:HEADS] + rows[2 * HEADS : 3 * HEADS] + rows[HEADS : 2 * HEADS] + rows[3 * HEADS :]
    rows += [vectors[k] for k in range(16)] + wide
    half = FACTORS // 2
    for ref, start in ((pay_ref, 0), (later_ref, half)):
        for k in range(0, half, 8):
            ref[k : k + 8, :] = stack(rows[start + k : start + k + 8])[0:8, :].astype(BF)
    sums_ref[...] = jnp.where(info_ref[0] == 0, stack(own_small), small_a[...] + small_b[...]).astype(BF)


def head_back_call(info, small_a, small_b, kept, own, other, wq, wp, wi, wo, table):
    length = own.shape[0]
    width, ff = wi.shape
    args = [small_a, small_b, kept, own, other]
    return pl.pallas_call(
        head_back_kernel,
        in_specs=[SCALARS] + [NEAR] * len(args) + [FAR] * 4 + [NEAR],
        out_specs=[NEAR] * 4,
        out_shape=[struct((2, length, width), F32)]
        + [struct((FACTORS // 2, width), BF)] * 2
        + [struct((ROW_TILE, width), BF)],
        scratch_shapes=[pltpu.VMEM(w.shape, BF) for w in (wq, wp, wi, wo)] + [pltpu.SemaphoreType.DMA((4,))],
        compiler_params=params_of(28),
        cost_estimate=cost(12),
        name="head_rows_grad",
    )(info, *args, *far(wq, wp, wi, wo), table)


def outer_final_kernel(info_ref, a_low, a_high, b_low, b_high, gt_ref, o_ref):
    step = pl.program_id(0)
    rows = a_low.shape[1]
    each = o_ref.shape[0] // rows
    per_half = pl.num_programs(0) // 2

    @pl.when(info_ref[0] == 1)
    def _():
        def fill(low, high, first, order):
            for p in range(each):
                piece = piece_at(low, high, jnp.bitwise_xor(first + p, order))
                o_ref[p * rows : (p + 1) * rows, :] = piece.astype(F32)

        pl.when(step < per_half)(lambda: fill(a_low, a_high, step * each, info_ref[4]))
        pl.when(step >= per_half)(lambda: fill(b_low, b_high, (step - per_half) * each, info_ref[3]))

    @pl.when(info_ref[0] == 0)
    def _():
        made = None
        for j in range(2):
            left = gt_ref[ACTS + 4 * j + step]
            term = tn(left, gt_ref[VECTORS + 2 * V_OUTER + j])
            made = term if made is None else made + term
        o_ref[...] = made


def outer_final_call(info, quarters, gt):
    width = quarters[0].shape[2]
    ff = 4 * quarters[0].shape[0] * quarters[0].shape[1]
    return pl.pallas_call(
        outer_final_kernel,
        grid=(ff // width,),
        in_specs=[SCALARS] + [full(a.shape) for a in quarters] + [full(gt.shape)],
        out_specs=pl.BlockSpec((width, width), lambda i: (i, 0)),
        out_shape=struct((ff, width), F32),
        compiler_params=params_of(32),
        cost_estimate=cost(5),
        name="outer_final",
    )(info, *quarters, gt)


def piece_at(low, high, place, cols=slice(None)):
    half = low.shape[0]
    inside = lax.rem(place, half)
    return jnp.where(place < half, low[inside, :, cols], high[inside, :, cols])


def unfold(halves, cols, order, target):
    low, high = halves
    rows = low.shape[1]
    for p in range(GROUP):
        target[p * rows : (p + 1) * rows, :] = piece_at(low, high, jnp.bitwise_xor(p, order), cols).astype(F32)


def inner_final_kernel(info_ref, a_low, a_high, b_low, b_high, gt_ref, o_ref):
    step = pl.program_id(0)
    width = o_ref.shape[1]

    @pl.when(info_ref[0] == 1)
    def _():
        for k in range(4):
            ref, order = (((a_low, a_high), info_ref[6]), ((b_low, b_high), info_ref[5]))[k // 2]
            cols = slice((k % 2) * width, (k % 2 + 1) * width)
            pl.when(step == k)(lambda ref=ref, order=order, cols=cols: unfold(ref, cols, order, o_ref))

    @pl.when(info_ref[0] == 0)
    def _():
        made = None
        for j in range(2):
            term = tn(gt_ref[VECTORS + 2 * V_NORMED + j], gt_ref[INNERS + 4 * j + step])
            made = term if made is None else made + term
        o_ref[...] = made


def inner_final_call(info, quarters, gt):
    width = gt.shape[2]
    ff = 2 * quarters[0].shape[2]
    return pl.pallas_call(
        inner_final_kernel,
        grid=(ff // width,),
        in_specs=[SCALARS] + [full(a.shape) for a in quarters] + [full(gt.shape)],
        out_specs=pl.BlockSpec((width, width), lambda i: (0, i)),
        out_shape=struct((width, ff), F32),
        compiler_params=params_of(32),
        cost_estimate=cost(5),
        name="inner_final",
    )(info, *quarters, gt)


def qkv_final_kernel(info_ref, a_low, a_high, b_low, b_high, gt_ref, o_ref, p_ref):
    width = p_ref.shape[0]
    wide = 3 * width // 2
    half = width // 2

    @pl.when(info_ref[0] == 1)
    def _():
        for ref, order, k in (((a_low, a_high), info_ref[8], 0), ((b_low, b_high), info_ref[7], 1)):
            unfold(ref, slice(0, wide), order, o_ref.at[:, k * wide : (k + 1) * wide])
            unfold(ref, slice(wide, wide + half), order, p_ref.at[:, k * half : (k + 1) * half])

    @pl.when(info_ref[0] == 0)
    def _():
        def pairs(left, right):
            return tn(gt_ref[VECTORS + 2 * left], gt_ref[VECTORS + 2 * right]) + tn(
                gt_ref[VECTORS + 2 * left + 1], gt_ref[VECTORS + 2 * right + 1]
            )

        p_ref[...] = pairs(V_CONTEXT, V_PROJ)
        o_ref[:, 0:width] = pairs(V_INPUT, V_GQUERY)
        chips = gt_ref.shape[1]
        lane = lax.broadcasted_iota(jnp.int32, (chips, width), 1)
        for place, base, key in ((1, KEY_SUMS, V_QUERY), (2, VALUE_SUMS, V_GCONTEXT)):
            made = None
            for j in range(2):
                left = gt_ref[base + HEADS * j : base + HEADS * j + HEADS].reshape(HEADS * chips, width)
                row = gt_ref[VECTORS + 2 * key + j]
                heads = [
                    jnp.where((lane >= HEAD_DIM * h) & (lane < HEAD_DIM * (h + 1)), row, jnp.zeros_like(row))
                    for h in range(HEADS)
                ]
                term = tn(left, jnp.concatenate(heads, axis=0))
                made = term if made is None else made + term
            o_ref[:, place * width : (place + 1) * width] = made


def qkv_final_call(info, quarters, gt):
    width = gt.shape[2]
    return pl.pallas_call(
        qkv_final_kernel,
        in_specs=[SCALARS] + [full(a.shape) for a in quarters] + [full(gt.shape)],
        out_specs=[full((width, 3 * width)), full((width, width))],
        out_shape=[struct((width, 3 * width), F32), struct((width, width), F32)],
        compiler_params=params_of(32),
        cost_estimate=cost(6),
        name="qkv_final",
    )(info, *quarters, gt)


def swap(value):
    return lax.ppermute(value, "section", SWAP)


def add_low(left, right):
    return (left.astype(F32) + right.astype(F32)).astype(BF)


def hop(value, stage, orders):
    chips = lax.axis_size("dp")
    pairs = [
        (section * chips + chip, section * chips + (chip ^ orders[section][stage]))
        for section in range(2)
        for chip in range(chips)
    ]
    return lax.ppermute(value, ("section", "dp"), pairs)


def after(value, *others):
    return lax.optimization_barrier((value,) + others)[0]


def beside(made, *sums):
    tied = lax.optimization_barrier(tuple(made) + tuple(one.coming for one in sums))
    for one, coming in zip(sums, tied[len(made) :]):
        one.coming = coming
    return tied[: len(made)]


class Sum:
    def __init__(self, keep, send, group):
        self.low, self.coming, self.orders = keep, swap(send), ORDERS[group]

    def add(self):
        half = self.coming.shape[0] // 2
        if half == 0:
            self.part = add_low(self.low, self.coming)
            return
        self.high = add_low(self.low[half:], self.coming[half:])
        self.low = self.part = add_low(self.low[:half], self.coming[:half])

    def halve(self, stage):
        self.coming = hop(self.high, stage, self.orders)

    def across(self):
        chips = lax.axis_size("dp")
        if chips > GROUP:
            groups = [[low + GROUP * high for high in range(chips // GROUP)] for low in range(GROUP)]
            self.part = lax.psum(self.part, "dp", axis_index_groups=groups)

    def double(self, stage):
        self.coming = hop(self.part, stage, self.orders)

    def join(self):
        self.part = jnp.concatenate([self.part, self.coming], axis=0)

    def quarters(self):
        return (swap(self.part), swap(self.coming), self.part, self.coming)


class Line:
    def __init__(self):
        self.token = None

    def __call__(self, value):
        return value if self.token is None else after(value, self.token)

    def run(self, work, *args):
        made = work(*args)
        tied = lax.optimization_barrier(tuple(made))
        self.token = tied[0]
        return tied

    def take(self, group):
        group.coming = self(group.coming)
        self.token = group.coming

    def halve(self, group, stage):
        self.take(group)
        group.add()
        group.halve(stage)
        self.token = group.part

    def double(self, group, stage):
        self.take(group)
        group.add()
        group.across()
        group.double(stage)
        self.token = group.part

    def join(self, group, stage):
        self.take(group)
        group.join()
        if stage is not None:
            group.double(stage)
        self.token = group.part


class Gather:
    ORDERS = ((8, 4, 2, 1), (4, 8, 1, 2))

    def __init__(self, value):
        self.part = value[None]

    def double(self, stage):
        self.coming = hop(self.part, stage, self.ORDERS)

    def join(self):
        self.part = lax.optimization_barrier(jnp.concatenate([self.part, self.coming], axis=0))

    def across(self):
        chips = lax.axis_size("dp")
        if chips > GROUP:
            groups = [[low + GROUP * high for high in range(chips // GROUP)] for low in range(GROUP)]
            every = lax.all_gather(self.part, "dp", axis_index_groups=groups)
            self.part = every.reshape((-1,) + self.part.shape[1:])


def order_of(chip, orders):
    place = jnp.int32(0)
    for stage in range(4):
        bit = (chip // orders[stage]) % 2
        place = place + bit * (8 >> stage)
    return place


def local(embeddings, cotangent, lengths, *weights):
    (wq, query_bias, value_bias, wp, proj_bias, attn_gain, attn_bias, wi, inner_bias, wo, outer_bias, ffn_gain, ffn_bias) = (
        piece[0] for piece in weights
    )
    section = lax.axis_index("section")
    chip = lax.axis_index("dp")
    first_section = section == 0
    inputs = embeddings[0]
    width = inputs.shape[2]
    scalars = [section, jnp.where(first_section, lengths[0], lengths[1]), jnp.where(first_section, lengths[1], lengths[0])]
    for orders in ORDERS:
        places = [order_of(chip, order) for order in orders]
        scalars += [jnp.where(first_section, places[0], places[1]), jnp.where(first_section, places[1], places[0])]
    info = jnp.stack(scalars).astype(jnp.int32)
    vectors = [weights[k] for k in (1, 2, 4, 5, 6, 8, 10, 11, 12)]
    own, other, own_table = qkv_call(info, inputs, wq, vectors)
    tables = (own_table, swap(own_table))
    wq_pair = (wq, swap(wq))
    wp_pair = (wp, swap(wp))
    xq_pair = (own, swap(other))
    wi_pair = (wi, swap(wi))
    wo_pair = (wo, swap(wo))
    head = head_call(info, own, other, wp, wi, wo, own_table)
    arrived = swap(head[0])
    pairs = (xq_pair, wq_pair, wp_pair, wi_pair, wo_pair)
    (z, wp_d, wi_d, wo_d, context, lse, fixed, n1, r1, slope, gf, sg, small1, outer_keep, outer_send) = train_call(
        info, pairs, tables, head[0], arrived, cotangent
    )
    g1 = Sum(outer_keep, outer_send, 0)

    made = inner_call(info, gf, slope, sg, n1, r1, wi_d, wo_d, wp_d, tables)
    inner_keep, inner_send, gh, ga, gc, small2 = beside(made, g1)
    g1.add()
    g1.halve(0)
    g2 = Sum(inner_keep, inner_send, 1)

    made = attention_call(info, xq_pair, fixed, after(gc, g1.part), ga, context, lse)
    qkv_keep, qkv_send, g_qkv, small3 = beside(made, g1, g2)
    g3 = Sum(qkv_keep, qkv_send, 2)
    line = Line()
    line.halve(g2, 0)
    line.halve(g1, 1)
    gx, dsmall = line.run(input_call, info, line(g_qkv), gh, wq_pair, small1, small2, small3)
    dsmall_other = swap(dsmall)
    line.halve(g3, 0)
    encoder_gx, factors_a, factors_b, own_sums = line.run(
        head_back_call, info, dsmall, line(dsmall_other), head[1], own, other, wq, wp, wi, wo, own_table
    )
    factors_b = swap(factors_b)
    gx_other = swap(gx)
    line.halve(g1, 2)
    line.halve(g2, 1)
    line.halve(g3, 1)
    factors = Gather(jnp.concatenate([jnp.where(first_section, factors_a, line(factors_b)), own_sums]))
    factors.double(0)
    line.token = factors.part
    line.halve(g1, 3)
    line.halve(g2, 2)
    line.join(factors, 1)
    line.halve(g3, 2)
    line.double(g1, 3)
    line.join(factors, 2)
    line.halve(g2, 3)
    line.halve(g3, 3)
    line.join(g1, 2)
    line.double(g2, 3)
    line.join(factors, 3)
    line.double(g3, 3)
    line.join(g2, 2)
    line.join(g1, 1)
    line.join(g3, 2)
    line.join(g2, 1)
    line.join(g1, 0)
    (normed,) = line.run(lambda *a: (mixing_call(*a),), info, xq_pair, wp_pair, (own_table, line(tables[1])))
    line.join(g3, 1)
    line.join(g2, 0)
    line.join(factors, None)
    factors.across()
    factors_half = factors.part[:, : FACTORS // 2]
    factors_more = swap(factors_half)
    line.take(g1)
    outer_quarters = g1.quarters()
    (e_low,) = line.run(lambda *a: (feed_call(*a),), info, line(normed), wi_pair, wo_pair, tables)
    z_other = swap(jnp.where(first_section, z, e_low))
    z_mine = jnp.where(first_section, e_low, z)
    line.join(g3, 0)
    decoder_gx = jnp.stack([line(gx_other), gx])
    later = jnp.arange(gx.shape[0])[None, :, None] > 0
    (embed_grads,) = line.run(lambda a: (jnp.where(first_section, encoder_gx, jnp.where(later, a, 0.0)),), decoder_gx)
    more = line(factors_more).reshape((-1, 2, 2, 2, 2) + factors_half.shape[1:])
    more = jnp.transpose(more, (0, 2, 1, 4, 3, 5, 6)).reshape(factors_half.shape)
    gt = jnp.transpose(jnp.concatenate([factors_half, more], axis=1), (1, 0, 2))
    sums = jnp.sum(factors.part[:, FACTORS // 2 :].astype(F32), axis=0)
    gt, sums = line.run(lambda *a: a, gt, sums)
    outputs = jnp.where(first_section, jnp.stack([z_mine, line(z_other)]), jnp.stack([z_other, z_mine]))
    (outputs,) = line.run(lambda a: (a,), outputs)
    (outer_grad,) = line.run(lambda *a: (outer_final_call(*a),), info, outer_quarters, line(gt))
    line.take(g2)
    inner_quarters = g2.quarters()
    line.take(g3)
    qkv_quarters = g3.quarters()
    (inner_grad,) = line.run(lambda *a: (inner_final_call(*a),), info, inner_quarters, line(gt))
    qkv_grad, proj_grad = qkv_final_call(info, qkv_quarters, line(gt))
    results = (
        outputs,
        embed_grads,
        qkv_grad,
        sums[0],
        sums[1],
        proj_grad,
        sums[2],
        sums[3],
        sums[4],
        inner_grad,
        sums[5:9].reshape(-1),
        outer_grad,
        sums[9],
        sums[10],
        sums[11],
    )
    return tuple(piece[None] for piece in results)


def solution(mesh):
    matrix = P("section", None, None)
    vector = P("section", None)
    return jax.shard_map(
        local,
        mesh=mesh,
        in_specs=(P("section", "dp", None, None), P("dp", None, None), P("dp"))
        + (matrix, vector, vector, matrix, vector, vector, vector)
        + (matrix, vector, matrix, vector, vector, vector),
        out_specs=(P("section", "dp", None, None), P("section", "dp", None, None))
        + (matrix, vector, vector, matrix, vector, vector, vector)
        + (matrix, vector, matrix, vector, vector, vector),
        check_vma=False,
    )
```

```python
import math

import jax
import jax.numpy as jnp
from jax import lax
from jax.experimental import pallas as pl
from jax.experimental.pallas import tpu as pltpu
from jax.sharding import PartitionSpec as P

HEADS = 12
HEAD_DIM = 64
PAIR = 2 * HEAD_DIM
EPSILON = 1e-06
BIG_NEG = -1e30
BF = jnp.bfloat16
F32 = jnp.float32
CHUNK = 768
STRIP = 512
GROUP = 16
ROW_TILE = 16
ORDERS = (
    ((2, 1, 8, 4), (1, 4, 2, 8)),
    ((8, 1, 2, 4), (2, 4, 8, 1)),
    ((1, 2, 4, 8), (2, 1, 8, 4)),
)
SWAP = ((0, 1), (1, 0))
KEY_SUMS, VALUE_SUMS, QUERIES, GCONTEXTS = 0, 24, 48, 50
OUTERS, NORMEDS, CONTEXTS, PROJS, INPUTS, GQUERIES, ACTS, INNERS = 0, 2, 4, 6, 8, 10, 12, 20
SUMS, FACTORS = 52, 64


def params_of(mebibytes):
    return pltpu.CompilerParams(vmem_limit_bytes=mebibytes * 1024 * 1024)


def cost(micros):
    return pl.CostEstimate(flops=int(micros * 0.11e9), bytes_accessed=int(micros * 0.2e6), transcendentals=0)


def nn(left, right):
    return lax.dot_general(left, right, (((1,), (0,)), ((), ())), preferred_element_type=F32)


def nt(left, right):
    return lax.dot_general(left, right, (((1,), (1,)), ((), ())), preferred_element_type=F32)


def tn(left, right):
    return lax.dot_general(left, right, (((0,), (0,)), ((), ())), preferred_element_type=F32)


def turned(value):
    return jnp.transpose(value.astype(F32)).astype(BF)


def col_sum(value):
    return jnp.sum(value.astype(F32), axis=0, keepdims=True)


def row_norm(hidden):
    centred = hidden - jnp.mean(hidden, axis=-1, keepdims=True)
    scale = lax.rsqrt(jnp.mean(centred * centred, axis=-1, keepdims=True) + EPSILON)
    return (centred * scale, scale)


def norm_back(grad, normal, scale, gain):
    scaled = grad * gain
    return scale * (
        scaled
        - jnp.mean(scaled, axis=-1, keepdims=True)
        - normal * jnp.mean(scaled * normal, axis=-1, keepdims=True)
    )


def gelu_pair(value):
    bell = jnp.exp(-0.5 * (value * value))
    t = 1.0 / (1.0 + (0.3275911 / math.sqrt(2.0)) * jnp.abs(value))
    series = 0.5307027145 * t - 0.7265760135
    series = series * t + 0.7107068705
    series = series * t - 0.142248368
    series = series * t + 0.127414796
    tail = (series * t) * bell
    mass = jnp.where(value >= 0.0, 1.0 - tail, tail)
    return (value * mass, mass + value * (bell * (1.0 / math.sqrt(2.0 * math.pi))))


def fetch(first, own, other, target, sem):
    @pl.when(first)
    def _():
        pltpu.make_async_copy(own, target, sem).start()

    @pl.when(jnp.logical_not(first))
    def _():
        pltpu.make_async_copy(other, target, sem).start()


def landed(own, target, sem):
    pltpu.make_async_copy(own, target, sem).wait()


FAR = pl.BlockSpec(memory_space=pltpu.HBM)
ANYWHERE = pl.BlockSpec(memory_space=pl.ANY)
SCALARS = pl.BlockSpec(memory_space=pltpu.SMEM)
NEAR = pl.BlockSpec(memory_space=pltpu.VMEM)


def struct(shape, kind):
    return jax.ShapeDtypeStruct(tuple(shape), kind)


def near(shape, kind):
    return pltpu.VMEM(tuple(shape), kind)


def full(shape):
    return pl.BlockSpec(tuple(shape), lambda *_: (0,) * len(shape))


def far(*values):
    return tuple(pltpu.with_memory_space_constraint(value, pltpu.HBM) for value in values)


def stay(*values):
    return tuple(pltpu.with_memory_space_constraint(value, pltpu.VMEM) for value in values)


QUERY_B, VALUE_B, PROJ_B, ATTN_G, ATTN_B, INNER_B, OUTER_B, FFN_G, FFN_B = range(9)
TABLE_ROWS = (0, 1, 2, 3, 4, 5, 9, 10, 11)


def layer_vectors(mine, other, own):
    def pick(k, part=0):
        row = TABLE_ROWS[k] + part
        return jnp.where(own, mine[row : row + 1, :], other[row : row + 1, :])

    return pick


def qkv_kernel(info_ref, x_ref, w_ref, *refs):
    vectors = refs[:9]
    qb_ref, vb_ref = vectors[QUERY_B], vectors[VALUE_B]
    own_ref, other_ref, table_ref = refs[9:]
    step = pl.program_id(0)
    half = pl.num_programs(0) // 2
    width = x_ref.shape[2]
    x = x_ref[0]

    def put(ref):
        for k, shift in enumerate((qb_ref[...], None, vb_ref[...])):
            made = nn(x, w_ref[:, k * width : (k + 1) * width])
            ref[:, k * width : (k + 1) * width] = (made if shift is None else made + shift).astype(BF)
        ref[:, 3 * width :] = x

    pl.when(step < half)(lambda: put(other_ref))
    pl.when(step >= half)(lambda: put(own_ref))

    @pl.when(step == 0)
    def _():
        for ref, row in zip(vectors, TABLE_ROWS):
            for part in range(ref.shape[1] // width):
                table_ref[row + part : row + part + 1, :] = ref[:, part * width : (part + 1) * width]


def qkv_call(info, inputs, weight, vectors, rows=256):
    count, length, width = inputs.shape
    wide = weight.shape[1] + width
    half = length // rows
    return pl.pallas_call(
        qkv_kernel,
        grid_spec=pltpu.PrefetchScalarGridSpec(
            num_scalar_prefetch=1,
            grid=(2 * half,),
            in_specs=[
                pl.BlockSpec(
                    (1, rows, width),
                    lambda i, info: (jnp.where(i < half, 1 - info[0], info[0]), lax.rem(i, half), 0),
                ),
                pl.BlockSpec(weight.shape, lambda i, info: (0, 0), pipeline_mode=pl.Buffered(1)),
            ]
            + [full(v.shape) for v in vectors],
            out_specs=[
                pl.BlockSpec((rows, wide), lambda i, info: (jnp.maximum(i - half, 0), 0)),
                pl.BlockSpec((rows, wide), lambda i, info: (jnp.minimum(i, half - 1), 0)),
                full((ROW_TILE, width)),
            ],
        ),
        out_shape=[struct((length, wide), BF)] * 2 + [struct((ROW_TILE, width), F32)],
        compiler_params=params_of(20),
        cost_estimate=cost(6),
        name="qkv",
    )(info, *far(inputs, weight, *vectors))


def by_head(value, rows):
    width = value.shape[1]
    lane = lax.broadcasted_iota(jnp.int32, (rows, width), 1)
    row = lax.broadcasted_iota(jnp.int32, (rows, width), 0)
    return jnp.where((lane >= row * HEAD_DIM) & (lane < (row + 1) * HEAD_DIM), value, jnp.zeros((), value.dtype))


def heads_of(value):
    rows, width = value.shape
    lane = lax.broadcasted_iota(jnp.int32, (rows, width), 1)
    row = lax.broadcasted_iota(jnp.int32, (rows, width), 0)
    kept = jnp.where((lane >= row * HEAD_DIM) & (lane < (row + 1) * HEAD_DIM), value, 0.0)
    return jnp.sum(kept, axis=0, keepdims=True)


def two_rows(first, second):
    rows = lax.broadcasted_iota(jnp.int32, (ROW_TILE, first.shape[1]), 0)
    zero = jnp.zeros((), first.dtype)
    return jnp.where(rows == 0, first, jnp.where(rows == 1, second, zero))


def kept_places(width, ff, length):
    sizes = (("n1", width), ("n2", width), ("context", width), ("acts", ff), ("slope", ff), ("probs", 2 * length))
    places, start = {}, 0
    for name, size in sizes + (("r1", PAIR), ("r2", PAIR)):
        places[name] = (start, size)
        start += size
    return places


def head_kernel(
    info_ref, own_ref, other_ref, wp_ref, wi_ref, wo_ref, table,
    e_ref, kept_ref, acts, wp, wi, wo, sems,
):
    copies = [
        pltpu.make_async_copy(wp_ref, wp, sems.at[0]),
        pltpu.make_async_copy(wi_ref, wi, sems.at[1]),
        pltpu.make_async_copy(wo_ref, wo, sems.at[2]),
    ]
    for copy in copies:
        copy.start()
    pick = layer_vectors(table, table, info_ref[0] == 0)
    width, ff = wi.shape
    length = own_ref.shape[0]
    places = kept_places(width, ff, length)

    def put(name, value, offset=0):
        start = places[name][0] + offset
        kept_ref[:, start : start + value.shape[1]] = value.astype(F32)

    lane = lax.broadcasted_iota(jnp.int32, (ROW_TILE, length), 1)
    contexts = []
    for i, ref in enumerate((own_ref, other_ref)):
        query = by_head(ref[0:1, 0:width] * jnp.asarray(0.125, BF), ROW_TILE)
        scores = nt(query, ref[:, width : 2 * width])
        scores = jnp.where(lane < info_ref[1 + i], scores, BIG_NEG)
        raised = jnp.exp(scores - jnp.max(scores, axis=-1, keepdims=True))
        probs = raised / jnp.sum(raised, axis=-1, keepdims=True)
        put("probs", probs, i * length)
        contexts.append(heads_of(nn(probs.astype(BF), ref[:, 2 * width : 3 * width])))
    context = two_rows(*contexts).astype(BF)
    put("context", context)
    inputs = two_rows(own_ref[0:1, 3 * width :], other_ref[0:1, 3 * width :])
    copies[0].wait()
    n1, r1 = row_norm(inputs.astype(F32) + (nn(context, wp[...]) + pick(PROJ_B)))
    put("n1", n1)
    put("r1", r1)
    normed = n1 * pick(ATTN_G) + pick(ATTN_B)
    copies[1].wait()
    low = normed.astype(BF)
    for c in range(ff // width):
        cols = slice(c * width, (c + 1) * width)
        act, slope = gelu_pair(nn(low, wi[:, cols]) + pick(INNER_B, c))
        act = act.astype(BF)
        acts[:, cols] = act
        put("acts", act, c * width)
        put("slope", slope, c * width)
    copies[2].wait()
    n2, r2 = row_norm(normed + (nn(acts[...], wo[...]) + pick(OUTER_B)))
    put("n2", n2)
    put("r2", r2)
    e_ref[...] = (n2 * pick(FFN_G) + pick(FFN_B)).astype(BF)


def head_call(info, own, other, wp, wi, wo, table):
    length = own.shape[0]
    width, ff = wi.shape
    kept = max(place + size for place, size in kept_places(width, ff, length).values())
    shapes = [struct((ROW_TILE, width), BF), struct((ROW_TILE, kept), F32)]
    return pl.pallas_call(
        head_kernel,
        in_specs=[SCALARS, NEAR, NEAR, FAR, FAR, FAR, NEAR],
        out_specs=[NEAR] * len(shapes),
        out_shape=shapes,
        scratch_shapes=[pltpu.VMEM((ROW_TILE, ff), BF)]
        + [pltpu.VMEM(w.shape, BF) for w in (wp, wi, wo)]
        + [pltpu.SemaphoreType.DMA((3,))],
        compiler_params=params_of(22),
        cost_estimate=cost(7),
        name="head_rows",
    )(info, own, other, *far(wp, wi, wo), table)


def replace_first(xq, fixed):
    top_rows = xq[0:ROW_TILE, :]
    at_first = lax.broadcasted_iota(jnp.int32, top_rows.shape, 0) == 0
    xq[0:ROW_TILE, :] = jnp.where(at_first, fixed, top_rows)


def attention_parts(xq, j, width, lane, bias_col):
    base = pl.multiple_of(j * PAIR, PAIR)
    q = xq[:, pl.ds(base, PAIR)] * jnp.asarray(0.125, BF)
    k = xq[:, pl.ds(base + width, PAIR)]
    v = xq[:, pl.ds(base + 2 * width, PAIR)]
    zero = jnp.zeros_like(k)
    parts = []
    for h in range(2):
        mine = (lane >= HEAD_DIM * h) & (lane < HEAD_DIM * (h + 1))
        spare = lane == HEAD_DIM * (1 - h)
        qh = jnp.where(mine, q, jnp.where(spare, jnp.ones_like(q), zero))
        kh = jnp.where(mine, k, jnp.where(spare, bias_col, zero))
        parts.append((mine, qh, kh))
    return base, q, k, v, parts


def place_rows(ref, value, order):
    pieces, rows = ref.shape[0], ref.shape[1]
    for p in range(pieces):
        ref[jnp.bitwise_xor(p, order)] = value[p * rows : (p + 1) * rows, :]


def attend(xq, ctx, lse_scr, width, lane, bias_col):
    def pair_body(j, carry):
        base, q, k, v, parts = attention_parts(xq, j, width, lane, bias_col)
        sides = []
        for h, (mine, qh, kh) in enumerate(parts):
            vh = jnp.where(mine, v, jnp.ones_like(v))
            scores = nt(qh, kh)
            top = jnp.max(scores, axis=-1, keepdims=True)
            made = nn(jnp.exp(scores - top).astype(BF), vh)
            mass = made[:, HEAD_DIM * (1 - h) : HEAD_DIM * (1 - h) + 1]
            sides.append(made * (1.0 / mass))
            if lse_scr is not None:
                lse_scr[...] = jnp.where(lane == 2 * j + h, top + jnp.log(mass), lse_scr[...])
        ctx[:, pl.ds(base, PAIR)] = jnp.where(lane < HEAD_DIM, sides[0], sides[1]).astype(BF)
        return carry

    lax.fori_loop(0, HEADS // 2, pair_body, 0)


def mixing_kernel(info_ref, xq_a, xq_b, wp_a, wp_b, mine, table, normed_ref, xq, wp, ctx, sems):
    own = info_ref[0] == 0
    fetch(own, xq_a, xq_b, xq, sems.at[0])
    fetch(own, wp_a, wp_b, wp, sems.at[1])
    width = wp.shape[0]
    length = xq.shape[0]
    pick = layer_vectors(mine, table, own)
    lane = lax.broadcasted_iota(jnp.int32, (length, PAIR), 1)
    row = lax.broadcasted_iota(jnp.int32, (length, PAIR), 0)
    bias_col = jnp.where(row < info_ref[1], 0.0, BIG_NEG).astype(BF)
    landed(xq_a, xq, sems.at[0])
    attend(xq, ctx, None, width, lane, bias_col)
    landed(wp_a, wp, sems.at[1])
    n1, r1 = row_norm(xq[:, 3 * width :].astype(F32) + (nn(ctx[...], wp[...]) + pick(PROJ_B)))
    normed_ref[...] = n1 * pick(ATTN_G) + pick(ATTN_B)


def mixing_call(info, xq, wp, tables):
    length = xq[0].shape[0]
    width = wp[0].shape[0]
    return pl.pallas_call(
        mixing_kernel,
        in_specs=[SCALARS] + [FAR] * 4 + [NEAR] * 2,
        out_specs=NEAR,
        out_shape=struct((length, width), F32),
        scratch_shapes=[
            pltpu.VMEM(xq[0].shape, BF),
            pltpu.VMEM(wp[0].shape, BF),
            pltpu.VMEM((length, width), BF),
            pltpu.SemaphoreType.DMA((2,)),
        ],
        compiler_params=params_of(16),
        cost_estimate=cost(10),
        name="mixing",
    )(info, *far(*xq, *wp), *tables)


def train_kernel(
    info_ref, xq_a, xq_b, wq_a, wq_b, wp_a, wp_b, wi_a, wi_b, wo_a, wo_b, mine, table, head_ref, arrived_ref, cot_ref,
    z_ref, wp, wi, wo, ctx, lse_ref, fixed_ref, n1_ref, r1_ref, slope_ref, gf_ref, sg_ref, small_ref, keep_ref, send_ref,
    xq, lse_scr, sems,
):
    section = info_ref[0]
    own = section == 1
    fetch(own, xq_a, xq_b, xq, sems.at[0])
    width = wp.shape[0]
    length = xq.shape[0]
    ff = wi.shape[1]
    thirds = [(pl.ds(k * width, width), wo.at[pl.ds(k * width, width)]) for k in range(3)]
    for k, (cols, place) in enumerate(thirds):
        fetch(own, wq_a.at[:, cols], wq_b.at[:, cols], place, sems.at[5 + k])
    fetch(own, wp_a, wp_b, wp, sems.at[2])
    pick = layer_vectors(mine, table, own)
    lane = lax.broadcasted_iota(jnp.int32, (length, PAIR), 1)
    row = lax.broadcasted_iota(jnp.int32, (length, PAIR), 0)
    bias_col = jnp.where(row < info_ref[1], 0.0, BIG_NEG).astype(BF)
    many = jnp.broadcast_to(jnp.where(section == 0, head_ref[0:1, :], arrived_ref[1:2, :]), (ROW_TILE, width))
    fixed = []
    for k, shift in enumerate((pick(QUERY_B), None, pick(VALUE_B))):
        cols, place = thirds[k]
        landed(wq_a.at[:, cols], place, sems.at[5 + k])
        made = nn(many, place[...])
        fixed.append((made if shift is None else made + shift).astype(BF))
    fixed = jnp.concatenate(fixed + [many], axis=1)
    fixed_ref[...] = fixed
    landed(xq_a, xq, sems.at[0])
    fetch(own, wi_a, wi_b, wi, sems.at[3])
    fetch(own, wo_a, wo_b, wo, sems.at[4])
    copy = pltpu.make_async_copy(cot_ref.at[section], gf_ref, sems.at[1])
    copy.start()
    replace_first(xq, fixed)
    attend(xq, ctx, lse_scr, width, lane, bias_col)
    lse_ref[...] = jnp.transpose(lse_scr[...])[0:ROW_TILE, :]
    landed(wp_a, wp, sems.at[2])
    n1, r1 = row_norm(xq[:, 3 * width :].astype(F32) + (nn(ctx[...], wp[...]) + pick(PROJ_B)))
    n1_ref[...] = n1
    r1_ref[...] = r1
    normed = n1 * pick(ATTN_G) + pick(ATTN_B)
    low = normed.astype(BF)
    landed(wi_a, wi, sems.at[3])
    landed(wo_a, wo, sems.at[4])
    total = None
    for c in range(ff // CHUNK):
        cols = slice(c * CHUNK, (c + 1) * CHUNK)
        act, slope = gelu_pair(nn(low, wi[:, cols]) + pick(INNER_B, c))
        act = act.astype(BF)
        xq[:, cols] = act
        slope_ref[:, cols] = slope.astype(BF)
        term = nn(act, wo[cols, :])
        total = term if total is None else total + term
    n2, r2 = row_norm(normed + (total + pick(OUTER_B)))
    gain = pick(FFN_G)
    z_ref[...] = (n2 * gain + pick(FFN_B)).astype(BF)
    wide_row = lax.broadcasted_iota(jnp.int32, n2.shape, 0)
    copy.wait()
    grad = jnp.where(wide_row < info_ref[1], gf_ref[...].astype(F32), 0.0)
    second = norm_back(grad, n2, r2, gain)
    sg_ref[...] = second
    gf = second.astype(BF)
    gf_ref[...] = gf
    small_ref[0:1, :] = col_sum(gf)
    small_ref[1:2, :] = col_sum(grad * n2)
    small_ref[2:3, :] = col_sum(grad)
    half_chunks = ff // CHUNK // 2
    rows = send_ref.shape[1]
    each = CHUNK // rows
    for ref, half, order in ((send_ref, 1 - section, info_ref[4]), (keep_ref, section, info_ref[3])):
        for c in range(half_chunks):
            cols = pl.ds(pl.multiple_of((half * half_chunks + c) * CHUNK, CHUNK), CHUNK)
            made = tn(xq[:, cols], gf).astype(BF)
            for p in range(each):
                ref[jnp.bitwise_xor(c * each + p, order)] = made[p * rows : (p + 1) * rows, :]


def train_call(info, pairs, tables, head, arrived, cot):
    xq, wq, wp, wi, wo = (piece[0] for piece in pairs)
    length = xq.shape[0]
    width, ff = wi.shape
    args = [info]
    in_specs = [SCALARS]
    for pair in pairs:
        args += far(*pair)
        in_specs += [FAR, FAR]
    args += [*tables, head, arrived, *far(cot)]
    shapes = [
        struct((length, width), BF),
        near(wp.shape, BF),
        near(wi.shape, BF),
        near(wo.shape, BF),
        near((length, width), BF),
        near((ROW_TILE, length), F32),
        near((ROW_TILE, 4 * width), BF),
        near((length, width), F32),
        near((length, 1), F32),
        near((length, ff), BF),
        near((length, width), BF),
        near((length, width), F32),
        near((8, width), F32),
        near((GROUP, ff // 2 // GROUP, width), BF),
        near((GROUP, ff // 2 // GROUP, width), BF),
    ]
    return pl.pallas_call(
        train_kernel,
        in_specs=in_specs + [NEAR] * 4 + [FAR],
        out_specs=[NEAR] * len(shapes),
        out_shape=shapes,
        scratch_shapes=[
            pltpu.VMEM(xq.shape, BF),
            pltpu.VMEM((length, PAIR), F32),
            pltpu.SemaphoreType.DMA((8,)),
        ],
        compiler_params=params_of(14),
        cost_estimate=cost(26),
        name="layer_train",
    )(*args)


def feed_kernel(info_ref, normed_ref, wi_a, wi_b, wo_a, wo_b, mine, other, z_ref, wi, wo, sems):
    own = info_ref[0] == 0
    fetch(own, wi_a, wi_b, wi, sems.at[0])
    fetch(own, wo_a, wo_b, wo, sems.at[1])
    pick = layer_vectors(mine, other, own)
    normed = normed_ref[...]
    low = normed.astype(BF)
    landed(wi_a, wi, sems.at[0])
    landed(wo_a, wo, sems.at[1])
    total = None
    for c in range(wi.shape[1] // CHUNK):
        cols = slice(c * CHUNK, (c + 1) * CHUNK)
        act, slope = gelu_pair(nn(low, wi[:, cols]) + pick(INNER_B, c))
        term = nn(act.astype(BF), wo[cols, :])
        total = term if total is None else total + term
    n2, r2 = row_norm(normed + (total + pick(OUTER_B)))
    z_ref[...] = (n2 * pick(FFN_G) + pick(FFN_B)).astype(BF)


def feed_call(info, normed, wi, wo, tables):
    return pl.pallas_call(
        feed_kernel,
        in_specs=[SCALARS, NEAR] + [FAR] * 4 + [NEAR] * 2,
        out_specs=NEAR,
        out_shape=struct(normed.shape, BF),
        scratch_shapes=[pltpu.VMEM(wi[0].shape, BF), pltpu.VMEM(wo[0].shape, BF), pltpu.SemaphoreType.DMA((2,))],
        compiler_params=params_of(24),
        cost_estimate=cost(11),
        name="layer_feed",
    )(info, normed, *far(*wi, *wo), *tables)


def inner_kernel(
    info_ref, gf_ref, slope_ref, sg_ref, n1_ref, r1_ref, wi_ref, wo_ref, wp_ref, mine, table,
    keep_ref, send_ref, gh_ref, ga_ref, gc_ref, small_ref,
):
    section = info_ref[0]
    pick = layer_vectors(mine, table, section == 1)
    gain = pick(ATTN_G)
    low = jnp.transpose(n1_ref[...] * gain + pick(ATTN_B)).astype(BF)
    ff = wi_ref.shape[1]
    half_chunks = ff // CHUNK // 2
    gf = gf_ref[...]
    gn = sg_ref[...]
    for ref, half, order in ((send_ref, 1 - section, info_ref[6]), (keep_ref, section, info_ref[5])):
        for c in range(half_chunks):
            block = half * half_chunks + c
            cols = pl.ds(pl.multiple_of(block * CHUNK, CHUNK), CHUNK)
            gu = (nt(gf, wo_ref[cols, :]) * slope_ref[:, cols].astype(F32)).astype(BF)
            small_ref[pl.ds(3 + block, 1), :] = col_sum(gu)
            place_rows(ref.at[:, :, c * CHUNK : (c + 1) * CHUNK], nn(low, gu).astype(BF), order)
            gn = gn + nt(gu, wi_ref[:, cols])
    n1 = n1_ref[...]
    gh = norm_back(gn, n1, r1_ref[...], gain)
    gh_ref[...] = gh
    ga = gh.astype(BF)
    ga_ref[...] = ga
    gc_ref[...] = nt(ga, wp_ref[...]).astype(BF)
    small_ref[0:1, :] = col_sum(ga)
    small_ref[1:2, :] = col_sum(gn * n1)
    small_ref[2:3, :] = col_sum(gn)


def inner_call(info, gf, slope, sg, n1, r1, wi, wo, wp, tables):
    tokens, width = gf.shape
    ff = wi.shape[1]
    shapes = [
        near((GROUP, width // GROUP, ff // 2), BF),
        near((GROUP, width // GROUP, ff // 2), BF),
        near((tokens, width), F32),
        near((tokens, width), BF),
        near((tokens, width), BF),
        near((8, width), F32),
    ]
    return pl.pallas_call(
        inner_kernel,
        in_specs=[SCALARS] + [NEAR] * 10,
        out_specs=[NEAR] * len(shapes),
        out_shape=shapes,
        compiler_params=params_of(12),
        cost_estimate=cost(10),
        name="inner_grad",
    )(info, *stay(gf, slope, sg, n1, r1, wi, wo, wp), *tables)


def attention_kernel(
    info_ref, xq_a, xq_b, fixed_ref, gc_ref, ga_ref, c_ref, lse_ref, keep_ref, send_ref, g_ref, small_ref,
    xq, xt_scr, ct_scr, mean_scr, sem,
):
    section = info_ref[0]
    fetch(section == 1, xq_a, xq_b, xq, sem)
    length, width = gc_ref.shape
    row = lax.broadcasted_iota(jnp.int32, (length, PAIR), 0)
    lane = lax.broadcasted_iota(jnp.int32, (length, PAIR), 1)
    bias_col = jnp.where(row < info_ref[1], 0.0, BIG_NEG).astype(BF)
    ct_scr[...] = turned(c_ref[...])
    product = gc_ref[...].astype(F32) * c_ref[...].astype(F32)
    high = product.astype(BF)
    low = (product - high.astype(F32)).astype(BF)
    ones = by_head(jnp.ones((1, width), BF), ROW_TILE)
    mean_scr[...] = nt(ones, high) + nt(ones, low)
    landed(xq_a, xq, sem)
    replace_first(xq, fixed_ref[...])
    xt_scr[...] = turned(xq[:, 3 * width :])

    def pair_body(j, carry):
        base, q, k, v, parts = attention_parts(xq, j, width, lane, bias_col)
        kt = turned(k)
        gc = gc_ref[:, pl.ds(base, PAIR)]
        zero = jnp.zeros_like(gc)
        strips = [slice(s * STRIP, (s + 1) * STRIP) for s in range(length // STRIP)]
        gk = [None] * len(strips)
        gv = [None] * len(strips)
        gqt = []
        for h, (mine, qh, kh) in enumerate(parts):
            gch = jnp.where(mine, gc, zero)
            qz = jnp.where(mine, q, zero)
            lse = lse_ref[pl.ds(2 * j + h, 1), :]
            mean = mean_scr[pl.ds(2 * j + h, 1), :]
            gq_h = None
            for s, rows in enumerate(strips):
                probs = jnp.exp(nt(kh[rows, :], qh) - lse)
                gs = (probs * (nt(v[rows, :], gch) - mean)).astype(BF)
                gv_h = nn(probs.astype(BF), gch)
                gk_h = nn(gs, qz)
                term = nn(kt[HEAD_DIM * h : HEAD_DIM * (h + 1), rows], gs)
                gq_h = term if gq_h is None else gq_h + term
                gk[s] = gk_h if h == 0 else gk[s] + gk_h
                gv[s] = gv_h if h == 0 else gv[s] + gv_h
            gqt.append(gq_h)
        gq = jnp.transpose(jnp.concatenate(gqt, axis=0)) * 0.125
        g_ref[:, pl.ds(base, PAIR)] = gq.astype(BF)
        for s, rows in enumerate(strips):
            g_ref[rows, pl.ds(base + width, PAIR)] = gk[s].astype(BF)
            g_ref[rows, pl.ds(base + 2 * width, PAIR)] = gv[s].astype(BF)
        return carry

    lax.fori_loop(0, HEADS // 2, pair_body, 0)
    small_ref[0:1, :] = col_sum(g_ref[:, 0:width])
    small_ref[1:2, :] = col_sum(g_ref[:, 2 * width : 3 * width])
    wide = 3 * width // 2
    for ref, half, order in ((send_ref, 1 - section, info_ref[8]), (keep_ref, section, info_ref[7])):
        cols = pl.ds(pl.multiple_of(half * wide, PAIR), wide)
        place_rows(ref.at[:, :, 0:wide], nn(xt_scr[...], g_ref[:, cols]).astype(BF), order)
        cols = pl.ds(pl.multiple_of(half * (width // 2), PAIR), width // 2)
        place_rows(ref.at[:, :, wide:], nn(ct_scr[...], ga_ref[:, cols]).astype(BF), order)


def attention_call(info, xq, fixed, gc, ga, context, lse):
    length, width = gc.shape
    shapes = [
        near((GROUP, width // GROUP, 2 * width), BF),
        near((GROUP, width // GROUP, 2 * width), BF),
        near((length, 3 * width), BF),
        near((8, width), F32),
    ]
    return pl.pallas_call(
        attention_kernel,
        in_specs=[SCALARS, FAR, FAR] + [NEAR] * 5,
        out_specs=[NEAR] * len(shapes),
        out_shape=shapes,
        scratch_shapes=[
            pltpu.VMEM(xq[0].shape, BF),
            pltpu.VMEM((width, length), BF),
            pltpu.VMEM((width, length), BF),
            pltpu.VMEM((ROW_TILE, length), F32),
            pltpu.SemaphoreType.DMA(()),
        ],
        compiler_params=params_of(18),
        cost_estimate=cost(14),
        name="attention_grad",
    )(info, *far(*xq), *stay(fixed, gc, ga, context, lse))


def input_kernel(info_ref, w_a, w_b, g_ref, gh_ref, small1_ref, small2_ref, small3_ref, o_ref, small_ref, w, sem):
    fetch(info_ref[0] == 1, w_a, w_b, w, sem)
    landed(w_a, w, sem)
    made = gh_ref[...] + nt(g_ref[...], w[...])
    o_ref[...] = made
    small_ref[0:2, :] = small3_ref[0:2, :]
    small_ref[2:9, :] = small2_ref[0:7, :]
    small_ref[9:12, :] = small1_ref[0:3, :]
    small_ref[12:16, :] = made[0:4, :]


def input_call(info, g, gh, w, small1, small2, small3):
    return pl.pallas_call(
        input_kernel,
        in_specs=[SCALARS, FAR, FAR] + [NEAR] * 5,
        out_specs=[NEAR] * 2,
        out_shape=[struct(gh.shape, F32), struct((ROW_TILE, gh.shape[1]), F32)],
        scratch_shapes=[pltpu.VMEM(w[0].shape, BF), pltpu.SemaphoreType.DMA(())],
        compiler_params=params_of(12),
        cost_estimate=cost(4),
        name="input_grad",
    )(info, *far(*w), *stay(g, gh, small1, small2, small3))


def head_back_kernel(
    info_ref, small_a, small_b, kept_ref, own_ref, other_ref,
    wq_ref, wp_ref, wi_ref, wo_ref, table, x_ref, first_ref, second_ref, wq, wp, wi, wo, sems,
):
    copies = [
        pltpu.make_async_copy(ref, scr, sems.at[i])
        for i, (ref, scr) in enumerate(((wo_ref, wo), (wi_ref, wi), (wp_ref, wp), (wq_ref, wq)))
    ]
    for copy in copies:
        copy.start()
    width = wp.shape[0]
    length = own_ref.shape[0]
    ff = wi.shape[1]
    places = kept_places(width, ff, length)

    def kept(name, offset=0, size=None):
        start = places[name][0] + offset
        return kept_ref[:, start : start + (places[name][1] if size is None else size)]

    n1, n2 = kept("n1"), kept("n2")
    context = kept("context").astype(BF)
    pick = layer_vectors(table, table, info_ref[0] == 0)
    grad = two_rows(small_a[12:13, :], small_b[12:13, :]).astype(BF).astype(F32)
    second = norm_back(grad, n2, kept("r2", 0, 1), pick(FFN_G))
    gf = second.astype(BF)
    copies[0].wait()
    gu = (nt(gf, wo[...]) * kept("slope")).astype(BF)
    copies[1].wait()
    gn = second + nt(gu, wi[...])
    gh = norm_back(gn, n1, kept("r1", 0, 1), pick(ATTN_G))
    ga = gh.astype(BF)
    copies[2].wait()
    gc = nt(ga, wp[...]).astype(BF)
    normed = (n1 * pick(ATTN_G) + pick(ATTN_B)).astype(BF)
    copies[3].wait()
    query_bias = value_bias = jnp.zeros((1, width), F32)
    heads, rest = {}, {}
    for i, ref in enumerate((own_ref, other_ref)):
        mid = (1 - 2 * i) * info_ref[0] + i
        keys, values, inputs = ref[:, width : 2 * width], ref[:, 2 * width : 3 * width], ref[:, 3 * width :]
        query = ref[0:1, 0:width] * jnp.asarray(0.125, BF)
        gc_row = gc[i : i + 1, :]
        query_heads, gc_heads = by_head(query, ROW_TILE), by_head(gc_row, ROW_TILE)
        probs = kept("probs", i * length, length)
        gp = nt(gc_heads, values)
        gs = (probs * (gp - jnp.sum(probs * gp, axis=-1, keepdims=True))).astype(BF)
        low = probs.astype(BF)
        gq = (heads_of(nn(gs, keys)) * 0.125).astype(BF)
        for place, value in ((KEY_SUMS, nn(gs, inputs)), (VALUE_SUMS, nn(low, inputs))):
            for h in range(HEADS):
                heads[place + HEADS * i + h] = value[h : h + 1, :]
        key_back = nt(query_heads, wq[:, width : 2 * width]).astype(BF)
        value_back = nt(gc_heads, wq[:, 2 * width :]).astype(BF)
        gx = tn(gs, key_back) + tn(low, value_back)
        top = gh[i : i + 1, :] + nt(jnp.broadcast_to(gq, (ROW_TILE, width)), wq[:, 0:width])[0:1, :]
        at_first = lax.broadcasted_iota(jnp.int32, gx.shape, 0) == 0
        x_ref[mid] = gx + jnp.where(at_first, top, 0.0)
        query_bias = query_bias + gq.astype(F32)
        mass = jnp.sum(low.astype(F32), axis=-1, keepdims=True)
        value_bias = value_bias + heads_of(gc_heads.astype(F32) * mass)
        heads[QUERIES + i] = query
        heads[GCONTEXTS + i] = gc_row
        for place, value in ((OUTERS, gf), (NORMEDS, normed), (CONTEXTS, context), (PROJS, ga)):
            rest[place + i] = value[i : i + 1, :]
        rest[INPUTS + i] = ref[0:1, 3 * width :]
        rest[GQUERIES + i] = gq
    gu_sum = col_sum(gu)
    act = kept("acts").astype(BF)
    own_small = [query_bias, value_bias, col_sum(ga), col_sum(gn * n1), col_sum(gn)]
    own_small += [gu_sum[:, width * k : width * (k + 1)] for k in range(ff // width)]
    own_small += [col_sum(gf), col_sum(grad * n2), col_sum(grad)]

    for k in range(ff // width):
        for i in range(2):
            rest[ACTS + 4 * i + k] = act[i : i + 1, width * k : width * (k + 1)]
            rest[INNERS + 4 * i + k] = gu[i : i + 1, width * k : width * (k + 1)]
    row = lax.broadcasted_iota(jnp.int32, (8, width), 0)
    for ref, rows in ((first_ref, heads), (second_ref, rest)):
        for k, piece in enumerate(own_small):
            rows[SUMS + k] = jnp.where(info_ref[0] == 0, piece, small_a[k : k + 1, :] + small_b[k : k + 1, :])
        for start in range(0, FACTORS, 8):
            made = jnp.zeros((8, width), F32)
            for k in range(8):
                if start + k in rows:
                    made = jnp.where(row == k, rows[start + k].astype(F32), made)
            ref[start : start + 8, :] = made.astype(BF)


def head_back_call(info, small_a, small_b, kept, own, other, wq, wp, wi, wo, table):
    length = own.shape[0]
    width, ff = wi.shape
    args = [small_a, small_b, kept, own, other]
    return pl.pallas_call(
        head_back_kernel,
        in_specs=[SCALARS] + [NEAR] * len(args) + [FAR] * 4 + [NEAR],
        out_specs=[NEAR] * 3,
        out_shape=[struct((2, length, width), F32)] + [struct((FACTORS, width), BF)] * 2,
        scratch_shapes=[pltpu.VMEM(w.shape, BF) for w in (wq, wp, wi, wo)] + [pltpu.SemaphoreType.DMA((4,))],
        compiler_params=params_of(28),
        cost_estimate=cost(12),
        name="head_rows_grad",
    )(info, *args, *far(wq, wp, wi, wo), table)


def piece_at(low, high, place, cols=slice(None)):
    half = low.shape[0]
    inside = lax.rem(place, half)
    return jnp.where(place < half, low[inside, :, cols], high[inside, :, cols])


def feed_final_kernel(outer, info_ref, a_low, a_high, b_low, b_high, rest_ref, o_ref, buffers, sems):
    width = buffers.shape[1]
    rows = a_low.shape[1]
    first = 4 if outer else 6
    halves = ((a_low, a_high, info_ref[first]), (b_low, b_high, info_ref[first - 1]))

    def products(left, right):
        return sum(tn(rest_ref[left[0] + j * left[1]], rest_ref[right[0] + j * right[1]]) for j in range(2))

    copies = []
    for k in range(4):
        slot = k % 2
        if k >= 2:
            copies[k - 2].wait()

        @pl.when(info_ref[0] == 1)
        def _():
            low, high, order = halves[k // 2]
            for p in range(width // rows):
                if outer:
                    piece = piece_at(low, high, jnp.bitwise_xor((k % 2) * (width // rows) + p, order))
                else:
                    cols = slice((k % 2) * width, (k % 2 + 1) * width)
                    piece = piece_at(low, high, jnp.bitwise_xor(p, order), cols)
                buffers[slot, p * rows : (p + 1) * rows, :] = piece.astype(F32)

        @pl.when(info_ref[0] == 0)
        def _():
            left, right = ((ACTS + k, 4), (OUTERS, 1)) if outer else ((NORMEDS, 1), (INNERS + k, 4))
            buffers[slot] = products(left, right)

        block = slice(k * width, (k + 1) * width)
        target = o_ref.at[block, :] if outer else o_ref.at[:, block]
        copies.append(pltpu.make_async_copy(buffers.at[slot], target, sems.at[slot]))
        copies[-1].start()
    copies[-2].wait()
    copies[-1].wait()


def feed_final_call(outer, info, quarters, rest):
    width = rest.shape[2]
    ff = 4 * width
    return pl.pallas_call(
        lambda *refs: feed_final_kernel(outer, *refs),
        in_specs=[SCALARS] + [NEAR] * 5,
        out_specs=FAR,
        out_shape=struct((ff, width) if outer else (width, ff), F32),
        scratch_shapes=[pltpu.VMEM((2, width, width), F32), pltpu.SemaphoreType.DMA((2,))],
        compiler_params=params_of(10),
        cost_estimate=cost(4),
        name="outer_final" if outer else "inner_final",
    )(info, *quarters, rest)


def qkv_final_kernel(info_ref, a_low, a_high, b_low, b_high, heads_ref, rest_ref, o_ref, p_ref, made, made_p, sems):
    width = p_ref.shape[0]
    wide = 3 * width // 2
    half = width // 2
    rows = a_low.shape[1]

    @pl.when(info_ref[0] == 1)
    def _():
        copies = []
        for k, (low, high, order) in enumerate(((a_low, a_high, info_ref[8]), (b_low, b_high, info_ref[7]))):
            for p in range(GROUP):
                place = jnp.bitwise_xor(p, order)
                at = slice(p * rows, (p + 1) * rows)
                made[at, k * wide : (k + 1) * wide] = piece_at(low, high, place, slice(0, wide)).astype(F32)
                piece = piece_at(low, high, place, slice(wide, wide + half))
                made_p[at, k * half : (k + 1) * half] = piece.astype(F32)
            cols = slice(k * wide, (k + 1) * wide)
            copies.append(pltpu.make_async_copy(made.at[:, cols], o_ref.at[:, cols], sems.at[k]))
            copies[-1].start()
        copies.append(pltpu.make_async_copy(made_p, p_ref, sems.at[2]))
        copies[-1].start()
        for copy in copies:
            copy.wait()

    @pl.when(info_ref[0] == 0)
    def _():
        def pairs(left, right):
            return tn(rest_ref[left], rest_ref[right]) + tn(rest_ref[left + 1], rest_ref[right + 1])

        made_p[...] = pairs(CONTEXTS, PROJS)
        copies = [pltpu.make_async_copy(made_p, p_ref, sems.at[3])]
        copies[-1].start()
        chips = heads_ref.shape[1]
        lane = lax.broadcasted_iota(jnp.int32, (chips, width), 1)
        for place, base, key in ((0, 0, 0), (1, KEY_SUMS, QUERIES), (2, VALUE_SUMS, GCONTEXTS)):
            cols = slice(place * width, (place + 1) * width)
            if place == 0:
                made[:, cols] = pairs(INPUTS, GQUERIES)
            else:
                term = None
                for j in range(2):
                    left = heads_ref[base + HEADS * j : base + HEADS * j + HEADS].reshape(HEADS * chips, width)
                    row = heads_ref[key + j]
                    heads = [
                        jnp.where((lane >= HEAD_DIM * h) & (lane < HEAD_DIM * (h + 1)), row, jnp.zeros_like(row))
                        for h in range(HEADS)
                    ]
                    one = tn(left, jnp.concatenate(heads, axis=0))
                    term = one if term is None else term + one
                made[:, cols] = term
            copies.append(pltpu.make_async_copy(made.at[:, cols], o_ref.at[:, cols], sems.at[4 + place]))
            copies[-1].start()
        for copy in copies:
            copy.wait()


def qkv_final_call(info, quarters, heads, rest):
    width = rest.shape[2]
    return pl.pallas_call(
        qkv_final_kernel,
        in_specs=[SCALARS] + [NEAR] * 6,
        out_specs=[FAR, FAR],
        out_shape=[struct((width, 3 * width), F32), struct((width, width), F32)],
        scratch_shapes=[
            pltpu.VMEM((width, 3 * width), F32),
            pltpu.VMEM((width, width), F32),
            pltpu.SemaphoreType.DMA((7,)),
        ],
        compiler_params=params_of(16),
        cost_estimate=cost(4),
        name="qkv_final",
    )(info, *quarters, heads, rest)


def swap(value):
    return lax.ppermute(value, "section", SWAP)


def add_low(left, right):
    return (left.astype(F32) + right.astype(F32)).astype(BF)


def hop(value, stage, orders):
    chips = lax.axis_size("dp")
    pairs = [
        (section * chips + chip, section * chips + (chip ^ orders[section][stage]))
        for section in range(2)
        for chip in range(chips)
    ]
    return lax.ppermute(value, ("section", "dp"), pairs)


def after(value, *others):
    return lax.optimization_barrier((value,) + others)[0]


def beside(made, *sums):
    tied = lax.optimization_barrier(tuple(made) + tuple(one.coming for one in sums))
    for one, coming in zip(sums, tied[len(made) :]):
        one.coming = coming
    return tied[: len(made)]


class Sum:
    def __init__(self, keep, send, group):
        self.low, self.coming, self.orders = keep, swap(send), ORDERS[group]

    def add(self):
        half = self.coming.shape[0] // 2
        if half == 0:
            self.part = add_low(self.low, self.coming)
            return
        self.high = add_low(self.low[half:], self.coming[half:])
        self.low = self.part = add_low(self.low[:half], self.coming[:half])

    def halve(self, stage):
        self.coming = hop(self.high, stage, self.orders)

    def across(self):
        chips = lax.axis_size("dp")
        if chips > GROUP:
            groups = [[low + GROUP * high for high in range(chips // GROUP)] for low in range(GROUP)]
            self.part = lax.psum(self.part, "dp", axis_index_groups=groups)

    def double(self, stage):
        self.coming = hop(self.part, stage, self.orders)

    def join(self):
        self.part = jnp.concatenate([self.part, self.coming], axis=0)

    def quarters(self, line):
        return (swap(line(self.part)), swap(line(self.coming)), self.part, self.coming)


class Line:
    def __init__(self):
        self.token = None

    def __call__(self, value):
        return value if self.token is None else after(value, self.token)

    def run(self, work, *args):
        made = work(*args)
        tied = lax.optimization_barrier(tuple(made))
        self.token = tied[0]
        return tied

    def take(self, group):
        group.coming = self(group.coming)
        self.token = group.coming

    def halve(self, group, stage):
        self.take(group)
        group.add()
        group.halve(stage)
        self.token = group.part

    def double(self, group, stage):
        self.take(group)
        group.add()
        group.across()
        group.double(stage)
        self.token = group.part

    def join(self, group, stage):
        self.take(group)
        group.join()
        if stage is not None:
            group.double(stage)
        self.token = group.part


class Gather:
    ORDERS = ((8, 4, 2, 1), (4, 8, 1, 2))

    def __init__(self, value):
        self.part = value[None]

    def double(self, stage):
        self.coming = hop(self.part, stage, self.ORDERS)

    def join(self):
        self.part = lax.optimization_barrier(jnp.concatenate([self.part, self.coming], axis=0))

    def across(self):
        chips = lax.axis_size("dp")
        if chips > GROUP:
            groups = [[low + GROUP * high for high in range(chips // GROUP)] for low in range(GROUP)]
            every = lax.all_gather(self.part, "dp", axis_index_groups=groups)
            self.part = every.reshape((-1,) + self.part.shape[1:])


def order_of(chip, orders):
    place = jnp.int32(0)
    for stage in range(4):
        bit = (chip // orders[stage]) % 2
        place = place + bit * (8 >> stage)
    return place


def local(embeddings, cotangent, lengths, *weights):
    (wq, query_bias, value_bias, wp, proj_bias, attn_gain, attn_bias, wi, inner_bias, wo, outer_bias, ffn_gain, ffn_bias) = (
        piece[0] for piece in weights
    )
    section = lax.axis_index("section")
    chip = lax.axis_index("dp")
    first_section = section == 0
    inputs = embeddings[0]
    width = inputs.shape[2]
    scalars = [section, jnp.where(first_section, lengths[0], lengths[1]), jnp.where(first_section, lengths[1], lengths[0])]
    for orders in ORDERS:
        places = [order_of(chip, order) for order in orders]
        scalars += [jnp.where(first_section, places[0], places[1]), jnp.where(first_section, places[1], places[0])]
    info = jnp.stack(scalars).astype(jnp.int32)
    vectors = [weights[k] for k in (1, 2, 4, 5, 6, 8, 10, 11, 12)]
    own, other, own_table = qkv_call(info, inputs, wq, vectors)
    tables = (own_table, swap(own_table))
    wq_pair = (wq, swap(wq))
    wp_pair = (wp, swap(wp))
    xq_pair = (own, swap(other))
    wi_pair = (wi, swap(wi))
    wo_pair = (wo, swap(wo))
    head = head_call(info, own, other, wp, wi, wo, own_table)
    arrived = swap(head[0])
    pairs = (xq_pair, wq_pair, wp_pair, wi_pair, wo_pair)
    (z, wp_d, wi_d, wo_d, context, lse, fixed, n1, r1, slope, gf, sg, small1, outer_keep, outer_send) = train_call(
        info, pairs, tables, head[0], arrived, cotangent
    )
    g1 = Sum(outer_keep, outer_send, 0)

    made = inner_call(info, gf, slope, sg, n1, r1, wi_d, wo_d, wp_d, tables)
    inner_keep, inner_send, gh, ga, gc, small2 = beside(made, g1)
    g1.add()
    g1.halve(0)
    g2 = Sum(inner_keep, inner_send, 1)

    made = attention_call(info, xq_pair, fixed, after(gc, g1.part), ga, context, lse)
    qkv_keep, qkv_send, g_qkv, small3 = beside(made, g1)
    line = Line()
    line.halve(g2, 0)
    line.halve(g1, 1)
    g3 = Sum(qkv_keep, line(qkv_send), 2)
    gx, dsmall = line.run(input_call, info, line(g_qkv), gh, wq_pair, small1, small2, small3)
    dsmall_other = swap(line(dsmall))
    line.halve(g3, 0)
    encoder_gx, heads, rest = line.run(
        head_back_call, info, dsmall, line(dsmall_other), head[1], own, other, wq, wp, wi, wo, own_table
    )
    came = swap(line(rest))
    gx_other = swap(line(gx))
    line.halve(g1, 2)
    (normed,) = line.run(lambda *a: (mixing_call(*a),), info, xq_pair, wp_pair, (own_table, line(tables[1])))
    line.halve(g2, 1)
    line.halve(g3, 1)
    shared = jnp.where(first_section, heads, jnp.concatenate([line(came)[:SUMS], heads[SUMS:]]))
    factors = Gather(shared)
    factors.double(0)
    line.token = factors.part
    line.halve(g1, 3)
    line.halve(g2, 2)
    line.join(factors, 1)
    line.halve(g3, 2)
    line.double(g1, 3)
    line.join(factors, 2)
    line.halve(g2, 3)
    line.halve(g3, 3)
    line.join(g1, 2)
    line.double(g2, 3)
    line.join(factors, 3)
    line.double(g3, 3)
    line.join(g2, 2)
    line.join(g1, 1)
    line.join(g3, 2)
    line.join(g2, 1)
    line.join(g1, 0)
    (e_low,) = line.run(lambda *a: (feed_call(*a),), info, line(normed), wi_pair, wo_pair, tables)
    line.join(g3, 1)
    line.join(g2, 0)
    line.join(factors, None)
    factors.across()
    sums = jnp.sum(line(factors.part)[:, SUMS:].astype(F32), axis=0)
    heads_all = jnp.transpose(factors.part, (1, 0, 2))
    heads_all, sums = line.run(lambda *a: a, heads_all, sums)
    line.join(g3, 0)
    rest_all = swap(line(heads_all)[:SUMS])
    z_other = swap(line(jnp.where(first_section, z, e_low)))
    z_mine = jnp.where(first_section, e_low, z)
    line.take(g1)
    outer_quarters = g1.quarters(line)
    decoder_gx = jnp.stack([line(gx_other), gx])
    later = jnp.arange(gx.shape[0])[None, :, None] > 0
    (embed_grads,) = line.run(lambda a: (jnp.where(first_section, encoder_gx, jnp.where(later, a, 0.0)),), decoder_gx)
    outputs = jnp.where(first_section, jnp.stack([z_mine, line(z_other)]), jnp.stack([z_other, z_mine]))
    (outputs,) = line.run(lambda a: (a,), outputs)
    (outer_grad,) = line.run(lambda *a: (feed_final_call(True, *a),), info, outer_quarters, line(rest_all))
    line.take(g2)
    inner_quarters = g2.quarters(line)
    line.take(g3)
    qkv_quarters = g3.quarters(line)
    (inner_grad,) = line.run(lambda *a: (feed_final_call(False, *a),), info, inner_quarters, line(rest_all))
    qkv_grad, proj_grad = line.run(qkv_final_call, info, qkv_quarters, heads_all, line(rest_all))
    results = (
        outputs,
        embed_grads,
        qkv_grad,
        sums[0],
        sums[1],
        proj_grad,
        sums[2],
        sums[3],
        sums[4],
        inner_grad,
        sums[5:9].reshape(-1),
        outer_grad,
        sums[9],
        sums[10],
        sums[11],
    )
    return tuple(piece[None] for piece in results)


def solution(mesh):
    matrix = P("section", None, None)
    vector = P("section", None)
    return jax.shard_map(
        local,
        mesh=mesh,
        in_specs=(P("section", "dp", None, None), P("dp", None, None), P("dp"))
        + (matrix, vector, vector, matrix, vector, vector, vector)
        + (matrix, vector, matrix, vector, vector, vector),
        out_specs=(P("section", "dp", None, None), P("section", "dp", None, None))
        + (matrix, vector, vector, matrix, vector, vector, vector)
        + (matrix, vector, matrix, vector, vector, vector),
        check_vma=False,
    )
```

```python
import math

import jax
import jax.numpy as jnp
from jax import lax
from jax.experimental import pallas as pl
from jax.experimental.pallas import tpu as pltpu
from jax.sharding import PartitionSpec as P

HEADS = 12
HEAD_DIM = 64
PAIR = 2 * HEAD_DIM
EPSILON = 1e-06
BIG_NEG = -1e30
BF = jnp.bfloat16
F32 = jnp.float32
CHUNK = 768
GROUP = 16
ROW_TILE = 16
ORDERS = (
    ((2, 1, 8, 4), (1, 4, 2, 8)),
    ((8, 1, 2, 4), (2, 4, 8, 1)),
    ((1, 2, 4, 8), (2, 1, 8, 4)),
)
SWAP = ((0, 1), (1, 0))
KEY_SUMS, VALUE_SUMS, QUERIES, GCONTEXTS = 0, 24, 48, 50
OUTERS, NORMEDS, CONTEXTS, PROJS, INPUTS, GQUERIES, ACTS, INNERS = 0, 2, 4, 6, 8, 10, 12, 20
SUMS, FACTORS = 52, 64


def params_of(mebibytes):
    return pltpu.CompilerParams(vmem_limit_bytes=mebibytes * 1024 * 1024)


def cost(micros):
    return pl.CostEstimate(flops=int(micros * 0.11e9), bytes_accessed=int(micros * 0.2e6), transcendentals=0)


def nn(left, right):
    return lax.dot_general(left, right, (((1,), (0,)), ((), ())), preferred_element_type=F32)


def nt(left, right):
    return lax.dot_general(left, right, (((1,), (1,)), ((), ())), preferred_element_type=F32)


def tn(left, right):
    return lax.dot_general(left, right, (((0,), (0,)), ((), ())), preferred_element_type=F32)


def turned(value):
    return jnp.transpose(value.astype(F32)).astype(BF)


def col_sum(value):
    return jnp.sum(value.astype(F32), axis=0, keepdims=True)


def row_norm(hidden):
    centred = hidden - jnp.mean(hidden, axis=-1, keepdims=True)
    scale = lax.rsqrt(jnp.mean(centred * centred, axis=-1, keepdims=True) + EPSILON)
    return (centred * scale, scale)


def norm_back(grad, normal, scale, gain):
    scaled = grad * gain
    return scale * (
        scaled
        - jnp.mean(scaled, axis=-1, keepdims=True)
        - normal * jnp.mean(scaled * normal, axis=-1, keepdims=True)
    )


def gelu_pair(value):
    bell = jnp.exp(-0.5 * (value * value))
    t = 1.0 / (1.0 + (0.3275911 / math.sqrt(2.0)) * jnp.abs(value))
    series = 0.5307027145 * t - 0.7265760135
    series = series * t + 0.7107068705
    series = series * t - 0.142248368
    series = series * t + 0.127414796
    tail = (series * t) * bell
    mass = jnp.where(value >= 0.0, 1.0 - tail, tail)
    return (value * mass, mass + value * (bell * (1.0 / math.sqrt(2.0 * math.pi))))


def fetch(first, own, other, target, sem):
    @pl.when(first)
    def _():
        pltpu.make_async_copy(own, target, sem).start()

    @pl.when(jnp.logical_not(first))
    def _():
        pltpu.make_async_copy(other, target, sem).start()


def landed(own, target, sem):
    pltpu.make_async_copy(own, target, sem).wait()


FAR = pl.BlockSpec(memory_space=pltpu.HBM)
ANYWHERE = pl.BlockSpec(memory_space=pl.ANY)
SCALARS = pl.BlockSpec(memory_space=pltpu.SMEM)
NEAR = pl.BlockSpec(memory_space=pltpu.VMEM)


def struct(shape, kind):
    return jax.ShapeDtypeStruct(tuple(shape), kind)


def near(shape, kind):
    return pltpu.VMEM(tuple(shape), kind)


def full(shape):
    return pl.BlockSpec(tuple(shape), lambda *_: (0,) * len(shape))


def far(*values):
    return tuple(pltpu.with_memory_space_constraint(value, pltpu.HBM) for value in values)


def stay(*values):
    return tuple(pltpu.with_memory_space_constraint(value, pltpu.VMEM) for value in values)


QUERY_B, VALUE_B, PROJ_B, ATTN_G, ATTN_B, INNER_B, OUTER_B, FFN_G, FFN_B = range(9)
TABLE_ROWS = (0, 1, 2, 3, 4, 5, 9, 10, 11)


def layer_vectors(mine, other, own):
    def pick(k, part=0):
        row = TABLE_ROWS[k] + part
        return jnp.where(own, mine[row : row + 1, :], other[row : row + 1, :])

    return pick


def qkv_kernel(info_ref, x_ref, w_ref, *refs):
    vectors = refs[:9]
    qb_ref, vb_ref = vectors[QUERY_B], vectors[VALUE_B]
    own_ref, other_ref, table_ref = refs[9:]
    step = pl.program_id(0)
    half = pl.num_programs(0) // 2
    width = x_ref.shape[2]
    x = x_ref[0]

    def put(ref):
        for k, shift in enumerate((qb_ref[...], None, vb_ref[...])):
            made = nn(x, w_ref[:, k * width : (k + 1) * width])
            ref[:, k * width : (k + 1) * width] = (made if shift is None else made + shift).astype(BF)
        ref[:, 3 * width :] = x

    pl.when(step < half)(lambda: put(other_ref))
    pl.when(step >= half)(lambda: put(own_ref))

    @pl.when(step == 0)
    def _():
        for ref, row in zip(vectors, TABLE_ROWS):
            for part in range(ref.shape[1] // width):
                table_ref[row + part : row + part + 1, :] = ref[:, part * width : (part + 1) * width]


def qkv_call(info, inputs, weight, vectors, rows=256):
    count, length, width = inputs.shape
    wide = weight.shape[1] + width
    half = length // rows
    return pl.pallas_call(
        qkv_kernel,
        grid_spec=pltpu.PrefetchScalarGridSpec(
            num_scalar_prefetch=1,
            grid=(2 * half,),
            in_specs=[
                pl.BlockSpec(
                    (1, rows, width),
                    lambda i, info: (jnp.where(i < half, 1 - info[0], info[0]), lax.rem(i, half), 0),
                ),
                pl.BlockSpec(weight.shape, lambda i, info: (0, 0), pipeline_mode=pl.Buffered(1)),
            ]
            + [full(v.shape) for v in vectors],
            out_specs=[
                pl.BlockSpec((rows, wide), lambda i, info: (jnp.maximum(i - half, 0), 0)),
                pl.BlockSpec((rows, wide), lambda i, info: (jnp.minimum(i, half - 1), 0)),
                full((ROW_TILE, width)),
            ],
        ),
        out_shape=[struct((length, wide), BF)] * 2 + [struct((ROW_TILE, width), F32)],
        compiler_params=params_of(20),
        cost_estimate=cost(6),
        name="qkv",
    )(info, *far(inputs, weight, *vectors))


def by_head(value, rows):
    width = value.shape[1]
    lane = lax.broadcasted_iota(jnp.int32, (rows, width), 1)
    row = lax.broadcasted_iota(jnp.int32, (rows, width), 0)
    return jnp.where((lane >= row * HEAD_DIM) & (lane < (row + 1) * HEAD_DIM), value, jnp.zeros((), value.dtype))


def heads_of(value):
    rows, width = value.shape
    lane = lax.broadcasted_iota(jnp.int32, (rows, width), 1)
    row = lax.broadcasted_iota(jnp.int32, (rows, width), 0)
    kept = jnp.where((lane >= row * HEAD_DIM) & (lane < (row + 1) * HEAD_DIM), value, 0.0)
    return jnp.sum(kept, axis=0, keepdims=True)


def two_rows(first, second):
    rows = lax.broadcasted_iota(jnp.int32, (ROW_TILE, first.shape[1]), 0)
    zero = jnp.zeros((), first.dtype)
    return jnp.where(rows == 0, first, jnp.where(rows == 1, second, zero))


def kept_places(width, ff, length):
    sizes = (("n1", width), ("n2", width), ("context", width), ("acts", ff), ("slope", ff), ("probs", 2 * length))
    places, start = {}, 0
    for name, size in sizes + (("r1", PAIR), ("r2", PAIR)):
        places[name] = (start, size)
        start += size
    return places


def head_kernel(
    info_ref, own_ref, other_ref, wp_ref, wi_ref, wo_ref, table,
    e_ref, kept_ref, acts, wp, wi, wo, sems,
):
    copies = [
        pltpu.make_async_copy(wp_ref, wp, sems.at[0]),
        pltpu.make_async_copy(wi_ref, wi, sems.at[1]),
        pltpu.make_async_copy(wo_ref, wo, sems.at[2]),
    ]
    for copy in copies:
        copy.start()
    pick = layer_vectors(table, table, info_ref[0] == 0)
    width, ff = wi.shape
    length = own_ref.shape[0]
    places = kept_places(width, ff, length)

    def put(name, value, offset=0):
        start = places[name][0] + offset
        kept_ref[:, start : start + value.shape[1]] = value.astype(F32)

    lane = lax.broadcasted_iota(jnp.int32, (ROW_TILE, length), 1)
    contexts = []
    for i, ref in enumerate((own_ref, other_ref)):
        query = by_head(ref[0:1, 0:width] * jnp.asarray(0.125, BF), ROW_TILE)
        scores = nt(query, ref[:, width : 2 * width])
        scores = jnp.where(lane < info_ref[1 + i], scores, BIG_NEG)
        raised = jnp.exp(scores - jnp.max(scores, axis=-1, keepdims=True))
        probs = raised / jnp.sum(raised, axis=-1, keepdims=True)
        put("probs", probs, i * length)
        contexts.append(heads_of(nn(probs.astype(BF), ref[:, 2 * width : 3 * width])))
    context = two_rows(*contexts).astype(BF)
    put("context", context)
    inputs = two_rows(own_ref[0:1, 3 * width :], other_ref[0:1, 3 * width :])
    copies[0].wait()
    n1, r1 = row_norm(inputs.astype(F32) + (nn(context, wp[...]) + pick(PROJ_B)))
    put("n1", n1)
    put("r1", r1)
    normed = n1 * pick(ATTN_G) + pick(ATTN_B)
    copies[1].wait()
    low = normed.astype(BF)
    for c in range(ff // width):
        cols = slice(c * width, (c + 1) * width)
        act, slope = gelu_pair(nn(low, wi[:, cols]) + pick(INNER_B, c))
        act = act.astype(BF)
        acts[:, cols] = act
        put("acts", act, c * width)
        put("slope", slope, c * width)
    copies[2].wait()
    n2, r2 = row_norm(normed + (nn(acts[...], wo[...]) + pick(OUTER_B)))
    put("n2", n2)
    put("r2", r2)
    e_ref[0:ROW_TILE, :] = table[...]
    e_ref[ROW_TILE:, :] = (n2 * pick(FFN_G) + pick(FFN_B)).astype(BF).astype(F32)


def head_call(info, own, other, wp, wi, wo, table):
    length = own.shape[0]
    width, ff = wi.shape
    kept = max(place + size for place, size in kept_places(width, ff, length).values())
    shapes = [struct((2 * ROW_TILE, width), F32), struct((ROW_TILE, kept), F32)]
    return pl.pallas_call(
        head_kernel,
        in_specs=[SCALARS, NEAR, NEAR, FAR, FAR, FAR, NEAR],
        out_specs=[NEAR] * len(shapes),
        out_shape=shapes,
        scratch_shapes=[pltpu.VMEM((ROW_TILE, ff), BF)]
        + [pltpu.VMEM(w.shape, BF) for w in (wp, wi, wo)]
        + [pltpu.SemaphoreType.DMA((3,))],
        compiler_params=params_of(22),
        cost_estimate=cost(7),
        name="head_rows",
    )(info, own, other, *far(wp, wi, wo), table)


def replace_first(xq, fixed):
    top_rows = xq[0:ROW_TILE, :]
    at_first = lax.broadcasted_iota(jnp.int32, top_rows.shape, 0) == 0
    xq[0:ROW_TILE, :] = jnp.where(at_first, fixed, top_rows)


def attention_parts(xq, j, width, lane, bias_col):
    base = pl.multiple_of(j * PAIR, PAIR)
    q = xq[:, pl.ds(base, PAIR)] * jnp.asarray(0.125, BF)
    k = xq[:, pl.ds(base + width, PAIR)]
    v = xq[:, pl.ds(base + 2 * width, PAIR)]
    zero = jnp.zeros_like(k)
    parts = []
    for h in range(2):
        mine = (lane >= HEAD_DIM * h) & (lane < HEAD_DIM * (h + 1))
        spare = lane == HEAD_DIM * (1 - h)
        qh = jnp.where(mine, q, jnp.where(spare, jnp.ones_like(q), zero))
        kh = jnp.where(mine, k, jnp.where(spare, bias_col, zero))
        parts.append((mine, qh, kh))
    return base, q, k, v, parts


def place_rows(ref, value, order):
    pieces, rows = ref.shape[0], ref.shape[1]
    for p in range(pieces):
        ref[jnp.bitwise_xor(p, order)] = value[p * rows : (p + 1) * rows, :]


def attend(xq, ctx, lse_scr, width, lane, bias_col):
    def pair_body(j, carry):
        base, q, k, v, parts = attention_parts(xq, j, width, lane, bias_col)
        sides = []
        for h, (mine, qh, kh) in enumerate(parts):
            vh = jnp.where(mine, v, jnp.ones_like(v))
            scores = nt(qh, kh)
            top = jnp.max(scores, axis=-1, keepdims=True)
            made = nn(jnp.exp(scores - top).astype(BF), vh)
            mass = made[:, HEAD_DIM * (1 - h) : HEAD_DIM * (1 - h) + 1]
            sides.append(made * (1.0 / mass))
            if lse_scr is not None:
                lse_scr[...] = jnp.where(lane == 2 * j + h, top + jnp.log(mass), lse_scr[...])
        ctx[:, pl.ds(base, PAIR)] = jnp.where(lane < HEAD_DIM, sides[0], sides[1]).astype(BF)
        return carry

    lax.fori_loop(0, HEADS // 2, pair_body, 0)


def mixing_kernel(info_ref, xq_a, xq_b, wp_a, wp_b, mine, table, normed_ref, xq, wp, ctx, sems):
    own = info_ref[0] == 0
    fetch(own, xq_a, xq_b, xq, sems.at[0])
    fetch(own, wp_a, wp_b, wp, sems.at[1])
    width = wp.shape[0]
    length = xq.shape[0]
    pick = layer_vectors(mine, table, own)
    lane = lax.broadcasted_iota(jnp.int32, (length, PAIR), 1)
    row = lax.broadcasted_iota(jnp.int32, (length, PAIR), 0)
    bias_col = jnp.where(row < info_ref[1], 0.0, BIG_NEG).astype(BF)
    landed(xq_a, xq, sems.at[0])
    attend(xq, ctx, None, width, lane, bias_col)
    landed(wp_a, wp, sems.at[1])
    n1, r1 = row_norm(xq[:, 3 * width :].astype(F32) + (nn(ctx[...], wp[...]) + pick(PROJ_B)))
    normed_ref[...] = n1 * pick(ATTN_G) + pick(ATTN_B)


def mixing_call(info, xq, wp, tables):
    length = xq[0].shape[0]
    width = wp[0].shape[0]
    return pl.pallas_call(
        mixing_kernel,
        in_specs=[SCALARS] + [FAR] * 4 + [NEAR] * 2,
        out_specs=NEAR,
        out_shape=struct((length, width), F32),
        scratch_shapes=[
            pltpu.VMEM(xq[0].shape, BF),
            pltpu.VMEM(wp[0].shape, BF),
            pltpu.VMEM((length, width), BF),
            pltpu.SemaphoreType.DMA((2,)),
        ],
        compiler_params=params_of(16),
        cost_estimate=cost(10),
        name="mixing",
    )(info, *far(*xq, *wp), *tables)


def train_kernel(
    info_ref, xq_a, xq_b, wq_a, wq_b, wp_a, wp_b, wi_a, wi_b, wo_a, wo_b, mine, table, cot_ref,
    z_ref, wp, wi, wo, ctx, lse_ref, fixed_ref, n1_ref, r1_ref, slope_ref, gf_ref, sg_ref, small_ref, keep_ref, send_ref,
    xq, lse_scr, sems,
):
    section = info_ref[0]
    own = section == 1
    fetch(own, xq_a, xq_b, xq, sems.at[0])
    width = wp.shape[0]
    length = xq.shape[0]
    ff = wi.shape[1]
    thirds = [(pl.ds(k * width, width), wo.at[pl.ds(k * width, width)]) for k in range(3)]
    for k, (cols, place) in enumerate(thirds):
        fetch(own, wq_a.at[:, cols], wq_b.at[:, cols], place, sems.at[5 + k])
    fetch(own, wp_a, wp_b, wp, sems.at[2])
    pick = layer_vectors(mine, table, own)
    lane = lax.broadcasted_iota(jnp.int32, (length, PAIR), 1)
    row = lax.broadcasted_iota(jnp.int32, (length, PAIR), 0)
    bias_col = jnp.where(row < info_ref[1], 0.0, BIG_NEG).astype(BF)
    first = jnp.where(section == 0, mine[ROW_TILE : ROW_TILE + 1, :], table[ROW_TILE + 1 : ROW_TILE + 2, :])
    many = jnp.broadcast_to(first.astype(BF), (ROW_TILE, width))
    fixed = []
    for k, shift in enumerate((pick(QUERY_B), None, pick(VALUE_B))):
        cols, place = thirds[k]
        landed(wq_a.at[:, cols], place, sems.at[5 + k])
        made = nn(many, place[...])
        fixed.append((made if shift is None else made + shift).astype(BF))
    fixed = jnp.concatenate(fixed + [many], axis=1)
    fixed_ref[...] = fixed
    landed(xq_a, xq, sems.at[0])
    fetch(own, wi_a, wi_b, wi, sems.at[3])
    fetch(own, wo_a, wo_b, wo, sems.at[4])
    copy = pltpu.make_async_copy(cot_ref.at[section], gf_ref, sems.at[1])
    copy.start()
    replace_first(xq, fixed)
    attend(xq, ctx, lse_scr, width, lane, bias_col)
    lse_ref[...] = jnp.transpose(lse_scr[...])[0:ROW_TILE, :]
    landed(wp_a, wp, sems.at[2])
    n1, r1 = row_norm(xq[:, 3 * width :].astype(F32) + (nn(ctx[...], wp[...]) + pick(PROJ_B)))
    n1_ref[...] = n1
    r1_ref[...] = r1
    normed = n1 * pick(ATTN_G) + pick(ATTN_B)
    low = normed.astype(BF)
    landed(wi_a, wi, sems.at[3])
    landed(wo_a, wo, sems.at[4])
    total = None
    for c in range(ff // CHUNK):
        cols = slice(c * CHUNK, (c + 1) * CHUNK)
        act, slope = gelu_pair(nn(low, wi[:, cols]) + pick(INNER_B, c))
        act = act.astype(BF)
        xq[:, cols] = act
        slope_ref[:, cols] = slope.astype(BF)
        term = nn(act, wo[cols, :])
        total = term if total is None else total + term
    n2, r2 = row_norm(normed + (total + pick(OUTER_B)))
    gain = pick(FFN_G)
    z_ref[...] = (n2 * gain + pick(FFN_B)).astype(BF)
    wide_row = lax.broadcasted_iota(jnp.int32, n2.shape, 0)
    copy.wait()
    grad = jnp.where(wide_row < info_ref[1], gf_ref[...].astype(F32), 0.0)
    second = norm_back(grad, n2, r2, gain)
    sg_ref[...] = second
    gf = second.astype(BF)
    gf_ref[...] = gf
    small_ref[0:1, :] = col_sum(gf)
    small_ref[1:2, :] = col_sum(grad * n2)
    small_ref[2:3, :] = col_sum(grad)
    half_chunks = ff // CHUNK // 2
    rows = send_ref.shape[1]
    each = CHUNK // rows
    for ref, half, order in ((send_ref, 1 - section, info_ref[4]), (keep_ref, section, info_ref[3])):
        for c in range(half_chunks):
            cols = pl.ds(pl.multiple_of((half * half_chunks + c) * CHUNK, CHUNK), CHUNK)
            made = tn(xq[:, cols], gf).astype(BF)
            for p in range(each):
                ref[jnp.bitwise_xor(c * each + p, order)] = made[p * rows : (p + 1) * rows, :]


def train_call(info, pairs, tables, cot):
    xq, wq, wp, wi, wo = (piece[0] for piece in pairs)
    length = xq.shape[0]
    width, ff = wi.shape
    args = [info]
    in_specs = [SCALARS]
    for pair in pairs:
        args += far(*pair)
        in_specs += [FAR, FAR]
    args += [*tables, *far(cot)]
    shapes = [
        struct((length, width), BF),
        near(wp.shape, BF),
        near(wi.shape, BF),
        near(wo.shape, BF),
        near((length, width), BF),
        near((ROW_TILE, length), F32),
        near((ROW_TILE, 4 * width), BF),
        near((length, width), F32),
        near((length, 1), F32),
        near((length, ff), BF),
        near((length, width), BF),
        near((length, width), F32),
        near((8, width), F32),
        near((GROUP, ff // 2 // GROUP, width), BF),
        near((GROUP, ff // 2 // GROUP, width), BF),
    ]
    return pl.pallas_call(
        train_kernel,
        in_specs=in_specs + [NEAR] * 2 + [FAR],
        out_specs=[NEAR] * len(shapes),
        out_shape=shapes,
        scratch_shapes=[
            pltpu.VMEM(xq.shape, BF),
            pltpu.VMEM((length, PAIR), F32),
            pltpu.SemaphoreType.DMA((8,)),
        ],
        compiler_params=params_of(14),
        cost_estimate=cost(26),
        name="layer_train",
    )(*args)


def feed_kernel(info_ref, normed_ref, wi_a, wi_b, wo_a, wo_b, mine, other, z_ref, wi, wo, sems):
    own = info_ref[0] == 0
    fetch(own, wi_a, wi_b, wi, sems.at[0])
    fetch(own, wo_a, wo_b, wo, sems.at[1])
    pick = layer_vectors(mine, other, own)
    normed = normed_ref[...]
    low = normed.astype(BF)
    landed(wi_a, wi, sems.at[0])
    landed(wo_a, wo, sems.at[1])
    total = None
    for c in range(wi.shape[1] // CHUNK):
        cols = slice(c * CHUNK, (c + 1) * CHUNK)
        act, slope = gelu_pair(nn(low, wi[:, cols]) + pick(INNER_B, c))
        term = nn(act.astype(BF), wo[cols, :])
        total = term if total is None else total + term
    n2, r2 = row_norm(normed + (total + pick(OUTER_B)))
    z_ref[...] = (n2 * pick(FFN_G) + pick(FFN_B)).astype(BF)


def feed_call(info, normed, wi, wo, tables):
    return pl.pallas_call(
        feed_kernel,
        in_specs=[SCALARS, NEAR] + [FAR] * 4 + [NEAR] * 2,
        out_specs=NEAR,
        out_shape=struct(normed.shape, BF),
        scratch_shapes=[pltpu.VMEM(wi[0].shape, BF), pltpu.VMEM(wo[0].shape, BF), pltpu.SemaphoreType.DMA((2,))],
        compiler_params=params_of(24),
        cost_estimate=cost(11),
        name="layer_feed",
    )(info, normed, *far(*wi, *wo), *tables)


def inner_kernel(
    info_ref, gf_ref, slope_ref, sg_ref, n1_ref, r1_ref, wi_ref, wo_ref, wp_ref, mine, table,
    keep_ref, send_ref, gh_ref, ga_ref, gc_ref, small_ref,
):
    section = info_ref[0]
    pick = layer_vectors(mine, table, section == 1)
    gain = pick(ATTN_G)
    low = jnp.transpose(n1_ref[...] * gain + pick(ATTN_B)).astype(BF)
    ff = wi_ref.shape[1]
    half_chunks = ff // CHUNK // 2
    gf = gf_ref[...]
    gn = sg_ref[...]
    for ref, half, order in ((send_ref, 1 - section, info_ref[6]), (keep_ref, section, info_ref[5])):
        for c in range(half_chunks):
            block = half * half_chunks + c
            cols = pl.ds(pl.multiple_of(block * CHUNK, CHUNK), CHUNK)
            gu = (nt(gf, wo_ref[cols, :]) * slope_ref[:, cols].astype(F32)).astype(BF)
            small_ref[pl.ds(3 + block, 1), :] = col_sum(gu)
            place_rows(ref.at[:, :, c * CHUNK : (c + 1) * CHUNK], nn(low, gu).astype(BF), order)
            gn = gn + nt(gu, wi_ref[:, cols])
    n1 = n1_ref[...]
    gh = norm_back(gn, n1, r1_ref[...], gain)
    gh_ref[...] = gh
    ga = gh.astype(BF)
    ga_ref[...] = ga
    gc_ref[...] = nt(ga, wp_ref[...]).astype(BF)
    small_ref[0:1, :] = col_sum(ga)
    small_ref[1:2, :] = col_sum(gn * n1)
    small_ref[2:3, :] = col_sum(gn)


def inner_call(info, gf, slope, sg, n1, r1, wi, wo, wp, tables):
    tokens, width = gf.shape
    ff = wi.shape[1]
    shapes = [
        near((GROUP, width // GROUP, ff // 2), BF),
        near((GROUP, width // GROUP, ff // 2), BF),
        near((tokens, width), F32),
        near((tokens, width), BF),
        near((tokens, width), BF),
        near((8, width), F32),
    ]
    return pl.pallas_call(
        inner_kernel,
        in_specs=[SCALARS] + [NEAR] * 10,
        out_specs=[NEAR] * len(shapes),
        out_shape=shapes,
        compiler_params=params_of(12),
        cost_estimate=cost(10),
        name="inner_grad",
    )(info, *stay(gf, slope, sg, n1, r1, wi, wo, wp), *tables)


def attention_kernel(
    info_ref, xq_a, xq_b, fixed_ref, gc_ref, ga_ref, c_ref, lse_ref, keep_ref, send_ref, g_ref, small_ref,
    xq, xt_scr, ct_scr, mean_scr, sem,
):
    section = info_ref[0]
    fetch(section == 1, xq_a, xq_b, xq, sem)
    length, width = gc_ref.shape
    row = lax.broadcasted_iota(jnp.int32, (length, PAIR), 0)
    lane = lax.broadcasted_iota(jnp.int32, (length, PAIR), 1)
    bias_col = jnp.where(row < info_ref[1], 0.0, BIG_NEG).astype(BF)
    ct_scr[...] = turned(c_ref[...])
    product = gc_ref[...].astype(F32) * c_ref[...].astype(F32)
    high = product.astype(BF)
    low = (product - high.astype(F32)).astype(BF)
    ones = by_head(jnp.ones((1, width), BF), ROW_TILE)
    mean_scr[...] = nt(ones, high) + nt(ones, low)
    landed(xq_a, xq, sem)
    replace_first(xq, fixed_ref[...])
    xt_scr[...] = turned(xq[:, 3 * width :])

    def pair_body(j, carry):
        base, q, k, v, parts = attention_parts(xq, j, width, lane, bias_col)
        kt = turned(k)
        gc = gc_ref[:, pl.ds(base, PAIR)]
        zero = jnp.zeros_like(gc)
        strips = [slice(0, length)]
        gk = [None] * len(strips)
        gv = [None] * len(strips)
        gqt = []
        for h, (mine, qh, kh) in enumerate(parts):
            gch = jnp.where(mine, gc, zero)
            qz = jnp.where(mine, q, zero)
            lse = lse_ref[pl.ds(2 * j + h, 1), :]
            mean = mean_scr[pl.ds(2 * j + h, 1), :]
            gq_h = None
            for s, rows in enumerate(strips):
                probs = jnp.exp(nt(kh[rows, :], qh) - lse)
                gs = (probs * (nt(v[rows, :], gch) - mean)).astype(BF)
                gv_h = nn(probs.astype(BF), gch)
                gk_h = nn(gs, qz)
                term = nn(kt[HEAD_DIM * h : HEAD_DIM * (h + 1), rows], gs)
                gq_h = term if gq_h is None else gq_h + term
                gk[s] = gk_h if h == 0 else gk[s] + gk_h
                gv[s] = gv_h if h == 0 else gv[s] + gv_h
            gqt.append(gq_h)
        gq = jnp.transpose(jnp.concatenate(gqt, axis=0)) * 0.125
        g_ref[:, pl.ds(base, PAIR)] = gq.astype(BF)
        for s, rows in enumerate(strips):
            g_ref[rows, pl.ds(base + width, PAIR)] = gk[s].astype(BF)
            g_ref[rows, pl.ds(base + 2 * width, PAIR)] = gv[s].astype(BF)
        return carry

    lax.fori_loop(0, HEADS // 2, pair_body, 0)
    small_ref[0:1, :] = col_sum(g_ref[:, 0:width])
    small_ref[1:2, :] = col_sum(g_ref[:, 2 * width : 3 * width])
    wide = 3 * width // 2
    for ref, half, order in ((send_ref, 1 - section, info_ref[8]), (keep_ref, section, info_ref[7])):
        cols = pl.ds(pl.multiple_of(half * wide, PAIR), wide)
        place_rows(ref.at[:, :, 0:wide], nn(xt_scr[...], g_ref[:, cols]).astype(BF), order)
        cols = pl.ds(pl.multiple_of(half * (width // 2), PAIR), width // 2)
        place_rows(ref.at[:, :, wide:], nn(ct_scr[...], ga_ref[:, cols]).astype(BF), order)


def attention_call(info, xq, fixed, gc, ga, context, lse):
    length, width = gc.shape
    shapes = [
        near((GROUP, width // GROUP, 2 * width), BF),
        near((GROUP, width // GROUP, 2 * width), BF),
        near((length, 3 * width), BF),
        near((8, width), F32),
    ]
    return pl.pallas_call(
        attention_kernel,
        in_specs=[SCALARS, FAR, FAR] + [NEAR] * 5,
        out_specs=[NEAR] * len(shapes),
        out_shape=shapes,
        scratch_shapes=[
            pltpu.VMEM(xq[0].shape, BF),
            pltpu.VMEM((width, length), BF),
            pltpu.VMEM((width, length), BF),
            pltpu.VMEM((ROW_TILE, length), F32),
            pltpu.SemaphoreType.DMA(()),
        ],
        compiler_params=params_of(18),
        cost_estimate=cost(14),
        name="attention_grad",
    )(info, *far(*xq), *stay(fixed, gc, ga, context, lse))


def input_kernel(info_ref, w_a, w_b, g_ref, gh_ref, small1_ref, small2_ref, small3_ref, o_ref, small_ref, w, sem):
    fetch(info_ref[0] == 1, w_a, w_b, w, sem)
    landed(w_a, w, sem)
    made = gh_ref[...] + nt(g_ref[...], w[...])
    o_ref[...] = made
    small_ref[0:2, :] = small3_ref[0:2, :]
    small_ref[2:9, :] = small2_ref[0:7, :]
    small_ref[9:12, :] = small1_ref[0:3, :]
    small_ref[12:16, :] = made[0:4, :]


def input_call(info, g, gh, w, small1, small2, small3):
    return pl.pallas_call(
        input_kernel,
        in_specs=[SCALARS, FAR, FAR] + [NEAR] * 5,
        out_specs=[NEAR] * 2,
        out_shape=[struct(gh.shape, F32), struct((ROW_TILE, gh.shape[1]), F32)],
        scratch_shapes=[pltpu.VMEM(w[0].shape, BF), pltpu.SemaphoreType.DMA(())],
        compiler_params=params_of(12),
        cost_estimate=cost(4),
        name="input_grad",
    )(info, *far(*w), *stay(g, gh, small1, small2, small3))


def head_back_kernel(
    info_ref, small_a, small_b, kept_ref, own_ref, other_ref,
    wq_ref, wp_ref, wi_ref, wo_ref, table, x_ref, first_ref, second_ref, wq, wp, wi, wo, sems,
):
    copies = [
        pltpu.make_async_copy(ref, scr, sems.at[i])
        for i, (ref, scr) in enumerate(((wo_ref, wo), (wi_ref, wi), (wp_ref, wp), (wq_ref, wq)))
    ]
    for copy in copies:
        copy.start()
    width = wp.shape[0]
    length = own_ref.shape[0]
    ff = wi.shape[1]
    places = kept_places(width, ff, length)

    def kept(name, offset=0, size=None):
        start = places[name][0] + offset
        return kept_ref[:, start : start + (places[name][1] if size is None else size)]

    n1, n2 = kept("n1"), kept("n2")
    context = kept("context").astype(BF)
    pick = layer_vectors(table, table, info_ref[0] == 0)
    grad = two_rows(small_a[12:13, :], small_b[12:13, :]).astype(BF).astype(F32)
    second = norm_back(grad, n2, kept("r2", 0, 1), pick(FFN_G))
    gf = second.astype(BF)
    copies[0].wait()
    gu = (nt(gf, wo[...]) * kept("slope")).astype(BF)
    copies[1].wait()
    gn = second + nt(gu, wi[...])
    gh = norm_back(gn, n1, kept("r1", 0, 1), pick(ATTN_G))
    ga = gh.astype(BF)
    copies[2].wait()
    gc = nt(ga, wp[...]).astype(BF)
    normed = (n1 * pick(ATTN_G) + pick(ATTN_B)).astype(BF)
    copies[3].wait()
    query_bias = value_bias = jnp.zeros((1, width), F32)
    heads, rest = {}, {}
    for i, ref in enumerate((own_ref, other_ref)):
        mid = (1 - 2 * i) * info_ref[0] + i
        keys, values, inputs = ref[:, width : 2 * width], ref[:, 2 * width : 3 * width], ref[:, 3 * width :]
        query = ref[0:1, 0:width] * jnp.asarray(0.125, BF)
        gc_row = gc[i : i + 1, :]
        query_heads, gc_heads = by_head(query, ROW_TILE), by_head(gc_row, ROW_TILE)
        probs = kept("probs", i * length, length)
        gp = nt(gc_heads, values)
        gs = (probs * (gp - jnp.sum(probs * gp, axis=-1, keepdims=True))).astype(BF)
        low = probs.astype(BF)
        gq = (heads_of(nn(gs, keys)) * 0.125).astype(BF)
        for place, value in ((KEY_SUMS, nn(gs, inputs)), (VALUE_SUMS, nn(low, inputs))):
            for h in range(HEADS):
                heads[place + HEADS * i + h] = value[h : h + 1, :]
        key_back = nt(query_heads, wq[:, width : 2 * width]).astype(BF)
        value_back = nt(gc_heads, wq[:, 2 * width :]).astype(BF)
        gx = tn(gs, key_back) + tn(low, value_back)
        top = gh[i : i + 1, :] + nt(jnp.broadcast_to(gq, (ROW_TILE, width)), wq[:, 0:width])[0:1, :]
        at_first = lax.broadcasted_iota(jnp.int32, gx.shape, 0) == 0
        x_ref[mid] = gx + jnp.where(at_first, top, 0.0)
        query_bias = query_bias + gq.astype(F32)
        mass = jnp.sum(low.astype(F32), axis=-1, keepdims=True)
        value_bias = value_bias + heads_of(gc_heads.astype(F32) * mass)
        heads[QUERIES + i] = query
        heads[GCONTEXTS + i] = gc_row
        for place, value in ((OUTERS, gf), (NORMEDS, normed), (CONTEXTS, context), (PROJS, ga)):
            rest[place + i] = value[i : i + 1, :]
        rest[INPUTS + i] = ref[0:1, 3 * width :]
        rest[GQUERIES + i] = gq
    gu_sum = col_sum(gu)
    act = kept("acts").astype(BF)
    own_small = [query_bias, value_bias, col_sum(ga), col_sum(gn * n1), col_sum(gn)]
    own_small += [gu_sum[:, width * k : width * (k + 1)] for k in range(ff // width)]
    own_small += [col_sum(gf), col_sum(grad * n2), col_sum(grad)]

    for k in range(ff // width):
        for i in range(2):
            rest[ACTS + 4 * i + k] = act[i : i + 1, width * k : width * (k + 1)]
            rest[INNERS + 4 * i + k] = gu[i : i + 1, width * k : width * (k + 1)]
    row = lax.broadcasted_iota(jnp.int32, (8, width), 0)
    for ref, rows in ((first_ref, heads), (second_ref, rest)):
        for k, piece in enumerate(own_small):
            rows[SUMS + k] = jnp.where(info_ref[0] == 0, piece, small_a[k : k + 1, :] + small_b[k : k + 1, :])
        for start in range(0, FACTORS, 8):
            made = jnp.zeros((8, width), F32)
            for k in range(8):
                if start + k in rows:
                    made = jnp.where(row == k, rows[start + k].astype(F32), made)
            ref[start : start + 8, :] = made.astype(BF)


def head_back_call(info, small_a, small_b, kept, own, other, wq, wp, wi, wo, table):
    length = own.shape[0]
    width, ff = wi.shape
    args = [small_a, small_b, kept, own, other]
    return pl.pallas_call(
        head_back_kernel,
        in_specs=[SCALARS] + [NEAR] * len(args) + [FAR] * 4 + [NEAR],
        out_specs=[NEAR] * 3,
        out_shape=[struct((2, length, width), F32)] + [struct((FACTORS, width), BF)] * 2,
        scratch_shapes=[pltpu.VMEM(w.shape, BF) for w in (wq, wp, wi, wo)] + [pltpu.SemaphoreType.DMA((4,))],
        compiler_params=params_of(28),
        cost_estimate=cost(12),
        name="head_rows_grad",
    )(info, *args, *far(wq, wp, wi, wo), table)


def piece_at(low, high, place, cols=slice(None)):
    half = low.shape[0]
    inside = lax.rem(place, half)
    return jnp.where(place < half, low[inside, :, cols], high[inside, :, cols])


def feed_final_kernel(outer, info_ref, a_low, a_high, b_low, b_high, rest_ref, o_ref, buffers, sems):
    width = buffers.shape[1]
    rows = a_low.shape[1]
    first = 4 if outer else 6
    halves = ((a_low, a_high, info_ref[first]), (b_low, b_high, info_ref[first - 1]))

    def products(left, right):
        return sum(tn(rest_ref[left[0] + j * left[1]], rest_ref[right[0] + j * right[1]]) for j in range(2))

    copies = []
    for k in range(4):
        slot = k % 2
        if k >= 2:
            copies[k - 2].wait()

        @pl.when(info_ref[0] == 1)
        def _():
            low, high, order = halves[k // 2]
            for p in range(width // rows):
                if outer:
                    piece = piece_at(low, high, jnp.bitwise_xor((k % 2) * (width // rows) + p, order))
                else:
                    cols = slice((k % 2) * width, (k % 2 + 1) * width)
                    piece = piece_at(low, high, jnp.bitwise_xor(p, order), cols)
                buffers[slot, p * rows : (p + 1) * rows, :] = piece.astype(F32)

        @pl.when(info_ref[0] == 0)
        def _():
            left, right = ((ACTS + k, 4), (OUTERS, 1)) if outer else ((NORMEDS, 1), (INNERS + k, 4))
            buffers[slot] = products(left, right)

        block = slice(k * width, (k + 1) * width)
        target = o_ref.at[block, :] if outer else o_ref.at[:, block]
        copies.append(pltpu.make_async_copy(buffers.at[slot], target, sems.at[slot]))
        copies[-1].start()
    copies[-2].wait()
    copies[-1].wait()


def feed_final_call(outer, info, quarters, rest):
    width = rest.shape[2]
    ff = 4 * width
    return pl.pallas_call(
        lambda *refs: feed_final_kernel(outer, *refs),
        in_specs=[SCALARS] + [NEAR] * 5,
        out_specs=FAR,
        out_shape=struct((ff, width) if outer else (width, ff), F32),
        scratch_shapes=[pltpu.VMEM((2, width, width), F32), pltpu.SemaphoreType.DMA((2,))],
        compiler_params=params_of(10),
        cost_estimate=cost(4),
        name="outer_final" if outer else "inner_final",
    )(info, *quarters, rest)


def qkv_final_kernel(info_ref, a_low, a_high, b_low, b_high, heads_ref, rest_ref, o_ref, p_ref, made, made_p, sems):
    width = p_ref.shape[0]
    wide = 3 * width // 2
    half = width // 2
    rows = a_low.shape[1]

    @pl.when(info_ref[0] == 1)
    def _():
        copies = []
        for k, (low, high, order) in enumerate(((a_low, a_high, info_ref[8]), (b_low, b_high, info_ref[7]))):
            for p in range(GROUP):
                place = jnp.bitwise_xor(p, order)
                at = slice(p * rows, (p + 1) * rows)
                made[at, k * wide : (k + 1) * wide] = piece_at(low, high, place, slice(0, wide)).astype(F32)
                piece = piece_at(low, high, place, slice(wide, wide + half))
                made_p[at, k * half : (k + 1) * half] = piece.astype(F32)
            cols = slice(k * wide, (k + 1) * wide)
            copies.append(pltpu.make_async_copy(made.at[:, cols], o_ref.at[:, cols], sems.at[k]))
            copies[-1].start()
        copies.append(pltpu.make_async_copy(made_p, p_ref, sems.at[2]))
        copies[-1].start()
        for copy in copies:
            copy.wait()

    @pl.when(info_ref[0] == 0)
    def _():
        def pairs(left, right):
            return tn(rest_ref[left], rest_ref[right]) + tn(rest_ref[left + 1], rest_ref[right + 1])

        made_p[...] = pairs(CONTEXTS, PROJS)
        copies = [pltpu.make_async_copy(made_p, p_ref, sems.at[3])]
        copies[-1].start()
        chips = heads_ref.shape[1]
        lane = lax.broadcasted_iota(jnp.int32, (chips, width), 1)
        for place, base, key in ((0, 0, 0), (1, KEY_SUMS, QUERIES), (2, VALUE_SUMS, GCONTEXTS)):
            cols = slice(place * width, (place + 1) * width)
            if place == 0:
                made[:, cols] = pairs(INPUTS, GQUERIES)
            else:
                term = None
                for j in range(2):
                    left = heads_ref[base + HEADS * j : base + HEADS * j + HEADS].reshape(HEADS * chips, width)
                    row = heads_ref[key + j]
                    heads = [
                        jnp.where((lane >= HEAD_DIM * h) & (lane < HEAD_DIM * (h + 1)), row, jnp.zeros_like(row))
                        for h in range(HEADS)
                    ]
                    one = tn(left, jnp.concatenate(heads, axis=0))
                    term = one if term is None else term + one
                made[:, cols] = term
            copies.append(pltpu.make_async_copy(made.at[:, cols], o_ref.at[:, cols], sems.at[4 + place]))
            copies[-1].start()
        for copy in copies:
            copy.wait()


def qkv_final_call(info, quarters, heads, rest):
    width = rest.shape[2]
    return pl.pallas_call(
        qkv_final_kernel,
        in_specs=[SCALARS] + [NEAR] * 6,
        out_specs=[FAR, FAR],
        out_shape=[struct((width, 3 * width), F32), struct((width, width), F32)],
        scratch_shapes=[
            pltpu.VMEM((width, 3 * width), F32),
            pltpu.VMEM((width, width), F32),
            pltpu.SemaphoreType.DMA((7,)),
        ],
        compiler_params=params_of(16),
        cost_estimate=cost(4),
        name="qkv_final",
    )(info, *quarters, heads, rest)


def swap(value):
    return lax.ppermute(value, "section", SWAP)


def add_low(left, right):
    return (left.astype(F32) + right.astype(F32)).astype(BF)


def hop(value, stage, orders):
    chips = lax.axis_size("dp")
    pairs = [
        (section * chips + chip, section * chips + (chip ^ orders[section][stage]))
        for section in range(2)
        for chip in range(chips)
    ]
    return lax.ppermute(value, ("section", "dp"), pairs)


def after(value, *others):
    return lax.optimization_barrier((value,) + others)[0]


def beside(made, *sums):
    tied = lax.optimization_barrier(tuple(made) + tuple(one.coming for one in sums))
    for one, coming in zip(sums, tied[len(made) :]):
        one.coming = coming
    return tied[: len(made)]


class Sum:
    def __init__(self, keep, send, group):
        self.low, self.coming, self.orders = keep, swap(send), ORDERS[group]

    def add(self):
        half = self.coming.shape[0] // 2
        if half == 0:
            self.part = add_low(self.low, self.coming)
            return
        self.high = add_low(self.low[half:], self.coming[half:])
        self.low = self.part = add_low(self.low[:half], self.coming[:half])

    def halve(self, stage):
        self.coming = hop(self.high, stage, self.orders)

    def across(self):
        chips = lax.axis_size("dp")
        if chips > GROUP:
            groups = [[low + GROUP * high for high in range(chips // GROUP)] for low in range(GROUP)]
            self.part = lax.psum(self.part, "dp", axis_index_groups=groups)

    def double(self, stage):
        self.coming = hop(self.part, stage, self.orders)

    def join(self):
        self.part = jnp.concatenate([self.part, self.coming], axis=0)

    def quarters(self, line):
        return (swap(line(self.part)), swap(line(self.coming)), self.part, self.coming)


class Line:
    def __init__(self):
        self.token = None

    def __call__(self, value):
        return value if self.token is None else after(value, self.token)

    def run(self, work, *args):
        made = work(*args)
        tied = lax.optimization_barrier(tuple(made))
        self.token = tied[0]
        return tied

    def take(self, group):
        group.coming = self(group.coming)
        self.token = group.coming

    def halve(self, group, stage):
        self.take(group)
        group.add()
        group.halve(stage)
        self.token = group.part

    def double(self, group, stage):
        self.take(group)
        group.add()
        group.across()
        group.double(stage)
        self.token = group.part

    def join(self, group, stage):
        self.take(group)
        group.join()
        if stage is not None:
            group.double(stage)
        self.token = group.part


class Gather:
    ORDERS = ((8, 4, 2, 1), (4, 8, 1, 2))

    def __init__(self, value):
        self.part = value[None]

    def double(self, stage):
        self.coming = hop(self.part, stage, self.ORDERS)

    def join(self):
        self.part = lax.optimization_barrier(jnp.concatenate([self.part, self.coming], axis=0))

    def across(self):
        chips = lax.axis_size("dp")
        if chips > GROUP:
            groups = [[low + GROUP * high for high in range(chips // GROUP)] for low in range(GROUP)]
            every = lax.all_gather(self.part, "dp", axis_index_groups=groups)
            self.part = every.reshape((-1,) + self.part.shape[1:])


def order_of(chip, orders):
    place = jnp.int32(0)
    for stage in range(4):
        bit = (chip // orders[stage]) % 2
        place = place + bit * (8 >> stage)
    return place


def local(embeddings, cotangent, lengths, *weights):
    (wq, query_bias, value_bias, wp, proj_bias, attn_gain, attn_bias, wi, inner_bias, wo, outer_bias, ffn_gain, ffn_bias) = (
        piece[0] for piece in weights
    )
    section = lax.axis_index("section")
    chip = lax.axis_index("dp")
    first_section = section == 0
    inputs = embeddings[0]
    width = inputs.shape[2]
    scalars = [section, jnp.where(first_section, lengths[0], lengths[1]), jnp.where(first_section, lengths[1], lengths[0])]
    for orders in ORDERS:
        places = [order_of(chip, order) for order in orders]
        scalars += [jnp.where(first_section, places[0], places[1]), jnp.where(first_section, places[1], places[0])]
    info = jnp.stack(scalars).astype(jnp.int32)
    vectors = [weights[k] for k in (1, 2, 4, 5, 6, 8, 10, 11, 12)]
    own, other, own_table = qkv_call(info, inputs, wq, vectors)
    wq_pair = (wq, swap(wq))
    wp_pair = (wp, swap(wp))
    xq_pair = (own, swap(other))
    wi_pair = (wi, swap(wi))
    wo_pair = (wo, swap(wo))
    head = head_call(info, own, other, wp, wi, wo, own_table)
    tables = (head[0], swap(head[0]))
    pairs = (xq_pair, wq_pair, wp_pair, wi_pair, wo_pair)
    (z, wp_d, wi_d, wo_d, context, lse, fixed, n1, r1, slope, gf, sg, small1, outer_keep, outer_send) = train_call(
        info, pairs, tables, cotangent
    )
    g1 = Sum(outer_keep, outer_send, 0)

    made = inner_call(info, gf, slope, sg, n1, r1, wi_d, wo_d, wp_d, tables)
    inner_keep, inner_send, gh, ga, gc, small2 = beside(made, g1)
    g1.add()
    g1.halve(0)
    g2 = Sum(inner_keep, inner_send, 1)

    made = attention_call(info, xq_pair, fixed, after(gc, g1.part), ga, context, lse)
    qkv_keep, qkv_send, g_qkv, small3 = beside(made, g1)
    line = Line()
    line.halve(g2, 0)
    line.halve(g1, 1)
    g3 = Sum(qkv_keep, line(qkv_send), 2)
    gx, dsmall = line.run(input_call, info, line(g_qkv), gh, wq_pair, small1, small2, small3)
    dsmall_other = swap(line(dsmall))
    line.halve(g3, 0)
    encoder_gx, heads, rest = line.run(
        head_back_call, info, dsmall, line(dsmall_other), head[1], own, other, wq, wp, wi, wo, own_table
    )
    came = swap(line(rest))
    gx_other = swap(line(gx))
    line.halve(g1, 2)
    (normed,) = line.run(lambda *a: (mixing_call(*a),), info, xq_pair, wp_pair, (tables[0], line(tables[1])))
    line.halve(g2, 1)
    line.halve(g3, 1)
    shared = jnp.where(first_section, heads, jnp.concatenate([line(came)[:SUMS], heads[SUMS:]]))
    factors = Gather(shared)
    factors.double(0)
    line.token = factors.part
    line.halve(g1, 3)
    line.halve(g2, 2)
    line.join(factors, 1)
    line.halve(g3, 2)
    line.double(g1, 3)
    line.join(factors, 2)
    line.halve(g2, 3)
    line.halve(g3, 3)
    line.join(g1, 2)
    line.double(g2, 3)
    line.join(factors, 3)
    line.double(g3, 3)
    line.join(g2, 2)
    line.join(g1, 1)
    line.join(g3, 2)
    line.join(g2, 1)
    line.join(g1, 0)
    line.join(g3, 1)
    line.join(g2, 0)
    line.join(factors, None)
    line.join(g3, 0)
    factors.across()
    sums = jnp.sum(line(factors.part)[:, SUMS:].astype(F32), axis=0)
    heads_all = jnp.transpose(factors.part, (1, 0, 2))
    heads_all, sums = line.run(lambda *a: a, heads_all, sums)
    (e_low,) = line.run(lambda *a: (feed_call(*a),), info, line(normed), wi_pair, wo_pair, tables)
    decoder_gx = jnp.stack([line(gx_other), gx])
    later = jnp.arange(gx.shape[0])[None, :, None] > 0
    (embed_grads,) = line.run(lambda a: (jnp.where(first_section, encoder_gx, jnp.where(later, a, 0.0)),), decoder_gx)
    line.take(g1)
    line.take(g2)
    rest_all = swap(line(heads_all)[:SUMS])
    z_other = swap(line(jnp.where(first_section, z, e_low)))
    z_mine = jnp.where(first_section, e_low, z)
    outer_quarters = g1.quarters(line)
    inner_quarters = g2.quarters(line)
    outputs = jnp.where(first_section, jnp.stack([z_mine, line(z_other)]), jnp.stack([z_other, z_mine]))
    (outputs,) = line.run(lambda a: (a,), outputs)
    (outer_grad,) = line.run(lambda *a: (feed_final_call(True, *a),), info, outer_quarters, line(rest_all))
    line.take(g3)
    qkv_quarters = g3.quarters(line)
    (inner_grad,) = line.run(lambda *a: (feed_final_call(False, *a),), info, inner_quarters, line(rest_all))
    qkv_grad, proj_grad = line.run(qkv_final_call, info, qkv_quarters, heads_all, line(rest_all))
    results = (
        outputs,
        embed_grads,
        qkv_grad,
        sums[0],
        sums[1],
        proj_grad,
        sums[2],
        sums[3],
        sums[4],
        inner_grad,
        sums[5:9].reshape(-1),
        outer_grad,
        sums[9],
        sums[10],
        sums[11],
    )
    return tuple(piece[None] for piece in results)


def solution(mesh):
    matrix = P("section", None, None)
    vector = P("section", None)
    return jax.shard_map(
        local,
        mesh=mesh,
        in_specs=(P("section", "dp", None, None), P("dp", None, None), P("dp"))
        + (matrix, vector, vector, matrix, vector, vector, vector)
        + (matrix, vector, matrix, vector, vector, vector),
        out_specs=(P("section", "dp", None, None), P("section", "dp", None, None))
        + (matrix, vector, vector, matrix, vector, vector, vector)
        + (matrix, vector, matrix, vector, vector, vector),
        check_vma=False,
    )
```

```python
import math

import jax
import jax.numpy as jnp
from jax import lax
from jax.experimental import pallas as pl
from jax.experimental.pallas import tpu as pltpu
from jax.sharding import PartitionSpec as P

HEADS = 12
HEAD_DIM = 64
PAIR = 2 * HEAD_DIM
EPSILON = 1e-06
BIG_NEG = -1e30
BF = jnp.bfloat16
F32 = jnp.float32
CHUNK = 768
GROUP = 16
ROW_TILE = 16
ORDERS = (
    ((2, 1, 8, 4), (1, 4, 2, 8)),
    ((8, 1, 2, 4), (2, 4, 8, 1)),
    ((1, 2, 4, 8), (2, 1, 8, 4)),
)
SWAP = ((0, 1), (1, 0))
KEY_SUMS, VALUE_SUMS, QUERIES, GCONTEXTS = 0, 24, 48, 50
OUTERS, NORMEDS, CONTEXTS, PROJS, INPUTS, GQUERIES, ACTS, INNERS = 0, 2, 4, 6, 8, 10, 12, 20
SUMS, FACTORS = 52, 64


def params_of(mebibytes):
    return pltpu.CompilerParams(vmem_limit_bytes=mebibytes * 1024 * 1024)


def cost(micros):
    return pl.CostEstimate(flops=int(micros * 0.11e9), bytes_accessed=int(micros * 0.2e6), transcendentals=0)


def nn(left, right):
    return lax.dot_general(left, right, (((1,), (0,)), ((), ())), preferred_element_type=F32)


def nt(left, right):
    return lax.dot_general(left, right, (((1,), (1,)), ((), ())), preferred_element_type=F32)


def tn(left, right):
    return lax.dot_general(left, right, (((0,), (0,)), ((), ())), preferred_element_type=F32)


def turned(value):
    return jnp.transpose(value.astype(BF))


def col_sum(value):
    return jnp.sum(value.astype(F32), axis=0, keepdims=True)


def row_norm(hidden):
    centred = hidden - jnp.mean(hidden, axis=-1, keepdims=True)
    scale = lax.rsqrt(jnp.mean(centred * centred, axis=-1, keepdims=True) + EPSILON)
    return (centred * scale, scale)


def norm_back(grad, normal, scale, gain):
    scaled = grad * gain
    return scale * (
        scaled
        - jnp.mean(scaled, axis=-1, keepdims=True)
        - normal * jnp.mean(scaled * normal, axis=-1, keepdims=True)
    )


def gelu_pair(value):
    bell = jnp.exp(-0.5 * (value * value))
    t = 1.0 / (1.0 + (0.3275911 / math.sqrt(2.0)) * jnp.abs(value))
    series = 0.5307027145 * t - 0.7265760135
    series = series * t + 0.7107068705
    series = series * t - 0.142248368
    series = series * t + 0.127414796
    tail = (series * t) * bell
    mass = jnp.where(value >= 0.0, 1.0 - tail, tail)
    return (value * mass, mass + value * (bell * (1.0 / math.sqrt(2.0 * math.pi))))


def fetch(first, own, other, target, sem):
    @pl.when(first)
    def _():
        pltpu.make_async_copy(own, target, sem).start()

    @pl.when(jnp.logical_not(first))
    def _():
        pltpu.make_async_copy(other, target, sem).start()


def landed(own, target, sem):
    pltpu.make_async_copy(own, target, sem).wait()


FAR = pl.BlockSpec(memory_space=pltpu.HBM)
ANYWHERE = pl.BlockSpec(memory_space=pl.ANY)
SCALARS = pl.BlockSpec(memory_space=pltpu.SMEM)
NEAR = pl.BlockSpec(memory_space=pltpu.VMEM)


def struct(shape, kind):
    return jax.ShapeDtypeStruct(tuple(shape), kind)


def near(shape, kind):
    return pltpu.VMEM(tuple(shape), kind)


def full(shape):
    return pl.BlockSpec(tuple(shape), lambda *_: (0,) * len(shape))


def far(*values):
    return tuple(pltpu.with_memory_space_constraint(value, pltpu.HBM) for value in values)


def stay(*values):
    return tuple(pltpu.with_memory_space_constraint(value, pltpu.VMEM) for value in values)


QUERY_B, VALUE_B, PROJ_B, ATTN_G, ATTN_B, INNER_B, OUTER_B, FFN_G, FFN_B = range(9)
TABLE_ROWS = (0, 1, 2, 3, 4, 5, 9, 10, 11)


def layer_vectors(mine, other, own):
    def pick(k, part=0):
        row = TABLE_ROWS[k] + part
        return jnp.where(own, mine[row : row + 1, :], other[row : row + 1, :])

    return pick


def qkv_kernel(info_ref, x_ref, w_ref, *refs):
    vectors = refs[:9]
    qb_ref, vb_ref = vectors[QUERY_B], vectors[VALUE_B]
    own_ref, other_ref, table_ref = refs[9:]
    step = pl.program_id(0)
    half = pl.num_programs(0) // 2
    width = x_ref.shape[2]
    x = x_ref[0]

    def put(ref):
        for k, shift in enumerate((qb_ref[...], None, vb_ref[...])):
            made = nn(x, w_ref[:, k * width : (k + 1) * width])
            ref[:, k * width : (k + 1) * width] = (made if shift is None else made + shift).astype(BF)
        ref[:, 3 * width :] = x

    pl.when(step < half)(lambda: put(other_ref))
    pl.when(step >= half)(lambda: put(own_ref))

    @pl.when(step == 0)
    def _():
        for ref, row in zip(vectors, TABLE_ROWS):
            for part in range(ref.shape[1] // width):
                table_ref[row + part : row + part + 1, :] = ref[:, part * width : (part + 1) * width]


def qkv_call(info, inputs, weight, vectors, rows=256):
    count, length, width = inputs.shape
    wide = weight.shape[1] + width
    half = length // rows
    return pl.pallas_call(
        qkv_kernel,
        grid_spec=pltpu.PrefetchScalarGridSpec(
            num_scalar_prefetch=1,
            grid=(2 * half,),
            in_specs=[
                pl.BlockSpec(
                    (1, rows, width),
                    lambda i, info: (jnp.where(i < half, 1 - info[0], info[0]), lax.rem(i, half), 0),
                ),
                pl.BlockSpec(weight.shape, lambda i, info: (0, 0), pipeline_mode=pl.Buffered(1)),
            ]
            + [full(v.shape) for v in vectors],
            out_specs=[
                pl.BlockSpec((rows, wide), lambda i, info: (jnp.maximum(i - half, 0), 0)),
                pl.BlockSpec((rows, wide), lambda i, info: (jnp.minimum(i, half - 1), 0)),
                full((ROW_TILE, width)),
            ],
        ),
        out_shape=[struct((length, wide), BF)] * 2 + [struct((ROW_TILE, width), F32)],
        compiler_params=params_of(20),
        cost_estimate=cost(6),
        name="qkv",
    )(info, *far(inputs, weight, *vectors))


def by_head(value, rows):
    width = value.shape[1]
    lane = lax.broadcasted_iota(jnp.int32, (rows, width), 1)
    row = lax.broadcasted_iota(jnp.int32, (rows, width), 0)
    return jnp.where((lane >= row * HEAD_DIM) & (lane < (row + 1) * HEAD_DIM), value, jnp.zeros((), value.dtype))


def heads_of(value):
    rows, width = value.shape
    lane = lax.broadcasted_iota(jnp.int32, (rows, width), 1)
    row = lax.broadcasted_iota(jnp.int32, (rows, width), 0)
    kept = jnp.where((lane >= row * HEAD_DIM) & (lane < (row + 1) * HEAD_DIM), value, 0.0)
    return jnp.sum(kept, axis=0, keepdims=True)


def two_rows(first, second):
    rows = lax.broadcasted_iota(jnp.int32, (ROW_TILE, first.shape[1]), 0)
    zero = jnp.zeros((), first.dtype)
    return jnp.where(rows == 0, first, jnp.where(rows == 1, second, zero))


def kept_places(width, ff, length):
    sizes = (("n1", width), ("n2", width), ("context", width), ("acts", ff), ("slope", ff), ("probs", 2 * length))
    places, start = {}, 0
    for name, size in sizes + (("r1", PAIR), ("r2", PAIR)):
        places[name] = (start, size)
        start += size
    return places


def head_kernel(
    info_ref, own_ref, other_ref, wp_ref, wi_ref, wo_ref, table,
    e_ref, kept_ref, acts, wp, wi, wo, sems,
):
    copies = [
        pltpu.make_async_copy(wp_ref, wp, sems.at[0]),
        pltpu.make_async_copy(wi_ref, wi, sems.at[1]),
        pltpu.make_async_copy(wo_ref, wo, sems.at[2]),
    ]
    for copy in copies:
        copy.start()
    pick = layer_vectors(table, table, info_ref[0] == 0)
    width, ff = wi.shape
    length = own_ref.shape[0]
    places = kept_places(width, ff, length)

    def put(name, value, offset=0):
        start = places[name][0] + offset
        kept_ref[:, start : start + value.shape[1]] = value.astype(F32)

    lane = lax.broadcasted_iota(jnp.int32, (ROW_TILE, length), 1)
    contexts = []
    for i, ref in enumerate((own_ref, other_ref)):
        query = by_head(ref[0:1, 0:width] * jnp.asarray(0.125, BF), ROW_TILE)
        scores = nt(query, ref[:, width : 2 * width])
        scores = jnp.where(lane < info_ref[1 + i], scores, BIG_NEG)
        raised = jnp.exp(scores - jnp.max(scores, axis=-1, keepdims=True))
        probs = raised / jnp.sum(raised, axis=-1, keepdims=True)
        put("probs", probs, i * length)
        contexts.append(heads_of(nn(probs.astype(BF), ref[:, 2 * width : 3 * width])))
    context = two_rows(*contexts).astype(BF)
    put("context", context)
    inputs = two_rows(own_ref[0:1, 3 * width :], other_ref[0:1, 3 * width :])
    copies[0].wait()
    n1, r1 = row_norm(inputs.astype(F32) + (nn(context, wp[...]) + pick(PROJ_B)))
    put("n1", n1)
    put("r1", r1)
    normed = n1 * pick(ATTN_G) + pick(ATTN_B)
    copies[1].wait()
    low = normed.astype(BF)
    for c in range(ff // width):
        cols = slice(c * width, (c + 1) * width)
        act, slope = gelu_pair(nn(low, wi[:, cols]) + pick(INNER_B, c))
        act = act.astype(BF)
        acts[:, cols] = act
        put("acts", act, c * width)
        put("slope", slope, c * width)
    copies[2].wait()
    n2, r2 = row_norm(normed + (nn(acts[...], wo[...]) + pick(OUTER_B)))
    put("n2", n2)
    put("r2", r2)
    e_ref[0:ROW_TILE, :] = table[...]
    e_ref[ROW_TILE:, :] = (n2 * pick(FFN_G) + pick(FFN_B)).astype(BF).astype(F32)


def head_call(info, own, other, wp, wi, wo, table):
    length = own.shape[0]
    width, ff = wi.shape
    kept = max(place + size for place, size in kept_places(width, ff, length).values())
    shapes = [struct((2 * ROW_TILE, width), F32), struct((ROW_TILE, kept), F32)]
    return pl.pallas_call(
        head_kernel,
        in_specs=[SCALARS, NEAR, NEAR, FAR, FAR, FAR, NEAR],
        out_specs=[NEAR] * len(shapes),
        out_shape=shapes,
        scratch_shapes=[pltpu.VMEM((ROW_TILE, ff), BF)]
        + [pltpu.VMEM(w.shape, BF) for w in (wp, wi, wo)]
        + [pltpu.SemaphoreType.DMA((3,))],
        compiler_params=params_of(22),
        cost_estimate=cost(7),
        name="head_rows",
    )(info, own, other, *far(wp, wi, wo), table)


def replace_first(xq, fixed):
    top_rows = xq[0:ROW_TILE, :]
    at_first = lax.broadcasted_iota(jnp.int32, top_rows.shape, 0) == 0
    xq[0:ROW_TILE, :] = jnp.where(at_first, fixed, top_rows)


def attention_parts(xq, j, width, lane, bias_col):
    base = pl.multiple_of(j * PAIR, PAIR)
    q = xq[:, pl.ds(base, PAIR)] * jnp.asarray(0.125, BF)
    k = xq[:, pl.ds(base + width, PAIR)]
    v = xq[:, pl.ds(base + 2 * width, PAIR)]
    zero = jnp.zeros_like(k)
    parts = []
    for h in range(2):
        mine = (lane >= HEAD_DIM * h) & (lane < HEAD_DIM * (h + 1))
        spare = lane == HEAD_DIM * (1 - h)
        qh = jnp.where(mine, q, jnp.where(spare, jnp.ones_like(q), zero))
        kh = jnp.where(mine, k, jnp.where(spare, bias_col, zero))
        parts.append((mine, qh, kh))
    return base, q, k, v, parts


def place_rows(ref, value, order):
    pieces, rows = ref.shape[0], ref.shape[1]
    for p in range(pieces):
        ref[jnp.bitwise_xor(p, order)] = value[p * rows : (p + 1) * rows, :]


def attend(xq, ctx, lse_scr, width, lane, bias_col):
    def pair_body(j, carry):
        base, q, k, v, parts = attention_parts(xq, j, width, lane, bias_col)
        sides = []
        for h, (mine, qh, kh) in enumerate(parts):
            vh = jnp.where(mine, v, jnp.ones_like(v))
            scores = nt(qh, kh)
            top = jnp.max(scores, axis=-1, keepdims=True)
            made = nn(jnp.exp(scores - top).astype(BF), vh)
            mass = made[:, HEAD_DIM * (1 - h) : HEAD_DIM * (1 - h) + 1]
            sides.append(made * (1.0 / mass))
            if lse_scr is not None:
                lse_scr[...] = jnp.where(lane == 2 * j + h, top + jnp.log(mass), lse_scr[...])
        ctx[:, pl.ds(base, PAIR)] = jnp.where(lane < HEAD_DIM, sides[0], sides[1]).astype(BF)
        return carry

    lax.fori_loop(0, HEADS // 2, pair_body, 0)


def mixing_kernel(info_ref, xq_a, xq_b, wp_a, wp_b, mine, table, normed_ref, xq, wp, ctx, sems):
    own = info_ref[0] == 0
    fetch(own, xq_a, xq_b, xq, sems.at[0])
    fetch(own, wp_a, wp_b, wp, sems.at[1])
    width = wp.shape[0]
    length = xq.shape[0]
    pick = layer_vectors(mine, table, own)
    lane = lax.broadcasted_iota(jnp.int32, (length, PAIR), 1)
    row = lax.broadcasted_iota(jnp.int32, (length, PAIR), 0)
    bias_col = jnp.where(row < info_ref[1], 0.0, BIG_NEG).astype(BF)
    landed(xq_a, xq, sems.at[0])
    attend(xq, ctx, None, width, lane, bias_col)
    landed(wp_a, wp, sems.at[1])
    n1, r1 = row_norm(xq[:, 3 * width :].astype(F32) + (nn(ctx[...], wp[...]) + pick(PROJ_B)))
    normed_ref[...] = n1 * pick(ATTN_G) + pick(ATTN_B)


def mixing_call(info, xq, wp, tables):
    length = xq[0].shape[0]
    width = wp[0].shape[0]
    return pl.pallas_call(
        mixing_kernel,
        in_specs=[SCALARS] + [FAR] * 4 + [NEAR] * 2,
        out_specs=NEAR,
        out_shape=struct((length, width), F32),
        scratch_shapes=[
            pltpu.VMEM(xq[0].shape, BF),
            pltpu.VMEM(wp[0].shape, BF),
            pltpu.VMEM((length, width), BF),
            pltpu.SemaphoreType.DMA((2,)),
        ],
        compiler_params=params_of(16),
        cost_estimate=cost(10),
        name="mixing",
    )(info, *far(*xq, *wp), *tables)


def train_kernel(
    info_ref, xq_a, xq_b, wq_a, wq_b, wp_a, wp_b, wi_a, wi_b, wo_a, wo_b, mine, table, cot_ref,
    z_ref, wp, wi, wo, ctx, lse_ref, fixed_ref, n1_ref, r1_ref, slope_ref, gf_ref, sg_ref, small_ref, keep_ref, send_ref,
    xq, lse_scr, sems,
):
    section = info_ref[0]
    own = section == 1
    fetch(own, xq_a, xq_b, xq, sems.at[0])
    width = wp.shape[0]
    length = xq.shape[0]
    ff = wi.shape[1]
    thirds = [(pl.ds(k * width, width), wo.at[pl.ds(k * width, width)]) for k in range(3)]
    for k, (cols, place) in enumerate(thirds):
        fetch(own, wq_a.at[:, cols], wq_b.at[:, cols], place, sems.at[5 + k])
    fetch(own, wp_a, wp_b, wp, sems.at[2])
    pick = layer_vectors(mine, table, own)
    lane = lax.broadcasted_iota(jnp.int32, (length, PAIR), 1)
    row = lax.broadcasted_iota(jnp.int32, (length, PAIR), 0)
    bias_col = jnp.where(row < info_ref[1], 0.0, BIG_NEG).astype(BF)
    first = jnp.where(section == 0, mine[ROW_TILE : ROW_TILE + 1, :], table[ROW_TILE + 1 : ROW_TILE + 2, :])
    many = jnp.broadcast_to(first.astype(BF), (ROW_TILE, width))
    fixed = []
    for k, shift in enumerate((pick(QUERY_B), None, pick(VALUE_B))):
        cols, place = thirds[k]
        landed(wq_a.at[:, cols], place, sems.at[5 + k])
        made = nn(many, place[...])
        fixed.append((made if shift is None else made + shift).astype(BF))
    fixed = jnp.concatenate(fixed + [many], axis=1)
    fixed_ref[...] = fixed
    landed(xq_a, xq, sems.at[0])
    fetch(own, wi_a, wi_b, wi, sems.at[3])
    fetch(own, wo_a, wo_b, wo, sems.at[4])
    copy = pltpu.make_async_copy(cot_ref.at[section], gf_ref, sems.at[1])
    copy.start()
    replace_first(xq, fixed)
    attend(xq, ctx, lse_scr, width, lane, bias_col)
    lse_ref[...] = jnp.transpose(lse_scr[...])[0:ROW_TILE, :]
    landed(wp_a, wp, sems.at[2])
    n1, r1 = row_norm(xq[:, 3 * width :].astype(F32) + (nn(ctx[...], wp[...]) + pick(PROJ_B)))
    n1_ref[...] = n1
    r1_ref[...] = r1
    normed = n1 * pick(ATTN_G) + pick(ATTN_B)
    low = normed.astype(BF)
    landed(wi_a, wi, sems.at[3])
    landed(wo_a, wo, sems.at[4])
    total = None
    for c in range(ff // CHUNK):
        cols = slice(c * CHUNK, (c + 1) * CHUNK)
        act, slope = gelu_pair(nn(low, wi[:, cols]) + pick(INNER_B, c))
        act = act.astype(BF)
        xq[:, cols] = act
        slope_ref[:, cols] = slope.astype(BF)
        term = nn(act, wo[cols, :])
        total = term if total is None else total + term
    n2, r2 = row_norm(normed + (total + pick(OUTER_B)))
    gain = pick(FFN_G)
    z_ref[...] = (n2 * gain + pick(FFN_B)).astype(BF)
    wide_row = lax.broadcasted_iota(jnp.int32, n2.shape, 0)
    copy.wait()
    grad = jnp.where(wide_row < info_ref[1], gf_ref[...].astype(F32), 0.0)
    second = norm_back(grad, n2, r2, gain)
    sg_ref[...] = second
    gf = second.astype(BF)
    gf_ref[...] = gf
    small_ref[0:1, :] = col_sum(gf)
    small_ref[1:2, :] = col_sum(grad * n2)
    small_ref[2:3, :] = col_sum(grad)
    half_chunks = ff // CHUNK // 2
    rows = send_ref.shape[1]
    each = CHUNK // rows
    for ref, half, order in ((send_ref, 1 - section, info_ref[4]), (keep_ref, section, info_ref[3])):
        for c in range(half_chunks):
            cols = pl.ds(pl.multiple_of((half * half_chunks + c) * CHUNK, CHUNK), CHUNK)
            made = tn(xq[:, cols], gf).astype(BF)
            for p in range(each):
                ref[jnp.bitwise_xor(c * each + p, order)] = made[p * rows : (p + 1) * rows, :]


def train_call(info, pairs, tables, cot):
    xq, wq, wp, wi, wo = (piece[0] for piece in pairs)
    length = xq.shape[0]
    width, ff = wi.shape
    args = [info]
    in_specs = [SCALARS]
    for pair in pairs:
        args += far(*pair)
        in_specs += [FAR, FAR]
    args += [*tables, *far(cot)]
    shapes = [
        struct((length, width), BF),
        near(wp.shape, BF),
        near(wi.shape, BF),
        near(wo.shape, BF),
        near((length, width), BF),
        near((ROW_TILE, length), F32),
        near((ROW_TILE, 4 * width), BF),
        near((length, width), F32),
        near((length, 1), F32),
        near((length, ff), BF),
        near((length, width), BF),
        near((length, width), F32),
        near((8, width), F32),
        near((GROUP, ff // 2 // GROUP, width), BF),
        near((GROUP, ff // 2 // GROUP, width), BF),
    ]
    return pl.pallas_call(
        train_kernel,
        in_specs=in_specs + [NEAR] * 2 + [FAR],
        out_specs=[NEAR] * len(shapes),
        out_shape=shapes,
        scratch_shapes=[
            pltpu.VMEM(xq.shape, BF),
            pltpu.VMEM((length, PAIR), F32),
            pltpu.SemaphoreType.DMA((8,)),
        ],
        compiler_params=params_of(14),
        cost_estimate=cost(26),
        name="layer_train",
    )(*args)


def feed_kernel(info_ref, normed_ref, wi_a, wi_b, wo_a, wo_b, mine, other, z_ref, wi, wo, sems):
    own = info_ref[0] == 0
    fetch(own, wi_a, wi_b, wi, sems.at[0])
    fetch(own, wo_a, wo_b, wo, sems.at[1])
    pick = layer_vectors(mine, other, own)
    normed = normed_ref[...]
    low = normed.astype(BF)
    landed(wi_a, wi, sems.at[0])
    landed(wo_a, wo, sems.at[1])
    total = None
    for c in range(wi.shape[1] // CHUNK):
        cols = slice(c * CHUNK, (c + 1) * CHUNK)
        act, slope = gelu_pair(nn(low, wi[:, cols]) + pick(INNER_B, c))
        term = nn(act.astype(BF), wo[cols, :])
        total = term if total is None else total + term
    n2, r2 = row_norm(normed + (total + pick(OUTER_B)))
    z_ref[...] = (n2 * pick(FFN_G) + pick(FFN_B)).astype(BF)


def feed_call(info, normed, wi, wo, tables):
    return pl.pallas_call(
        feed_kernel,
        in_specs=[SCALARS, NEAR] + [FAR] * 4 + [NEAR] * 2,
        out_specs=NEAR,
        out_shape=struct(normed.shape, BF),
        scratch_shapes=[pltpu.VMEM(wi[0].shape, BF), pltpu.VMEM(wo[0].shape, BF), pltpu.SemaphoreType.DMA((2,))],
        compiler_params=params_of(24),
        cost_estimate=cost(11),
        name="layer_feed",
    )(info, normed, *far(*wi, *wo), *tables)


def inner_kernel(
    info_ref, gf_ref, slope_ref, sg_ref, n1_ref, r1_ref, wi_ref, wo_ref, wp_ref, mine, table,
    keep_ref, send_ref, gh_ref, ga_ref, gc_ref, small_ref,
):
    section = info_ref[0]
    pick = layer_vectors(mine, table, section == 1)
    gain = pick(ATTN_G)
    low = turned(n1_ref[...] * gain + pick(ATTN_B))
    ff = wi_ref.shape[1]
    half_chunks = ff // CHUNK // 2
    gf = gf_ref[...]
    gn = sg_ref[...]
    for ref, half, order in ((send_ref, 1 - section, info_ref[6]), (keep_ref, section, info_ref[5])):
        for c in range(half_chunks):
            block = half * half_chunks + c
            cols = pl.ds(pl.multiple_of(block * CHUNK, CHUNK), CHUNK)
            gu = (nt(gf, wo_ref[cols, :]) * slope_ref[:, cols].astype(F32)).astype(BF)
            small_ref[pl.ds(3 + block, 1), :] = col_sum(gu)
            place_rows(ref.at[:, :, c * CHUNK : (c + 1) * CHUNK], nn(low, gu).astype(BF), order)
            gn = gn + nt(gu, wi_ref[:, cols])
    n1 = n1_ref[...]
    gh = norm_back(gn, n1, r1_ref[...], gain)
    gh_ref[...] = gh
    ga = gh.astype(BF)
    ga_ref[...] = ga
    gc_ref[...] = nt(ga, wp_ref[...]).astype(BF)
    small_ref[0:1, :] = col_sum(ga)
    small_ref[1:2, :] = col_sum(gn * n1)
    small_ref[2:3, :] = col_sum(gn)


def inner_call(info, gf, slope, sg, n1, r1, wi, wo, wp, tables):
    tokens, width = gf.shape
    ff = wi.shape[1]
    shapes = [
        near((GROUP, width // GROUP, ff // 2), BF),
        near((GROUP, width // GROUP, ff // 2), BF),
        near((tokens, width), F32),
        near((tokens, width), BF),
        near((tokens, width), BF),
        near((8, width), F32),
    ]
    return pl.pallas_call(
        inner_kernel,
        in_specs=[SCALARS] + [NEAR] * 10,
        out_specs=[NEAR] * len(shapes),
        out_shape=shapes,
        compiler_params=params_of(12),
        cost_estimate=cost(10),
        name="inner_grad",
    )(info, *stay(gf, slope, sg, n1, r1, wi, wo, wp), *tables)


def attention_kernel(
    info_ref, xq_a, xq_b, fixed_ref, gc_ref, ga_ref, c_ref, lse_ref, keep_ref, send_ref, g_ref, small_ref,
    xq, xt_scr, ct_scr, mean_scr, sem,
):
    section = info_ref[0]
    fetch(section == 1, xq_a, xq_b, xq, sem)
    length, width = gc_ref.shape
    row = lax.broadcasted_iota(jnp.int32, (length, PAIR), 0)
    lane = lax.broadcasted_iota(jnp.int32, (length, PAIR), 1)
    bias_col = jnp.where(row < info_ref[1], 0.0, BIG_NEG).astype(BF)
    ct_scr[...] = turned(c_ref[...])
    product = gc_ref[...].astype(F32) * c_ref[...].astype(F32)
    high = product.astype(BF)
    low = (product - high.astype(F32)).astype(BF)
    ones = by_head(jnp.ones((1, width), BF), ROW_TILE)
    mean_scr[...] = nt(ones, high) + nt(ones, low)
    landed(xq_a, xq, sem)
    replace_first(xq, fixed_ref[...])
    xt_scr[...] = turned(xq[:, 3 * width :])

    def pair_body(j, carry):
        base, q, k, v, parts = attention_parts(xq, j, width, lane, bias_col)
        kt = turned(k)
        gc = gc_ref[:, pl.ds(base, PAIR)]
        zero = jnp.zeros_like(gc)
        strips = [slice(0, length)]
        gk = [None] * len(strips)
        gv = [None] * len(strips)
        gqt = []
        for h, (mine, qh, kh) in enumerate(parts):
            gch = jnp.where(mine, gc, zero)
            qz = jnp.where(mine, q, zero)
            lse = lse_ref[pl.ds(2 * j + h, 1), :]
            mean = mean_scr[pl.ds(2 * j + h, 1), :]
            gq_h = None
            for s, rows in enumerate(strips):
                probs = jnp.exp(nt(kh[rows, :], qh) - lse)
                gs = (probs * (nt(v[rows, :], gch) - mean)).astype(BF)
                gv_h = nn(probs.astype(BF), gch)
                gk_h = nn(gs, qz)
                term = nn(kt[HEAD_DIM * h : HEAD_DIM * (h + 1), rows], gs)
                gq_h = term if gq_h is None else gq_h + term
                gk[s] = gk_h if h == 0 else gk[s] + gk_h
                gv[s] = gv_h if h == 0 else gv[s] + gv_h
            gqt.append(gq_h)
        gq = jnp.transpose(jnp.concatenate(gqt, axis=0)) * 0.125
        g_ref[:, pl.ds(base, PAIR)] = gq.astype(BF)
        for s, rows in enumerate(strips):
            g_ref[rows, pl.ds(base + width, PAIR)] = gk[s].astype(BF)
            g_ref[rows, pl.ds(base + 2 * width, PAIR)] = gv[s].astype(BF)
        return carry

    lax.fori_loop(0, HEADS // 2, pair_body, 0)
    small_ref[0:1, :] = col_sum(g_ref[:, 0:width])
    small_ref[1:2, :] = col_sum(g_ref[:, 2 * width : 3 * width])
    wide = 3 * width // 2
    for ref, half, order in ((send_ref, 1 - section, info_ref[8]), (keep_ref, section, info_ref[7])):
        cols = pl.ds(pl.multiple_of(half * wide, PAIR), wide)
        place_rows(ref.at[:, :, 0:wide], nn(xt_scr[...], g_ref[:, cols]).astype(BF), order)
        cols = pl.ds(pl.multiple_of(half * (width // 2), PAIR), width // 2)
        place_rows(ref.at[:, :, wide:], nn(ct_scr[...], ga_ref[:, cols]).astype(BF), order)


def attention_call(info, xq, fixed, gc, ga, context, lse):
    length, width = gc.shape
    shapes = [
        near((GROUP, width // GROUP, 2 * width), BF),
        near((GROUP, width // GROUP, 2 * width), BF),
        near((length, 3 * width), BF),
        near((8, width), F32),
    ]
    return pl.pallas_call(
        attention_kernel,
        in_specs=[SCALARS, FAR, FAR] + [NEAR] * 5,
        out_specs=[NEAR] * len(shapes),
        out_shape=shapes,
        scratch_shapes=[
            pltpu.VMEM(xq[0].shape, BF),
            pltpu.VMEM((width, length), BF),
            pltpu.VMEM((width, length), BF),
            pltpu.VMEM((ROW_TILE, length), F32),
            pltpu.SemaphoreType.DMA(()),
        ],
        compiler_params=params_of(18),
        cost_estimate=cost(14),
        name="attention_grad",
    )(info, *far(*xq), *stay(fixed, gc, ga, context, lse))


def input_kernel(info_ref, w_a, w_b, g_ref, gh_ref, small1_ref, small2_ref, small3_ref, o_ref, small_ref, w, sem):
    fetch(info_ref[0] == 1, w_a, w_b, w, sem)
    landed(w_a, w, sem)
    made = gh_ref[...] + nt(g_ref[...], w[...])
    o_ref[...] = made
    small_ref[0:2, :] = small3_ref[0:2, :]
    small_ref[2:9, :] = small2_ref[0:7, :]
    small_ref[9:12, :] = small1_ref[0:3, :]
    small_ref[12:16, :] = made[0:4, :]


def input_call(info, g, gh, w, small1, small2, small3):
    return pl.pallas_call(
        input_kernel,
        in_specs=[SCALARS, FAR, FAR] + [NEAR] * 5,
        out_specs=[NEAR] * 2,
        out_shape=[struct(gh.shape, F32), struct((ROW_TILE, gh.shape[1]), F32)],
        scratch_shapes=[pltpu.VMEM(w[0].shape, BF), pltpu.SemaphoreType.DMA(())],
        compiler_params=params_of(12),
        cost_estimate=cost(4),
        name="input_grad",
    )(info, *far(*w), *stay(g, gh, small1, small2, small3))


def head_back_kernel(
    info_ref, small_a, small_b, kept_ref, own_ref, other_ref,
    wq_ref, wp_ref, wi_ref, wo_ref, table, x_ref, first_ref, second_ref, wq, wp, wi, wo, sems,
):
    copies = [
        pltpu.make_async_copy(ref, scr, sems.at[i])
        for i, (ref, scr) in enumerate(((wo_ref, wo), (wi_ref, wi), (wp_ref, wp), (wq_ref, wq)))
    ]
    for copy in copies:
        copy.start()
    width = wp.shape[0]
    length = own_ref.shape[0]
    ff = wi.shape[1]
    places = kept_places(width, ff, length)

    def kept(name, offset=0, size=None):
        start = places[name][0] + offset
        return kept_ref[:, start : start + (places[name][1] if size is None else size)]

    n1, n2 = kept("n1"), kept("n2")
    context = kept("context").astype(BF)
    pick = layer_vectors(table, table, info_ref[0] == 0)
    grad = two_rows(small_a[12:13, :], small_b[12:13, :]).astype(BF).astype(F32)
    second = norm_back(grad, n2, kept("r2", 0, 1), pick(FFN_G))
    gf = second.astype(BF)
    copies[0].wait()
    gu = (nt(gf, wo[...]) * kept("slope")).astype(BF)
    copies[1].wait()
    gn = second + nt(gu, wi[...])
    gh = norm_back(gn, n1, kept("r1", 0, 1), pick(ATTN_G))
    ga = gh.astype(BF)
    copies[2].wait()
    gc = nt(ga, wp[...]).astype(BF)
    normed = (n1 * pick(ATTN_G) + pick(ATTN_B)).astype(BF)
    copies[3].wait()
    query_bias = value_bias = jnp.zeros((1, width), F32)
    heads, rest = {}, {}
    for i, ref in enumerate((own_ref, other_ref)):
        mid = (1 - 2 * i) * info_ref[0] + i
        keys, values, inputs = ref[:, width : 2 * width], ref[:, 2 * width : 3 * width], ref[:, 3 * width :]
        query = ref[0:1, 0:width] * jnp.asarray(0.125, BF)
        gc_row = gc[i : i + 1, :]
        query_heads, gc_heads = by_head(query, ROW_TILE), by_head(gc_row, ROW_TILE)
        probs = kept("probs", i * length, length)
        gp = nt(gc_heads, values)
        gs = (probs * (gp - jnp.sum(probs * gp, axis=-1, keepdims=True))).astype(BF)
        low = probs.astype(BF)
        gq = (heads_of(nn(gs, keys)) * 0.125).astype(BF)
        for place, value in ((KEY_SUMS, nn(gs, inputs)), (VALUE_SUMS, nn(low, inputs))):
            for h in range(HEADS):
                heads[place + HEADS * i + h] = value[h : h + 1, :]
        key_back = nt(query_heads, wq[:, width : 2 * width]).astype(BF)
        value_back = nt(gc_heads, wq[:, 2 * width :]).astype(BF)
        gx = tn(gs, key_back) + tn(low, value_back)
        top = gh[i : i + 1, :] + nt(jnp.broadcast_to(gq, (ROW_TILE, width)), wq[:, 0:width])[0:1, :]
        at_first = lax.broadcasted_iota(jnp.int32, gx.shape, 0) == 0
        x_ref[mid] = gx + jnp.where(at_first, top, 0.0)
        query_bias = query_bias + gq.astype(F32)
        mass = jnp.sum(low.astype(F32), axis=-1, keepdims=True)
        value_bias = value_bias + heads_of(gc_heads.astype(F32) * mass)
        heads[QUERIES + i] = query
        heads[GCONTEXTS + i] = gc_row
        for place, value in ((OUTERS, gf), (NORMEDS, normed), (CONTEXTS, context), (PROJS, ga)):
            rest[place + i] = value[i : i + 1, :]
        rest[INPUTS + i] = ref[0:1, 3 * width :]
        rest[GQUERIES + i] = gq
    gu_sum = col_sum(gu)
    act = kept("acts").astype(BF)
    own_small = [query_bias, value_bias, col_sum(ga), col_sum(gn * n1), col_sum(gn)]
    own_small += [gu_sum[:, width * k : width * (k + 1)] for k in range(ff // width)]
    own_small += [col_sum(gf), col_sum(grad * n2), col_sum(grad)]

    for k in range(ff // width):
        for i in range(2):
            rest[ACTS + 4 * i + k] = act[i : i + 1, width * k : width * (k + 1)]
            rest[INNERS + 4 * i + k] = gu[i : i + 1, width * k : width * (k + 1)]
    row = lax.broadcasted_iota(jnp.int32, (8, width), 0)
    for ref, rows in ((first_ref, heads), (second_ref, rest)):
        for k, piece in enumerate(own_small):
            rows[SUMS + k] = jnp.where(info_ref[0] == 0, piece, small_a[k : k + 1, :] + small_b[k : k + 1, :])
        for start in range(0, FACTORS, 8):
            made = jnp.zeros((8, width), F32)
            for k in range(8):
                if start + k in rows:
                    made = jnp.where(row == k, rows[start + k].astype(F32), made)
            ref[start : start + 8, :] = made.astype(BF)


def head_back_call(info, small_a, small_b, kept, own, other, wq, wp, wi, wo, table):
    length = own.shape[0]
    width, ff = wi.shape
    args = [small_a, small_b, kept, own, other]
    return pl.pallas_call(
        head_back_kernel,
        in_specs=[SCALARS] + [NEAR] * len(args) + [FAR] * 4 + [NEAR],
        out_specs=[NEAR] * 3,
        out_shape=[struct((2, length, width), F32)] + [struct((FACTORS, width), BF)] * 2,
        scratch_shapes=[pltpu.VMEM(w.shape, BF) for w in (wq, wp, wi, wo)] + [pltpu.SemaphoreType.DMA((4,))],
        compiler_params=params_of(28),
        cost_estimate=cost(12),
        name="head_rows_grad",
    )(info, *args, *far(wq, wp, wi, wo), table)


def piece_at(low, high, place, cols=slice(None)):
    half = low.shape[0]
    inside = lax.rem(place, half)
    return jnp.where(place < half, low[inside, :, cols], high[inside, :, cols])


def feed_final_kernel(outer, info_ref, a_low, a_high, b_low, b_high, rest_ref, o_ref, buffers, sems):
    width = buffers.shape[1]
    rows = a_low.shape[1]
    first = 4 if outer else 6
    halves = ((a_low, a_high, info_ref[first]), (b_low, b_high, info_ref[first - 1]))

    def products(left, right):
        return sum(tn(rest_ref[left[0] + j * left[1]], rest_ref[right[0] + j * right[1]]) for j in range(2))

    copies = []
    for k in range(4):
        slot = k % 2
        if k >= 2:
            copies[k - 2].wait()

        @pl.when(info_ref[0] == 1)
        def _():
            low, high, order = halves[k // 2]
            for p in range(width // rows):
                if outer:
                    piece = piece_at(low, high, jnp.bitwise_xor((k % 2) * (width // rows) + p, order))
                else:
                    cols = slice((k % 2) * width, (k % 2 + 1) * width)
                    piece = piece_at(low, high, jnp.bitwise_xor(p, order), cols)
                buffers[slot, p * rows : (p + 1) * rows, :] = piece.astype(F32)

        @pl.when(info_ref[0] == 0)
        def _():
            left, right = ((ACTS + k, 4), (OUTERS, 1)) if outer else ((NORMEDS, 1), (INNERS + k, 4))
            buffers[slot] = products(left, right)

        block = slice(k * width, (k + 1) * width)
        target = o_ref.at[block, :] if outer else o_ref.at[:, block]
        copies.append(pltpu.make_async_copy(buffers.at[slot], target, sems.at[slot]))
        copies[-1].start()
    copies[-2].wait()
    copies[-1].wait()


def feed_final_call(outer, info, quarters, rest):
    width = rest.shape[2]
    ff = 4 * width
    return pl.pallas_call(
        lambda *refs: feed_final_kernel(outer, *refs),
        in_specs=[SCALARS] + [NEAR] * 5,
        out_specs=FAR,
        out_shape=struct((ff, width) if outer else (width, ff), F32),
        scratch_shapes=[pltpu.VMEM((2, width, width), F32), pltpu.SemaphoreType.DMA((2,))],
        compiler_params=params_of(10),
        cost_estimate=cost(4),
        name="outer_final" if outer else "inner_final",
    )(info, *quarters, rest)


def qkv_final_kernel(info_ref, a_low, a_high, b_low, b_high, heads_ref, rest_ref, o_ref, p_ref, made, made_p, sems):
    width = p_ref.shape[0]
    wide = 3 * width // 2
    half = width // 2
    rows = a_low.shape[1]

    @pl.when(info_ref[0] == 1)
    def _():
        copies = []
        for k, (low, high, order) in enumerate(((a_low, a_high, info_ref[8]), (b_low, b_high, info_ref[7]))):
            for p in range(GROUP):
                place = jnp.bitwise_xor(p, order)
                at = slice(p * rows, (p + 1) * rows)
                made[at, k * wide : (k + 1) * wide] = piece_at(low, high, place, slice(0, wide)).astype(F32)
                piece = piece_at(low, high, place, slice(wide, wide + half))
                made_p[at, k * half : (k + 1) * half] = piece.astype(F32)
            cols = slice(k * wide, (k + 1) * wide)
            copies.append(pltpu.make_async_copy(made.at[:, cols], o_ref.at[:, cols], sems.at[k]))
            copies[-1].start()
        copies.append(pltpu.make_async_copy(made_p, p_ref, sems.at[2]))
        copies[-1].start()
        for copy in copies:
            copy.wait()

    @pl.when(info_ref[0] == 0)
    def _():
        def pairs(left, right):
            return tn(rest_ref[left], rest_ref[right]) + tn(rest_ref[left + 1], rest_ref[right + 1])

        made_p[...] = pairs(CONTEXTS, PROJS)
        copies = [pltpu.make_async_copy(made_p, p_ref, sems.at[3])]
        copies[-1].start()
        chips = heads_ref.shape[1]
        lane = lax.broadcasted_iota(jnp.int32, (chips, width), 1)
        for place, base, key in ((0, 0, 0), (1, KEY_SUMS, QUERIES), (2, VALUE_SUMS, GCONTEXTS)):
            cols = slice(place * width, (place + 1) * width)
            if place == 0:
                made[:, cols] = pairs(INPUTS, GQUERIES)
            else:
                term = None
                for j in range(2):
                    left = heads_ref[base + HEADS * j : base + HEADS * j + HEADS].reshape(HEADS * chips, width)
                    row = heads_ref[key + j]
                    heads = [
                        jnp.where((lane >= HEAD_DIM * h) & (lane < HEAD_DIM * (h + 1)), row, jnp.zeros_like(row))
                        for h in range(HEADS)
                    ]
                    one = tn(left, jnp.concatenate(heads, axis=0))
                    term = one if term is None else term + one
                made[:, cols] = term
            copies.append(pltpu.make_async_copy(made.at[:, cols], o_ref.at[:, cols], sems.at[4 + place]))
            copies[-1].start()
        for copy in copies:
            copy.wait()


def qkv_final_call(info, quarters, heads, rest):
    width = rest.shape[2]
    return pl.pallas_call(
        qkv_final_kernel,
        in_specs=[SCALARS] + [NEAR] * 6,
        out_specs=[FAR, FAR],
        out_shape=[struct((width, 3 * width), F32), struct((width, width), F32)],
        scratch_shapes=[
            pltpu.VMEM((width, 3 * width), F32),
            pltpu.VMEM((width, width), F32),
            pltpu.SemaphoreType.DMA((7,)),
        ],
        compiler_params=params_of(16),
        cost_estimate=cost(4),
        name="qkv_final",
    )(info, *quarters, heads, rest)


def swap(value):
    return lax.ppermute(value, "section", SWAP)


def add_low(left, right):
    return (left.astype(F32) + right.astype(F32)).astype(BF)


def hop(value, stage, orders):
    chips = lax.axis_size("dp")
    pairs = [
        (section * chips + chip, section * chips + (chip ^ orders[section][stage]))
        for section in range(2)
        for chip in range(chips)
    ]
    return lax.ppermute(value, ("section", "dp"), pairs)


def after(value, *others):
    return lax.optimization_barrier((value,) + others)[0]


def beside(made, *sums):
    tied = lax.optimization_barrier(tuple(made) + tuple(one.coming for one in sums))
    for one, coming in zip(sums, tied[len(made) :]):
        one.coming = coming
    return tied[: len(made)]


class Sum:
    def __init__(self, keep, send, group):
        self.low, self.coming, self.orders = keep, swap(send), ORDERS[group]

    def add(self):
        half = self.coming.shape[0] // 2
        if half == 0:
            self.part = add_low(self.low, self.coming)
            return
        self.high = add_low(self.low[half:], self.coming[half:])
        self.low = self.part = add_low(self.low[:half], self.coming[:half])

    def halve(self, stage):
        self.coming = hop(self.high, stage, self.orders)

    def across(self):
        chips = lax.axis_size("dp")
        if chips > GROUP:
            groups = [[low + GROUP * high for high in range(chips // GROUP)] for low in range(GROUP)]
            self.part = lax.psum(self.part, "dp", axis_index_groups=groups)

    def double(self, stage):
        self.coming = hop(self.part, stage, self.orders)

    def join(self):
        self.part = jnp.concatenate([self.part, self.coming], axis=0)

    def quarters(self, line):
        return (swap(line(self.part)), swap(line(self.coming)), self.part, self.coming)


class Line:
    def __init__(self):
        self.token = None

    def __call__(self, value):
        return value if self.token is None else after(value, self.token)

    def run(self, work, *args):
        made = work(*args)
        tied = lax.optimization_barrier(tuple(made))
        self.token = tied[0]
        return tied

    def take(self, group):
        group.coming = self(group.coming)
        self.token = group.coming

    def halve(self, group, stage):
        self.take(group)
        group.add()
        group.halve(stage)
        self.token = group.part

    def double(self, group, stage):
        self.take(group)
        group.add()
        group.across()
        group.double(stage)
        self.token = group.part

    def join(self, group, stage):
        self.take(group)
        group.join()
        if stage is not None:
            group.double(stage)
        self.token = group.part


class Gather:
    ORDERS = ((8, 4, 2, 1), (4, 8, 1, 2))

    def __init__(self, value):
        self.part = value[None]

    def double(self, stage):
        self.coming = hop(self.part, stage, self.ORDERS)

    def join(self):
        self.part = lax.optimization_barrier(jnp.concatenate([self.part, self.coming], axis=0))

    def across(self):
        chips = lax.axis_size("dp")
        if chips > GROUP:
            groups = [[low + GROUP * high for high in range(chips // GROUP)] for low in range(GROUP)]
            every = lax.all_gather(self.part, "dp", axis_index_groups=groups)
            self.part = every.reshape((-1,) + self.part.shape[1:])


def order_of(chip, orders):
    place = jnp.int32(0)
    for stage in range(4):
        bit = (chip // orders[stage]) % 2
        place = place + bit * (8 >> stage)
    return place


def local(embeddings, cotangent, lengths, *weights):
    (wq, query_bias, value_bias, wp, proj_bias, attn_gain, attn_bias, wi, inner_bias, wo, outer_bias, ffn_gain, ffn_bias) = (
        piece[0] for piece in weights
    )
    section = lax.axis_index("section")
    chip = lax.axis_index("dp")
    first_section = section == 0
    inputs = embeddings[0]
    width = inputs.shape[2]
    scalars = [section, jnp.where(first_section, lengths[0], lengths[1]), jnp.where(first_section, lengths[1], lengths[0])]
    for orders in ORDERS:
        places = [order_of(chip, order) for order in orders]
        scalars += [jnp.where(first_section, places[0], places[1]), jnp.where(first_section, places[1], places[0])]
    info = jnp.stack(scalars).astype(jnp.int32)
    vectors = [weights[k] for k in (1, 2, 4, 5, 6, 8, 10, 11, 12)]
    own, other, own_table = qkv_call(info, inputs, wq, vectors)
    wq_pair = (wq, swap(wq))
    wp_pair = (wp, swap(wp))
    xq_pair = (own, swap(other))
    wi_pair = (wi, swap(wi))
    wo_pair = (wo, swap(wo))
    head = head_call(info, own, other, wp, wi, wo, own_table)
    tables = (head[0], swap(head[0]))
    pairs = (xq_pair, wq_pair, wp_pair, wi_pair, wo_pair)
    (z, wp_d, wi_d, wo_d, context, lse, fixed, n1, r1, slope, gf, sg, small1, outer_keep, outer_send) = train_call(
        info, pairs, tables, cotangent
    )
    g1 = Sum(outer_keep, outer_send, 0)

    made = inner_call(info, gf, slope, sg, n1, r1, wi_d, wo_d, wp_d, tables)
    inner_keep, inner_send, gh, ga, gc, small2 = beside(made, g1)
    g1.add()
    g1.halve(0)
    g2 = Sum(inner_keep, inner_send, 1)

    made = attention_call(info, xq_pair, fixed, after(gc, g1.part), ga, context, lse)
    qkv_keep, qkv_send, g_qkv, small3 = beside(made, g1)
    line = Line()
    line.halve(g2, 0)
    line.halve(g1, 1)
    g3 = Sum(qkv_keep, line(qkv_send), 2)
    gx, dsmall = line.run(input_call, info, line(g_qkv), gh, wq_pair, small1, small2, small3)
    dsmall_other = swap(line(dsmall))
    line.halve(g3, 0)
    encoder_gx, heads, rest = line.run(
        head_back_call, info, dsmall, line(dsmall_other), head[1], own, other, wq, wp, wi, wo, own_table
    )
    came = swap(line(rest))
    gx_other = swap(line(gx))
    line.halve(g1, 2)
    (normed,) = line.run(lambda *a: (mixing_call(*a),), info, xq_pair, wp_pair, (tables[0], line(tables[1])))
    line.halve(g2, 1)
    line.halve(g3, 1)
    shared = jnp.where(first_section, heads, jnp.concatenate([line(came)[:SUMS], heads[SUMS:]]))
    factors = Gather(shared)
    factors.double(0)
    line.token = factors.part
    line.halve(g1, 3)
    line.halve(g2, 2)
    line.join(factors, 1)
    line.halve(g3, 2)
    line.double(g1, 3)
    line.join(factors, 2)
    line.halve(g2, 3)
    line.halve(g3, 3)
    line.join(g1, 2)
    line.double(g2, 3)
    line.join(factors, 3)
    line.double(g3, 3)
    line.join(g2, 2)
    line.join(g1, 1)
    line.join(g3, 2)
    line.join(g2, 1)
    line.join(g1, 0)
    line.join(g3, 1)
    line.join(g2, 0)
    line.join(factors, None)
    line.join(g3, 0)
    factors.across()
    sums = jnp.sum(line(factors.part)[:, SUMS:].astype(F32), axis=0)
    heads_all = jnp.transpose(factors.part, (1, 0, 2))
    heads_all, sums = line.run(lambda *a: a, heads_all, sums)
    (e_low,) = line.run(lambda *a: (feed_call(*a),), info, line(normed), wi_pair, wo_pair, tables)
    decoder_gx = jnp.stack([line(gx_other), gx])
    later = jnp.arange(gx.shape[0])[None, :, None] > 0
    (embed_grads,) = line.run(lambda a: (jnp.where(first_section, encoder_gx, jnp.where(later, a, 0.0)),), decoder_gx)
    line.take(g1)
    line.take(g2)
    rest_all = swap(line(heads_all)[:SUMS])
    z_other = swap(line(jnp.where(first_section, z, e_low)))
    z_mine = jnp.where(first_section, e_low, z)
    outer_quarters = g1.quarters(line)
    inner_quarters = g2.quarters(line)
    outputs = jnp.where(first_section, jnp.stack([z_mine, line(z_other)]), jnp.stack([z_other, z_mine]))
    (outputs,) = line.run(lambda a: (a,), outputs)
    (outer_grad,) = line.run(lambda *a: (feed_final_call(True, *a),), info, outer_quarters, line(rest_all))
    line.take(g3)
    qkv_quarters = g3.quarters(line)
    (inner_grad,) = line.run(lambda *a: (feed_final_call(False, *a),), info, inner_quarters, line(rest_all))
    qkv_grad, proj_grad = line.run(qkv_final_call, info, qkv_quarters, heads_all, line(rest_all))
    results = (
        outputs,
        embed_grads,
        qkv_grad,
        sums[0],
        sums[1],
        proj_grad,
        sums[2],
        sums[3],
        sums[4],
        inner_grad,
        sums[5:9].reshape(-1),
        outer_grad,
        sums[9],
        sums[10],
        sums[11],
    )
    return tuple(piece[None] for piece in results)


def solution(mesh):
    matrix = P("section", None, None)
    vector = P("section", None)
    return jax.shard_map(
        local,
        mesh=mesh,
        in_specs=(P("section", "dp", None, None), P("dp", None, None), P("dp"))
        + (matrix, vector, vector, matrix, vector, vector, vector)
        + (matrix, vector, matrix, vector, vector, vector),
        out_specs=(P("section", "dp", None, None), P("section", "dp", None, None))
        + (matrix, vector, vector, matrix, vector, vector, vector)
        + (matrix, vector, matrix, vector, vector, vector),
        check_vma=False,
    )
```
